32 devices in a mesh: dp: 8 (over z, x), dir: 4 (over y, core).
Axes of the slice: x: 2, y: 2, z: 4, core: 2. Of those that a mesh axis runs over, the one named last changes fastest.
Arguments:
- tokens: bfloat16 [16, 256, 1536], P('dp', 'dir'), may hold values from -6 to 6
- cond: bfloat16 [16, 1536], P('dp'), may hold values from -6 to 6
- counts: int32 [8], P('dp'), may hold values from 1 to 2, as said below
- valid: int32 [16, 256], P('dp'), may hold values from 0 to 1, as said below
- ada_weight: bfloat16 [1536, 4608], replicated, may hold values from -0.15625 to 0.15625
- ada_bias: bfloat16 [4608], replicated, may hold values from -3 to 3
- in_weight: bfloat16 [1536, 6144], P(None, 'dir'), may hold values from -0.15625 to 0.15625
- conv_weight: bfloat16 [6144, 4], P('dir'), may hold values from -3 to 3
- conv_bias: bfloat16 [6144], P('dir'), may hold values from -3 to 3
- xproj_weight: bfloat16 [6144, 128], P('dir'), may hold values from -0.109375 to 0.109375
- dtproj_weight: bfloat16 [96, 6144], P(None, 'dir'), may hold values from -0.625 to 0.625
- dt_bias: float32 [6144], P('dir'), may hold values from -6 to -2.5
- a_log: float32 [6144, 16], P('dir'), may hold values from 0 to 2.77
- skip_gain: float32 [6144], P('dir'), may hold values from 0.5 to 1.5
- out_weight: bfloat16 [3072, 1536], P('dir'), may hold values from -0.3125 to 0.3125
- cotangent: bfloat16 [16, 256, 1536], P('dp', 'dir'), may hold values from -6 to 6
Outputs:
- mixed: float32 [16, 256, 1536], P('dp', 'dir')
- tokens_grad: float32 [16, 256, 1536], P('dp', 'dir')
- cond_grad: float32 [16, 1536], P('dp')
- ada_weight_grad: float32 [1536, 4608], P('dp', 'dir')
- ada_bias_grad: float32 [4608], P('dp')
- in_weight_grad: float32 [1536, 6144], P('dp', 'dir')
- conv_weight_grad: float32 [6144, 4], P('dir')
- conv_bias_grad: float32 [6144], P('dir')
- xproj_weight_grad: float32 [6144, 128], P('dir')
- dtproj_weight_grad: float32 [96, 6144], P(None, 'dir')
- dt_bias_grad: float32 [6144], P('dir')
- a_log_grad: float32 [6144, 16], P('dir')
- skip_gain_grad: float32 [6144], P('dir')
- out_weight_grad: float32 [3072, 1536], P('dir', 'dp')
The draws below stay inside these ranges and needn't reach their ends.
Inputs may be any that keep to these rules, and one draw needn't show every extreme that they name: `counts`: the live slots of an index of dp are its first ones, the rest are empty; some index has all 2 live. The valid rows of an item are its first ones, 128 or more of them; some item is valid in all 256 rows.
All inputs are finite; a program needn't handle non-finite values.
Results may differ from the reference program's by a relative error of at most 0.014.
The reference program's roundings to bfloat16 on the way count: a program that leaves them out, or rounds other values in their place, can miss the bound.
Values may be sent and summed in bfloat16 or wider, within the bound.
No kernel may reach another device: no remote copies, remote signals or barrier semaphores. Data moves between devices by JAX's collectives and lax.ppermute only.
A program may use at most 256 MiB of HBM per device.

```python
from functools import partial
import jax
import jax.numpy as jnp
from jax import lax

D = 1536
INNER = 3072
STATE = 16
RANK = 96
CONV = 4
ITEM = 256
BLOCK = 16
SLOTS = 2
ITEMS = 16


def draw_counts(key, part):
    key = jax.random.fold_in(key, 11)
    first_key, second_key = jax.random.split(key)
    owners = ITEMS // SLOTS
    base_counts = jax.random.randint(first_key, (owners,), 1, SLOTS + 1)
    chosen = jax.random.randint(second_key, (), 0, owners)
    return jnp.where(jnp.arange(owners) == chosen, SLOTS, base_counts).astype(jnp.int32)


def draw_valid(key, part):
    key = jax.random.fold_in(key, 23)
    first_key, second_key = jax.random.split(key)
    lengths = jax.random.randint(first_key, (ITEMS,), ITEM // 2, ITEM + 1)
    chosen = jax.random.randint(second_key, (), 0, ITEMS)
    lengths = jnp.where(jnp.arange(ITEMS) == chosen, ITEM, lengths)
    return (jnp.arange(ITEM)[None, :] < lengths[:, None]).astype(jnp.int32)


def shard_levels(key, shape, shards, smallest, largest):
    gain, own = 1.0, jax.random.fold_in(key, 6)
    for axis_at, parts in shards:
        heights = jnp.exp(jax.random.uniform(jax.random.fold_in(own, axis_at), (parts,), jnp.float32, smallest / len(shards), largest / len(shards)))
        gain = gain * jnp.repeat(heights, shape[axis_at] // parts).reshape([-1 if axis == axis_at else 1 for axis in range(len(shape))])
    return gain


def bell_draw(stream_key, shape, scale, most, shards=(), held_as=jnp.bfloat16):
    factor_of = shard_levels(stream_key, shape, shards, -0.22, 0.18) if shards else 1.0
    values = jax.random.normal(stream_key, shape, jnp.float32) * scale * factor_of
    return jnp.minimum(jnp.maximum(values, -most), most).astype(held_as)


def setup_inputs(seed: int = 0) -> dict:
    key_of = jax.random.split(jax.random.key(seed), 17)
    return {
        "tokens": bell_draw(key_of[0], (ITEMS, ITEM, D), 1.0, 6.0, ((0, 8), (1, 4))),
        "cond": bell_draw(key_of[1], (ITEMS, D), 1.0, 6.0, ((0, 8),)),
        "counts": draw_counts(jax.random.fold_in(key_of[16], 71), 0),
        "valid": draw_valid(jax.random.fold_in(key_of[16], 71), 0),
        "ada_weight": bell_draw(key_of[4], (D, 3 * D), D ** -0.5, 0.15625),
        "ada_bias": bell_draw(key_of[5], (3 * D,), 0.5, 3.0),
        "in_weight": bell_draw(key_of[6], (D, 2 * INNER), D ** -0.5, 0.15625, ((1, 4),)),
        "conv_weight": bell_draw(key_of[7], (2 * INNER, CONV), CONV ** -0.5, 3.0, ((0, 4),)),
        "conv_bias": bell_draw(key_of[8], (2 * INNER,), 0.5, 3.0, ((0, 4),)),
        "xproj_weight": bell_draw(key_of[9], (2 * INNER, RANK + 2 * STATE), INNER ** -0.5, 0.109375, ((0, 4),)),
        "dtproj_weight": bell_draw(key_of[10], (RANK, 2 * INNER), RANK ** -0.5, 0.625, ((1, 4),)),
        "dt_bias": jnp.clip(-6.0 + 3.5 * jax.random.uniform(key_of[11], (2 * INNER,), jnp.float32) ** shard_levels(key_of[11], (2 * INNER,), ((0, 4),), -0.2, 0.2), -6.0, -2.5),
        "a_log": jnp.clip(2.77 * jax.random.uniform(key_of[12], (2 * INNER, STATE), jnp.float32) ** shard_levels(key_of[12], (2 * INNER, STATE), ((0, 4),), -0.2, 0.2), 0.0, 2.77),
        "skip_gain": jnp.clip(0.5 + 1.0 * jax.random.uniform(key_of[13], (2 * INNER,), jnp.float32) ** shard_levels(key_of[13], (2 * INNER,), ((0, 4),), -0.2, 0.2), 0.5, 1.5),
        "out_weight": bell_draw(key_of[14], (INNER, D), (INNER // 8) ** -0.5, 0.3125, ((0, 4),)),
        "cotangent": bell_draw(key_of[15], (ITEMS, ITEM, D), 1.0, 6.0, ((0, 8), (1, 4))),
    }


EPSILON = 1e-06

@jax.custom_vjp
def low(v):
    return lax.optimization_barrier(v.astype(jnp.bfloat16)).astype(jnp.float32)

@jax.custom_vjp
def low_back(v):
    return v

def low_keep(v):
    return (low(v), None)

def low_pass(kept, grad):
    return (grad,)

def back_keep(v):
    return (v, None)

def back_low(kept, grad):
    return (low(grad),)
low.defvjp(low_keep, low_pass)
low_back.defvjp(back_keep, back_low)

def matmul(left, right):
    return jnp.dot(left, right, precision=lax.Precision.HIGHEST, preferred_element_type=jnp.float32)

def causal_conv(values, kernel, offset_bias):
    length = values.shape[0]
    taps = kernel.shape[1]
    padded = jnp.pad(values, ((taps - 1, 0), (0, 0)))
    result = jnp.zeros_like(values) + offset_bias[None, :]
    for offset in range(taps):
        result = result + padded[offset:offset + length] * kernel[:, offset][None, :]
    return result

def ordered_scan(step_size, drive_in, b_input, c_output, decay_rates):
    channels = step_size.shape[1]

    def one_step(state_now, inputs):
        step_row, drive_row, b_row, c_row = inputs
        state_now = jnp.exp(step_row[:, None] * decay_rates) * state_now + (step_row * drive_row)[:, None] * b_row[None, :]
        return (state_now, lax.optimization_barrier(jnp.sum(state_now * c_row[None, :], axis=1)))

    def one_block(state_now, inputs):
        return lax.scan(one_step, state_now, inputs)
    shaped = tuple((a_item.reshape((a_item.shape[0] // BLOCK, BLOCK) + a_item.shape[1:]) for a_item in (step_size, drive_in, b_input, c_output)))
    state_zero = jnp.zeros((channels, b_input.shape[1]), step_size.dtype)
    _, outputs = lax.scan(jax.checkpoint(one_block), state_zero, shaped)
    return outputs.reshape(step_size.shape)

def direction_rows(table, direction):
    rest = table.shape[1:]
    return table.reshape((2, 2, INNER // 2) + rest)[:, direction].reshape((INNER,) + rest)

def direction_cols(table, direction):
    return table.reshape(table.shape[0], 2, 2, INNER // 2)[:, :, direction].reshape(table.shape[0], INNER)

def item_forward(params, inputs):
    in_weight, conv_weight, conv_bias, xproj_weight, dtproj_weight, dt_bias, a_log, skip_gain, out_weight = params
    values, live_rows, modulation = inputs
    shift_term = modulation[:D]
    scale_term = modulation[D:2 * D]
    gate_term = modulation[2 * D:]
    centred = values - lax.optimization_barrier(jnp.mean(values, axis=1, keepdims=True))
    spread = lax.optimization_barrier(jnp.mean(centred * centred, axis=1, keepdims=True))
    normed = low(live_rows[:, None] * (centred * lax.rsqrt(spread + EPSILON) * (1.0 + scale_term) + shift_term))
    projected = low_back(low(matmul(normed, in_weight)))
    shaped = projected.reshape(ITEM, 2, 2, INNER // 2)
    scan_input = shaped[:, :, 0, :].reshape(ITEM, INNER)
    gate_input = shaped[:, :, 1, :].reshape(ITEM, INNER)
    branch = jnp.zeros_like(values)
    for direction in range(2):
        conv_in = low_back(scan_input)
        gate_in = low_back(gate_input)
        mask_dir = live_rows
        if direction == 1:
            conv_in = jnp.flip(conv_in, 0)
            gate_in = jnp.flip(gate_in, 0)
            mask_dir = jnp.flip(mask_dir, 0)
        convolved = causal_conv(conv_in, direction_rows(conv_weight, direction), direction_rows(conv_bias, direction))
        mixer_in = low(mask_dir[:, None] * jax.nn.silu(convolved))
        doubled = low_back(matmul(mixer_in, direction_rows(xproj_weight, direction)))
        low_rank = low(doubled[:, :RANK])
        b_input = doubled[:, RANK:RANK + STATE]
        c_output = doubled[:, RANK + STATE:]
        pre_act = low_back(matmul(low_rank, direction_cols(dtproj_weight, direction)))
        step_size = jax.nn.softplus(pre_act + direction_rows(dt_bias, direction)[None, :])
        decay_rates = -jnp.exp(direction_rows(a_log, direction))
        scanned = ordered_scan(step_size, mixer_in, b_input, c_output, decay_rates)
        scanned = scanned + direction_rows(skip_gain, direction)[None, :] * mixer_in
        gated_out = low_back(low(scanned * jax.nn.silu(gate_in)))
        if direction == 1:
            gated_out = jnp.flip(gated_out, 0)
        branch = branch + matmul(gated_out, out_weight)
    branch = low_back(branch)
    return live_rows[:, None] * (values + gate_term[None, :] * branch)

def forward(tokens, cond, ada_weight, ada_bias, in_weight, conv_weight, conv_bias, xproj_weight, dtproj_weight, dt_bias, a_log, skip_gain, out_weight, live_mask):
    modulation = low_back(matmul(low(jax.nn.silu(cond)), ada_weight)) + ada_bias[None, :]
    params = (in_weight, conv_weight, conv_bias, xproj_weight, dtproj_weight, dt_bias, a_log, skip_gain, out_weight)
    return lax.map(jax.checkpoint(partial(item_forward, params)), (tokens, live_mask, modulation))

def reference(tokens, cond, counts, valid, ada_weight, ada_bias, in_weight, conv_weight, conv_bias, xproj_weight, dtproj_weight, dt_bias, a_log, skip_gain, out_weight, cotangent):
    item_index = jnp.arange(ITEMS, dtype=jnp.int32)
    owner_count = counts[item_index // SLOTS]
    live_items = (item_index % SLOTS < owner_count).astype(jnp.float32)
    live_mask = valid.astype(jnp.float32) * live_items[:, None]
    floats = tuple((array.astype(jnp.float32) for array in (tokens, cond, ada_weight, ada_bias, in_weight, conv_weight, conv_bias, xproj_weight, dtproj_weight, dt_bias, a_log, skip_gain, out_weight)))

    def with_mask(*arrays):
        return forward(*arrays, live_mask)
    mixed, pullback = jax.vjp(with_mask, *floats)
    grads = pullback(cotangent.astype(jnp.float32))
    return (mixed, grads[0], grads[1], grads[2], grads[3], grads[4], grads[5], grads[6], grads[7], grads[8], grads[9], grads[10], grads[11], grads[12])
```

```python
import functools

import jax
import jax.numpy as jnp
from jax import lax
from jax.experimental import pallas as pl
from jax.experimental.pallas import tpu as pltpu
from jax.sharding import PartitionSpec as P

EPSILON = 1e-06
LOG2E = 1.4426950408889634
CHUNK = 16
MARGIN = 8

bf16 = jnp.bfloat16
f32 = jnp.float32


def swap(block, axis, bit):
    count = lax.axis_size(axis)
    return lax.ppermute(block, axis, [(at, at ^ (1 << bit)) for at in range(count)])


def contract_rows(left, right):
    return lax.dot_general(
        left, right, (((0,), (0,)), ((), ())), preferred_element_type=f32
    )


def contract_cols(left, right):
    return lax.dot_general(
        left, right, (((1,), (1,)), ((), ())), preferred_element_type=f32
    )


def matmul(left, right):
    return jnp.dot(left, right, preferred_element_type=f32)


def ordered(bit, own, other, axis):
    return jnp.where(
        bit == 0,
        jnp.concatenate([own, other], axis),
        jnp.concatenate([other, own], axis),
    )


def halves(values, bit, axis):
    size = values.shape[axis] // 2
    keep = lax.dynamic_slice_in_dim(values, bit * size, size, axis)
    send = lax.dynamic_slice_in_dim(values, (1 - bit) * size, size, axis)
    return keep, send


def scatter_bits(values, axis, order):
    count = lax.axis_size(axis)
    bits = count.bit_length() - 1
    me = lax.axis_index(axis)
    rest = (values.shape[0] // count,) + values.shape[1:]
    values = values.reshape((2,) * bits + rest)
    left = list(range(bits - 1, -1, -1))
    for bit in order:
        at = left.index(bit)
        mine = (me >> bit) & 1
        keep = lax.dynamic_index_in_dim(values, mine, at, keepdims=False)
        send = lax.dynamic_index_in_dim(values, 1 - mine, at, keepdims=False)
        arrived = swap(send.astype(bf16), axis, bit)
        values = keep.astype(f32) + arrived.astype(f32)
        left.pop(at)
    return values


def gather_bits(values, axis, order):
    count = lax.axis_size(axis)
    bits = count.bit_length() - 1
    me = lax.axis_index(axis)
    have = []
    for bit in order:
        at = len([other for other in have if other > bit])
        mine = (me >> bit) & 1
        arrived = swap(values, axis, bit)
        values = jnp.where(
            mine == 0,
            jnp.stack([values, arrived], at),
            jnp.stack([arrived, values], at),
        )
        have.append(bit)
    return values.reshape((count,) + values.shape[bits:])


def bit_orders(axis):
    bits = lax.axis_size(axis).bit_length() - 1
    first = list(range(bits))
    second = list(range(bits))
    if bits > 1:
        second[0], second[1] = 1, 0
    return first, second


def shifted(padded, length, by, flip):
    return jnp.where(
        flip == 1,
        padded[MARGIN + by : MARGIN + by + length, :],
        padded[MARGIN - by : MARGIN - by + length, :],
    )


def conv_kernel(flip_ref, x_ref, mask_ref, taps_ref, xproj_ref, u_ref, dbl_ref, pad):
    step = pl.program_id(0)
    length, width = x_ref.shape
    flip = flip_ref[0]
    pad[0:MARGIN, :] = jnp.zeros((MARGIN, width), f32)
    pad[MARGIN + length :, :] = jnp.zeros((MARGIN, width), f32)
    pad[MARGIN : MARGIN + length, :] = x_ref[...].astype(f32)
    taps = taps_ref.shape[0] - 1
    conv = taps_ref[taps : taps + 1, :] + pad[MARGIN : MARGIN + length, :] * taps_ref[taps - 1 : taps, :]
    for by in range(1, taps):
        conv = conv + shifted(pad, length, by, flip) * taps_ref[taps - 1 - by : taps - by, :]
    u = (mask_ref[...] * (conv * jax.nn.sigmoid(conv))).astype(bf16)
    u_ref[...] = u
    part = matmul(u, xproj_ref[...])

    @pl.when(step == 0)
    def _():
        dbl_ref[...] = part

    @pl.when(step > 0)
    def _():
        dbl_ref[...] += part


def conv_back_kernel(
    flip_ref, x_ref, u_ref, mask_ref, taps_ref, xproj_ref, us_ref, dg_ref, xg_ref, packed_ref, pad
):
    length, width = x_ref.shape
    flip = flip_ref[0]
    pad[0:MARGIN, :] = jnp.zeros((MARGIN, width), f32)
    pad[MARGIN + length :, :] = jnp.zeros((MARGIN, width), f32)
    pad[MARGIN : MARGIN + length, :] = x_ref[...].astype(f32)
    taps = taps_ref.shape[0] - 1
    conv = taps_ref[taps : taps + 1, :] + pad[MARGIN : MARGIN + length, :] * taps_ref[taps - 1 : taps, :]
    for by in range(1, taps):
        conv = conv + shifted(pad, length, by, flip) * taps_ref[taps - 1 - by : taps - by, :]
    sig = jax.nn.sigmoid(conv)
    dg = dg_ref[...]
    u_grad = us_ref[...] + contract_cols(dg, xproj_ref[...])
    conv_grad = u_grad * mask_ref[...] * (sig * (1.0 + conv * (1.0 - sig)))
    cols = dg.shape[1]
    packed_ref[0:cols, :] = matmul(jnp.transpose(dg.astype(f32)).astype(bf16), u_ref[...])
    for by in range(taps):
        moved = pad[MARGIN : MARGIN + length, :] if by == 0 else shifted(pad, length, by, flip)
        row = cols + taps - 1 - by
        packed_ref[row : row + 1, :] = jnp.sum(conv_grad * moved, axis=0, keepdims=True)
    packed_ref[cols + taps : cols + taps + 1, :] = jnp.sum(conv_grad, axis=0, keepdims=True)
    rest = packed_ref.shape[0] - cols - taps - 1
    packed_ref[cols + taps + 1 :, :] = jnp.zeros((rest, width), f32)
    pad[MARGIN : MARGIN + length, :] = conv_grad
    grad = conv_grad * taps_ref[taps - 1 : taps, :]
    for by in range(1, taps):
        grad = grad + shifted(pad, length, by, 1 - flip) * taps_ref[taps - 1 - by : taps - by, :]
    xg_ref[...] = grad.astype(bf16)


def conv_call(flip, x, mask, taps, xproj, width):
    length, channels = x.shape
    cols = xproj.shape[1]
    return pl.pallas_call(
        conv_kernel,
        grid=(channels // width,),
        in_specs=[
            pl.BlockSpec(memory_space=pltpu.SMEM),
            pl.BlockSpec((length, width), lambda j: (0, j)),
            pl.BlockSpec((length, 1), lambda j: (0, 0)),
            pl.BlockSpec((taps.shape[0], width), lambda j: (0, j)),
            pl.BlockSpec((width, cols), lambda j: (j, 0)),
        ],
        out_specs=[
            pl.BlockSpec((length, width), lambda j: (0, j)),
            pl.BlockSpec((length, cols), lambda j: (0, 0)),
        ],
        out_shape=[
            jax.ShapeDtypeStruct((length, channels), bf16),
            jax.ShapeDtypeStruct((length, cols), f32),
        ],
        scratch_shapes=[pltpu.VMEM((length + 2 * MARGIN, width), f32)],
        compiler_params=pltpu.CompilerParams(vmem_limit_bytes=32 * 1024 * 1024),
        cost_estimate=pl.CostEstimate(flops=3000000000, bytes_accessed=4000000, transcendentals=400000),
        name="conv_forward",
    )(flip, x, mask, taps, xproj)


def conv_back_call(flip, x, u, mask, taps, xproj, us, dg, width):
    length, channels = x.shape
    cols = xproj.shape[1]
    rows = -(-(cols + taps.shape[0]) // 8) * 8
    return pl.pallas_call(
        conv_back_kernel,
        grid=(channels // width,),
        in_specs=[
            pl.BlockSpec(memory_space=pltpu.SMEM),
            pl.BlockSpec((length, width), lambda j: (0, j)),
            pl.BlockSpec((length, width), lambda j: (0, j)),
            pl.BlockSpec((length, 1), lambda j: (0, 0)),
            pl.BlockSpec((taps.shape[0], width), lambda j: (0, j)),
            pl.BlockSpec((width, cols), lambda j: (j, 0)),
            pl.BlockSpec((length, width), lambda j: (0, j)),
            pl.BlockSpec((length, cols), lambda j: (0, 0)),
        ],
        out_specs=[
            pl.BlockSpec((length, width), lambda j: (0, j)),
            pl.BlockSpec((rows, width), lambda j: (0, j)),
        ],
        out_shape=[
            jax.ShapeDtypeStruct((length, channels), bf16),
            jax.ShapeDtypeStruct((rows, channels), f32),
        ],
        scratch_shapes=[pltpu.VMEM((length + 2 * MARGIN, width), f32)],
        compiler_params=pltpu.CompilerParams(vmem_limit_bytes=32 * 1024 * 1024),
        cost_estimate=pl.CostEstimate(flops=4000000000, bytes_accessed=6000000, transcendentals=400000),
        name="conv_backward",
    )(flip, x, u, mask, taps, xproj, us, dg)


def scan_kernel(
    states, flip_ref, dbl_ref, dtp_ref, vec_ref, rate_ref, u_ref, z_ref, gg_ref,
    gated_ref, zg_ref, us_ref, part_ref, packed_ref,
    b_wide, c_wide, b_diag, c_diag, delta_s, drive_s, yg_s, y_s, r_s, w_s, low_t, rank_s,
    decay_s, state_s, prior_s, b_acc, c_acc,
):
    step = pl.program_id(0)
    length, width = u_ref.shape
    rank = dtp_ref.shape[0]
    group = CHUNK * states
    chunks = length // CHUNK
    flip = flip_ref[0]

    @pl.when(step == 0)
    def _():
        dbl = dbl_ref[...]
        turned = jnp.transpose(dbl)
        low_t[...] = turned[:rank, :].astype(bf16)
        for t in range(length):
            b_wide[t * states : (t + 1) * states, :] = jnp.broadcast_to(
                turned[rank : rank + states, t : t + 1], (states, 128)
            )
            c_wide[t * states : (t + 1) * states, :] = jnp.broadcast_to(
                turned[rank + states : rank + 2 * states, t : t + 1], (states, 128)
            )
        low = dbl.astype(bf16)
        row = lax.broadcasted_iota(jnp.int32, (dbl.shape[1], group), 0)
        col = lax.broadcasted_iota(jnp.int32, (dbl.shape[1], group), 1)
        pick_b = jnp.where(row == rank + col % states, 1.0, 0.0).astype(bf16)
        pick_c = jnp.where(row == rank + states + col % states, 1.0, 0.0).astype(bf16)
        at_row = lax.broadcasted_iota(jnp.int32, (length, group), 0)
        at_col = lax.broadcasted_iota(jnp.int32, (length, group), 1)
        same = (at_row % CHUNK) == (at_col // states)
        b_diag[...] = jnp.where(same, matmul(low, pick_b), 0.0).astype(bf16)
        c_diag[...] = jnp.where(same, matmul(low, pick_c), 0.0).astype(bf16)
        b_acc[...] = jnp.zeros_like(b_acc)
        c_acc[...] = jnp.zeros_like(c_acc)
        rank_s[...] = jnp.zeros_like(rank_s)

    low = dbl_ref[:, :rank].astype(bf16)
    pre = matmul(low, dtp_ref[...]) + vec_ref[0:1, :]
    delta = jnp.maximum(pre, 0.0) + jnp.log1p(jnp.exp(-jnp.abs(pre)))
    delta_s[...] = delta
    drive_s[...] = delta * u_ref[...].astype(f32)
    z = z_ref[...].astype(f32)
    yg_s[...] = gg_ref[...].astype(f32) * (z * jax.nn.sigmoid(z))
    rates = rate_ref[...]
    rates2 = rates * LOG2E

    def ahead(chunk, state):
        for at in range(CHUNK):
            turn = chunk * CHUNK + at
            t = jnp.where(flip == 1, length - 1 - turn, turn)
            row = pl.multiple_of(t * states, states)
            d = jnp.broadcast_to(delta_s[pl.ds(t, 1), :], (states, width))
            x = jnp.broadcast_to(drive_s[pl.ds(t, 1), :], (states, width))
            b = jnp.concatenate([b_wide[pl.ds(row, states), :]] * (width // 128), axis=1)
            decay = jnp.exp2(d * rates2)
            prior = decay * state
            state = prior + x * b
            decay_s[pl.ds(row, states), :] = decay
            prior_s[pl.ds(row, states), :] = prior.astype(bf16)
            state_s[pl.ds(row, states), :] = state.astype(bf16)
        place = jnp.where(flip == 1, chunks - 1 - chunk, chunk)
        rows = pl.ds(pl.multiple_of(place * CHUNK, CHUNK), CHUNK)
        block = state_s[pl.ds(pl.multiple_of(place * group, group), group), :]
        y_s[rows, :] = matmul(c_diag[rows, :], block)
        c_acc[rows, :] += contract_cols(yg_s[rows, :].astype(bf16), block)
        return state

    lax.fori_loop(0, chunks, ahead, jnp.zeros((states, width), f32))

    sum_row = lax.broadcasted_iota(jnp.int32, (CHUNK, group), 0)
    sum_col = lax.broadcasted_iota(jnp.int32, (CHUNK, group), 1)
    ones = jnp.where(sum_row == sum_col // states, 1.0, 0.0).astype(bf16)

    def back(chunk, carry):
        carried, total = carry
        for at in range(CHUNK):
            turn = chunk * CHUNK + at
            t = jnp.where(flip == 1, turn, length - 1 - turn)
            row = pl.multiple_of(t * states, states)
            d = jnp.broadcast_to(delta_s[pl.ds(t, 1), :], (states, width))
            x = jnp.broadcast_to(yg_s[pl.ds(t, 1), :], (states, width))
            c = jnp.concatenate([c_wide[pl.ds(row, states), :]] * (width // 128), axis=1)
            adj = carried + x * c
            both = adj * prior_s[pl.ds(row, states), :].astype(f32)
            total = total + d * both
            prior_s[pl.ds(row, states), :] = (both * rates).astype(bf16)
            state_s[pl.ds(row, states), :] = adj.astype(bf16)
            carried = decay_s[pl.ds(row, states), :] * adj
        place = jnp.where(flip == 1, chunk, chunks - 1 - chunk)
        rows = pl.ds(pl.multiple_of(place * CHUNK, CHUNK), CHUNK)
        wide = pl.ds(pl.multiple_of(place * group, group), group)
        block = state_s[wide, :]
        r_s[rows, :] = matmul(b_diag[rows, :], block)
        w_s[rows, :] = matmul(ones, prior_s[wide, :])
        b_acc[rows, :] += contract_cols(drive_s[rows, :].astype(bf16), block)
        return carried, total

    zero = jnp.zeros((states, width), f32)
    _, total = lax.fori_loop(0, chunks, back, (zero, zero))

    u = u_ref[...].astype(f32)
    z = z_ref[...].astype(f32)
    sig = jax.nn.sigmoid(z)
    skip = vec_ref[1:2, :]
    y = y_s[...] + skip * u
    gated_ref[...] = (y * (z * sig)).astype(bf16)
    zg_ref[...] = (gg_ref[...].astype(f32) * y * (sig * (1.0 + z * (1.0 - sig)))).astype(bf16)
    yg = yg_s[...]
    r = r_s[...]
    us_ref[...] = delta_s[...] * r + skip * yg
    pre = matmul(low, dtp_ref[...]) + vec_ref[0:1, :]
    pre_grad = (w_s[...] + u * r) * jax.nn.sigmoid(pre)
    pre_low = pre_grad.astype(bf16)
    rank_s[...] += contract_cols(pre_low, dtp_ref[...])
    packed_ref[0:rank, :] = matmul(low_t[...], pre_low)
    packed_ref[rank : rank + states, :] = total * rates
    packed_ref[rank + states : rank + states + 1, :] = jnp.sum(pre_grad, axis=0, keepdims=True)
    packed_ref[rank + states + 1 : rank + states + 2, :] = jnp.sum(yg * u, axis=0, keepdims=True)
    rest = packed_ref.shape[0] - rank - states - 2
    packed_ref[rank + states + 2 :, :] = jnp.zeros((rest, width), f32)

    @pl.when(step == pl.num_programs(0) - 1)
    def _():
        at_row = lax.broadcasted_iota(jnp.int32, (length, group), 0)
        at_col = lax.broadcasted_iota(jnp.int32, (length, group), 1)
        same = (at_row % CHUNK) == (at_col // states)
        row = lax.broadcasted_iota(jnp.int32, (group, 2 * states), 0)
        col = lax.broadcasted_iota(jnp.int32, (group, 2 * states), 1)
        put_b = jnp.where(col == row % states, 1.0, 0.0)
        put_c = jnp.where(col == states + row % states, 1.0, 0.0)
        hi = lax.Precision.HIGHEST
        pair = jnp.dot(
            jnp.where(same, b_acc[...], 0.0), put_b, precision=hi, preferred_element_type=f32
        ) + jnp.dot(jnp.where(same, c_acc[...], 0.0), put_c, precision=hi, preferred_element_type=f32)
        part_ref[...] = jnp.concatenate([rank_s[...], pair], axis=1)


def scan_call(flip, dbl, dtproj, vec, rates, u, z, gg, width):
    length, channels = u.shape
    states = rates.shape[0]
    rank = dtproj.shape[0]
    cols = dbl.shape[1]
    group = CHUNK * states
    rows = -(-(rank + states + 2) // 8) * 8
    whole = lambda *shape: pl.BlockSpec(shape, lambda j: (0,) * len(shape))
    block = lambda count: pl.BlockSpec((count, width), lambda j: (0, j))
    return pl.pallas_call(
        functools.partial(scan_kernel, states),
        grid=(channels // width,),
        in_specs=[
            pl.BlockSpec(memory_space=pltpu.SMEM),
            whole(length, cols),
            block(rank),
            block(2),
            block(states),
            block(length),
            block(length),
            block(length),
        ],
        out_specs=[block(length), block(length), block(length), whole(length, cols), block(rows)],
        out_shape=[
            jax.ShapeDtypeStruct((length, channels), bf16),
            jax.ShapeDtypeStruct((length, channels), bf16),
            jax.ShapeDtypeStruct((length, channels), f32),
            jax.ShapeDtypeStruct((length, cols), f32),
            jax.ShapeDtypeStruct((rows, channels), f32),
        ],
        scratch_shapes=[
            pltpu.VMEM((length * states, 128), f32),
            pltpu.VMEM((length * states, 128), f32),
            pltpu.VMEM((length, group), bf16),
            pltpu.VMEM((length, group), bf16),
            pltpu.VMEM((length, width), f32),
            pltpu.VMEM((length, width), f32),
            pltpu.VMEM((length, width), f32),
            pltpu.VMEM((length, width), f32),
            pltpu.VMEM((length, width), f32),
            pltpu.VMEM((length, width), f32),
            pltpu.VMEM((rank, length), bf16),
            pltpu.VMEM((length, rank), f32),
            pltpu.VMEM((length * states, width), f32),
            pltpu.VMEM((length * states, width), bf16),
            pltpu.VMEM((length * states, width), bf16),
            pltpu.VMEM((length, group), f32),
            pltpu.VMEM((length, group), f32),
        ],
        compiler_params=pltpu.CompilerParams(vmem_limit_bytes=48 * 1024 * 1024),
        cost_estimate=pl.CostEstimate(
            flops=30000000000, bytes_accessed=8000000, transcendentals=7000000
        ),
        name="scan_both",
    )(flip, dbl, dtproj, vec, rates, u, z, gg)


def local(
    tokens,
    cond,
    counts,
    valid,
    ada_weight,
    ada_bias,
    in_weight,
    conv_weight,
    conv_bias,
    xproj_weight,
    dtproj_weight,
    dt_bias,
    a_log,
    skip_gain,
    out_weight,
    cotangent,
):
    slot_count, shard_rows, model = tokens.shape
    dirs = lax.axis_size("dir")
    dps = lax.axis_size("dp")
    length = valid.shape[1]
    me = lax.axis_index("dir")
    dp_index = lax.axis_index("dp")
    core = me & 1
    chip = me >> 1
    half = in_weight.shape[1] // 2
    rank = dtproj_weight.shape[0]
    states = a_log.shape[1]
    flip = core.astype(jnp.int32).reshape(1)
    slots = range(slot_count)

    live_slots = (jnp.arange(slot_count) < counts[0]).astype(f32)
    full_mask = valid.astype(f32) * live_slots[:, None]
    mask_cols = full_mask[:, :, None]
    local_mask = lax.dynamic_slice_in_dim(full_mask, me * shard_rows, shard_rows, 1)

    def gather_rows(block):
        other = swap(block, "dir", 1)
        both = ordered(chip, block[None], other[None], 0)
        there = swap(both, "dir", 0)
        return ordered(core, both[:, None], there[:, None], 1).reshape(length, model)

    full_tokens = [gather_rows(tokens[slot]) for slot in slots]
    full_cot = [gather_rows(cotangent[slot]) for slot in slots]

    in_keep, in_send = halves(in_weight, core, 1)
    in_there = swap(in_send, "dir", 0)
    in_mixed = ordered(core, in_keep, in_there, 1)
    out_there = swap(out_weight, "dir", 0)
    out_pair = ordered(core, out_weight, out_there, 0)

    cond_act = jax.nn.silu(cond.astype(f32)).astype(bf16)
    modulation = matmul(cond_act, ada_weight) + ada_bias.astype(f32)[None, :]
    first, second = bit_orders("dp")
    act_all = gather_bits(cond_act, "dp", first)

    taps = jnp.concatenate(
        [jnp.transpose(conv_weight.astype(f32)), conv_bias.astype(f32)[None, :]], 0
    )
    vec = jnp.stack([dt_bias, skip_gain])
    rates = -jnp.exp(jnp.transpose(a_log))

    def sum_rows(partial):
        blocks = partial.reshape(dirs // 2, 2, shard_rows, model)
        keep = lax.dynamic_index_in_dim(blocks, core, 1, keepdims=False)
        send = lax.dynamic_index_in_dim(blocks, 1 - core, 1, keepdims=False)
        pair = keep + swap(send, "dir", 0)
        mine = lax.dynamic_index_in_dim(pair, chip, 0, keepdims=False)
        theirs = lax.dynamic_index_in_dim(pair, 1 - chip, 0, keepdims=False)
        return mine + swap(theirs.astype(bf16), "dir", 1).astype(f32)

    def forward(slot):
        shift = modulation[slot, :model]
        scale = modulation[slot, model : 2 * model]
        gate = modulation[slot, 2 * model :]
        mask = mask_cols[slot]
        raw = full_tokens[slot].astype(f32)
        centred = raw - jnp.mean(raw, axis=1, keepdims=True)
        spread = jnp.mean(centred * centred, axis=1, keepdims=True)
        hat = centred * lax.rsqrt(spread + EPSILON)
        normed = (mask * (hat * (1.0 + scale[None, :]) + shift[None, :])).astype(bf16)
        own = matmul(normed, in_mixed).astype(bf16)
        other = swap(own, "dir", 0)
        x = ordered(core, own[:, :half], other[:, :half], 1)
        z = ordered(core, own[:, half:], other[:, half:], 1)
        u, part = conv_call(flip, x, mask, taps, xproj_weight, half)
        dbl = part + swap(part, "dir", 1)
        branch_grad = (mask * full_cot[slot].astype(f32) * gate[None, :]).astype(bf16)
        gg = contract_cols(branch_grad, out_pair).astype(bf16)
        return normed, x, z, u, dbl, branch_grad, gg

    def scan(kept):
        normed, x, z, u, dbl, branch_grad, gg = kept
        return scan_call(flip, dbl, dtproj_weight, vec, rates, u, z, gg, channels_block)

    def sum_halves(values):
        keep, send = halves(values, core, 1)
        return (keep.astype(f32) + swap(send, "dir", 0).astype(f32)).astype(bf16)

    channels_block = 512 if dt_bias.shape[0] % 512 == 0 else 128

    kept, scanned = [], []
    for slot in slots:
        kept.append(forward(slot))
    for slot in slots:
        scanned.append(scan(kept[slot]))

    z_sums, gate_sums, mixed, gate_grads, x_sums = [], [], [], [], []
    conv_packs = []
    for slot in slots:
        normed, x, z, u, dbl, branch_grad, gg = kept[slot]
        gated, zg, us, part, packed = scanned[slot]
        dg = (part + swap(part, "dir", 1)).astype(bf16)
        xg, conv_pack = conv_back_call(
            flip, x, u, mask_cols[slot], taps, xproj_weight, us, dg, half
        )
        conv_packs.append(conv_pack)
        gate_sum = sum_halves(gated)
        z_sums.append(sum_halves(zg))
        x_sums.append(sum_halves(xg))
        gate_sums.append(gate_sum)
        branch = sum_rows(matmul(gate_sum, out_weight))
        gate = modulation[slot, 2 * model :]
        mask = local_mask[slot][:, None]
        raw = tokens[slot].astype(f32)
        mixed.append(mask * (raw + gate[None, :] * branch))
        res_grad = mask * cotangent[slot].astype(f32)
        gate_grads.append(jnp.sum(res_grad * branch, axis=0))

    normed_all = jnp.concatenate([kept[slot][0] for slot in slots], 0)
    branch_all = jnp.concatenate([kept[slot][5] for slot in slots], 0)
    out_part = contract_rows(branch_all, jnp.concatenate(gate_sums, 0))
    out_sum = jnp.transpose(scatter_bits(out_part, "dp", first))
    scan_pack = sum(scanned[slot][4] for slot in slots)
    z_part = contract_rows(normed_all, jnp.concatenate(z_sums, 0))
    z_sum = scatter_bits(z_part, "dp", second)

    token_grads, mod_rows = [], []
    for slot in slots:
        scale = modulation[slot, model : 2 * model]
        mask = local_mask[slot][:, None]
        raw = tokens[slot].astype(f32)
        centred = raw - jnp.mean(raw, axis=1, keepdims=True)
        spread = jnp.mean(centred * centred, axis=1, keepdims=True)
        inverse = lax.rsqrt(spread + EPSILON)
        hat = centred * inverse
        proj_grad = jnp.concatenate([x_sums[slot], z_sums[slot]], 1)
        normed_grad = mask * sum_rows(contract_cols(proj_grad, in_mixed))
        scaled = normed_grad * hat
        q = normed_grad * (1.0 + scale[None, :])
        token_part = inverse * (
            q
            - jnp.mean(q, axis=1, keepdims=True)
            - hat * jnp.mean(q * hat, axis=1, keepdims=True)
        )
        res_grad = mask * cotangent[slot].astype(f32)
        token_grads.append(res_grad + token_part)
        mod_rows.append(
            jnp.concatenate(
                [jnp.sum(normed_grad, axis=0), jnp.sum(scaled, axis=0), gate_grads[slot]]
            )
        )

    x_part = contract_rows(normed_all, jnp.concatenate(x_sums, 0))
    split = half // 2
    x_sum = jnp.concatenate(
        [
            scatter_bits(x_part[:, :split], "dp", first),
            scatter_bits(x_part[:, split:], "dp", second),
        ],
        1,
    )
    keep_sum = jnp.where(core == 0, x_sum, z_sum)
    send_sum = jnp.where(core == 0, z_sum, x_sum)
    in_sum = ordered(core, keep_sum, swap(send_sum, "dir", 0), 1)

    pack = jnp.concatenate([sum(conv_packs), scan_pack], 0)
    pack = gather_bits(scatter_bits(pack, "dp", second).astype(bf16), "dp", second[::-1])
    pack = pack.reshape(-1, pack.shape[-1]).astype(f32)
    cols = xproj_weight.shape[1]
    tap_count = conv_weight.shape[1]
    base = conv_packs[0].shape[0]
    xproj_sum = jnp.transpose(pack[:cols])
    kernel_sum = jnp.transpose(pack[cols : cols + tap_count])
    offset_sum = pack[cols + tap_count]
    dtproj_sum = pack[base : base + rank]
    rate_sum = jnp.transpose(pack[base + rank : base + rank + states])
    step_bias_sum = pack[base + rank + states]
    skip_sum = pack[base + rank + states + 1]

    mod_part = jnp.stack(mod_rows)
    mod_pair = mod_part + swap(mod_part, "dir", 0)
    mod_total = mod_pair + swap(mod_pair, "dir", 1)
    mod_low = mod_total.astype(bf16)
    cond_value = cond.astype(f32)
    sig = jax.nn.sigmoid(cond_value)
    cond_grad = contract_cols(mod_low, ada_weight) * sig * (1.0 + cond_value * (1.0 - sig))
    columns = ada_weight.shape[1] // dirs
    mod_mine = lax.dynamic_slice_in_dim(mod_low, me * columns, columns, 1)
    mod_all = gather_bits(mod_mine, "dp", first).reshape(-1, columns)
    rows = ada_weight.shape[0] // dps
    act_mine = lax.dynamic_slice_in_dim(act_all.reshape(-1, model), dp_index * rows, rows, 1)
    ada_sum = contract_rows(act_mine, mod_all)
    bias_part = jnp.sum(mod_total, axis=0)
    bias_sum = bias_part
    bits = dps.bit_length() - 1
    bias_blocks = bias_part.reshape((2,) * bits + (-1,))
    left = list(range(bits - 1, -1, -1))
    for bit in first:
        at = left.index(bit)
        mine = (dp_index >> bit) & 1
        keep = lax.dynamic_index_in_dim(bias_blocks, mine, at, keepdims=False)
        send = lax.dynamic_index_in_dim(bias_blocks, 1 - mine, at, keepdims=False)
        bias_blocks = keep + swap(send, "dp", bit)
        left.pop(at)
    bias_sum = bias_blocks

    return (
        jnp.stack(mixed),
        jnp.stack(token_grads),
        cond_grad,
        ada_sum,
        bias_sum,
        in_sum,
        kernel_sum,
        offset_sum,
        xproj_sum,
        dtproj_sum,
        step_bias_sum,
        rate_sum,
        skip_sum,
        out_sum,
    )


def solution(mesh):
    in_specs = (
        P("dp", "dir", None),
        P("dp", None),
        P("dp"),
        P("dp", None),
        P(),
        P(),
        P(None, "dir"),
        P("dir", None),
        P("dir"),
        P("dir", None),
        P(None, "dir"),
        P("dir"),
        P("dir", None),
        P("dir"),
        P("dir", None),
        P("dp", "dir", None),
    )
    out_specs = (
        P("dp", "dir", None),
        P("dp", "dir", None),
        P("dp", None),
        P("dp", "dir"),
        P("dp"),
        P("dp", "dir"),
        P("dir", None),
        P("dir"),
        P("dir", None),
        P(None, "dir"),
        P("dir"),
        P("dir", None),
        P("dir"),
        P("dir", "dp"),
    )
    return jax.shard_map(local, mesh=mesh, in_specs=in_specs, out_specs=out_specs, check_vma=False)
```

```python
import functools

import jax
import jax.numpy as jnp
from jax import lax
from jax.experimental import pallas as pl
from jax.experimental.pallas import tpu as pltpu
from jax.sharding import PartitionSpec as P

EPSILON = 1e-06
LOG2E = 1.4426950408889634
CHUNK = 16
MARGIN = 8

bf16 = jnp.bfloat16
f32 = jnp.float32


def swap(block, axis, bit):
    count = lax.axis_size(axis)
    return lax.ppermute(block, axis, [(at, at ^ (1 << bit)) for at in range(count)])


def contract_rows(left, right):
    return lax.dot_general(
        left, right, (((0,), (0,)), ((), ())), preferred_element_type=f32
    )


def contract_cols(left, right):
    return lax.dot_general(
        left, right, (((1,), (1,)), ((), ())), preferred_element_type=f32
    )


def matmul(left, right):
    return jnp.dot(left, right, preferred_element_type=f32)


def ordered(bit, own, other, axis):
    return jnp.where(
        bit == 0,
        jnp.concatenate([own, other], axis),
        jnp.concatenate([other, own], axis),
    )


def halves(values, bit, axis):
    size = values.shape[axis] // 2
    keep = lax.dynamic_slice_in_dim(values, bit * size, size, axis)
    send = lax.dynamic_slice_in_dim(values, (1 - bit) * size, size, axis)
    return keep, send


class Scatter:
    def __init__(self, values, axis, order):
        count = lax.axis_size(axis)
        self.bits = count.bit_length() - 1
        self.axis, self.order = axis, list(order)
        self.values = values.reshape((2,) * self.bits + (values.shape[0] // count,) + values.shape[1:])
        self.left = list(range(self.bits - 1, -1, -1))
        self.split()

    def split(self):
        if not self.order:
            return
        at = self.left.index(self.order[0])
        mine = (lax.axis_index(self.axis) >> self.order[0]) & 1
        self.keep = lax.dynamic_index_in_dim(self.values, mine, at, keepdims=False)
        send = lax.dynamic_index_in_dim(self.values, 1 - mine, at, keepdims=False)
        self.send = send.astype(bf16)

    def step(self):
        bit = self.order.pop(0)
        self.left.remove(bit)
        arrived = swap(self.send, self.axis, bit)
        self.values = self.keep.astype(f32) + arrived.astype(f32)
        self.split()

    def finish(self):
        while self.order:
            self.step()
        return self.values


def scatter_bits(values, axis, order):
    return Scatter(values, axis, order).finish()


def ahead_of(later, *earlier):
    return lax.optimization_barrier((later,) + earlier)


def gather_bits(values, axis, order):
    count = lax.axis_size(axis)
    bits = count.bit_length() - 1
    me = lax.axis_index(axis)
    have = []
    for bit in order:
        at = len([other for other in have if other > bit])
        mine = (me >> bit) & 1
        arrived = swap(values, axis, bit)
        values = jnp.where(
            mine == 0,
            jnp.stack([values, arrived], at),
            jnp.stack([arrived, values], at),
        )
        have.append(bit)
    return values.reshape((count,) + values.shape[bits:])


def bit_orders(axis):
    bits = lax.axis_size(axis).bit_length() - 1
    first = list(range(bits))
    second = list(range(bits))
    if bits > 1:
        second[0], second[1] = 1, 0
    return first, second


def shifted(padded, length, by, flip):
    return jnp.where(
        flip == 1,
        padded[MARGIN + by : MARGIN + by + length, :],
        padded[MARGIN - by : MARGIN - by + length, :],
    )


def conv_kernel(flip_ref, x_ref, mask_ref, taps_ref, xproj_ref, u_ref, dbl_ref, pad):
    step = pl.program_id(0)
    length, width = x_ref.shape
    flip = flip_ref[0]
    pad[0:MARGIN, :] = jnp.zeros((MARGIN, width), f32)
    pad[MARGIN + length :, :] = jnp.zeros((MARGIN, width), f32)
    pad[MARGIN : MARGIN + length, :] = x_ref[...].astype(f32)
    taps = taps_ref.shape[0] - 1
    conv = taps_ref[taps : taps + 1, :] + pad[MARGIN : MARGIN + length, :] * taps_ref[taps - 1 : taps, :]
    for by in range(1, taps):
        conv = conv + shifted(pad, length, by, flip) * taps_ref[taps - 1 - by : taps - by, :]
    u = (mask_ref[...] * (conv * jax.nn.sigmoid(conv))).astype(bf16)
    u_ref[...] = u
    part = matmul(u, xproj_ref[...])

    @pl.when(step == 0)
    def _():
        dbl_ref[...] = part

    @pl.when(step > 0)
    def _():
        dbl_ref[...] += part


def conv_back_kernel(
    flip_ref, x_ref, u_ref, mask_ref, taps_ref, xproj_ref, us_ref, dg_ref, xg_ref, packed_ref, pad
):
    length, width = x_ref.shape
    flip = flip_ref[0]
    pad[0:MARGIN, :] = jnp.zeros((MARGIN, width), f32)
    pad[MARGIN + length :, :] = jnp.zeros((MARGIN, width), f32)
    pad[MARGIN : MARGIN + length, :] = x_ref[...].astype(f32)
    taps = taps_ref.shape[0] - 1
    conv = taps_ref[taps : taps + 1, :] + pad[MARGIN : MARGIN + length, :] * taps_ref[taps - 1 : taps, :]
    for by in range(1, taps):
        conv = conv + shifted(pad, length, by, flip) * taps_ref[taps - 1 - by : taps - by, :]
    sig = jax.nn.sigmoid(conv)
    dg = dg_ref[...]
    u_grad = us_ref[...] + contract_cols(dg, xproj_ref[...])
    conv_grad = u_grad * mask_ref[...] * (sig * (1.0 + conv * (1.0 - sig)))
    cols = dg.shape[1]
    packed_ref[0:cols, :] = matmul(jnp.transpose(dg.astype(f32)).astype(bf16), u_ref[...])
    for by in range(taps):
        moved = pad[MARGIN : MARGIN + length, :] if by == 0 else shifted(pad, length, by, flip)
        row = cols + taps - 1 - by
        packed_ref[row : row + 1, :] = jnp.sum(conv_grad * moved, axis=0, keepdims=True)
    packed_ref[cols + taps : cols + taps + 1, :] = jnp.sum(conv_grad, axis=0, keepdims=True)
    rest = packed_ref.shape[0] - cols - taps - 1
    packed_ref[cols + taps + 1 :, :] = jnp.zeros((rest, width), f32)
    pad[MARGIN : MARGIN + length, :] = conv_grad
    grad = conv_grad * taps_ref[taps - 1 : taps, :]
    for by in range(1, taps):
        grad = grad + shifted(pad, length, by, 1 - flip) * taps_ref[taps - 1 - by : taps - by, :]
    xg_ref[...] = grad.astype(bf16)


def conv_call(flip, x, mask, taps, xproj, width):
    length, channels = x.shape
    cols = xproj.shape[1]
    return pl.pallas_call(
        conv_kernel,
        grid=(channels // width,),
        in_specs=[
            pl.BlockSpec(memory_space=pltpu.SMEM),
            pl.BlockSpec((length, width), lambda j: (0, j)),
            pl.BlockSpec((length, 1), lambda j: (0, 0)),
            pl.BlockSpec((taps.shape[0], width), lambda j: (0, j)),
            pl.BlockSpec((width, cols), lambda j: (j, 0)),
        ],
        out_specs=[
            pl.BlockSpec((length, width), lambda j: (0, j)),
            pl.BlockSpec((length, cols), lambda j: (0, 0)),
        ],
        out_shape=[
            jax.ShapeDtypeStruct((length, channels), bf16),
            jax.ShapeDtypeStruct((length, cols), f32),
        ],
        scratch_shapes=[pltpu.VMEM((length + 2 * MARGIN, width), f32)],
        compiler_params=pltpu.CompilerParams(vmem_limit_bytes=32 * 1024 * 1024),
        cost_estimate=pl.CostEstimate(flops=3000000000, bytes_accessed=4000000, transcendentals=400000),
        name="conv_forward",
    )(flip, x, mask, taps, xproj)


def conv_back_call(flip, x, u, mask, taps, xproj, us, dg, width):
    length, channels = x.shape
    cols = xproj.shape[1]
    rows = -(-(cols + taps.shape[0]) // 8) * 8
    return pl.pallas_call(
        conv_back_kernel,
        grid=(channels // width,),
        in_specs=[
            pl.BlockSpec(memory_space=pltpu.SMEM),
            pl.BlockSpec((length, width), lambda j: (0, j)),
            pl.BlockSpec((length, width), lambda j: (0, j)),
            pl.BlockSpec((length, 1), lambda j: (0, 0)),
            pl.BlockSpec((taps.shape[0], width), lambda j: (0, j)),
            pl.BlockSpec((width, cols), lambda j: (j, 0)),
            pl.BlockSpec((length, width), lambda j: (0, j)),
            pl.BlockSpec((length, cols), lambda j: (0, 0)),
        ],
        out_specs=[
            pl.BlockSpec((length, width), lambda j: (0, j)),
            pl.BlockSpec((rows, width), lambda j: (0, j)),
        ],
        out_shape=[
            jax.ShapeDtypeStruct((length, channels), bf16),
            jax.ShapeDtypeStruct((rows, channels), f32),
        ],
        scratch_shapes=[pltpu.VMEM((length + 2 * MARGIN, width), f32)],
        compiler_params=pltpu.CompilerParams(vmem_limit_bytes=32 * 1024 * 1024),
        cost_estimate=pl.CostEstimate(flops=4000000000, bytes_accessed=6000000, transcendentals=400000),
        name="conv_backward",
    )(flip, x, u, mask, taps, xproj, us, dg)


def spread(dbl_ref, first, b_wide, c_wide, rows_s, states):
    length, cols = dbl_ref.shape
    rest = dbl_ref[...]
    row = lax.broadcasted_iota(jnp.int32, (cols, cols), 0)
    col = lax.broadcasted_iota(jnp.int32, (cols, cols), 1)
    rows = jnp.zeros((length, cols), f32)
    for part in range(3):
        piece = rest.astype(bf16)
        rest = rest - piece.astype(f32)
        pick = ((row == first + col % (2*states)) & (col // (2*states) == part))
        rows = rows + matmul(piece, jnp.where(pick, 1.0, 0.0).astype(bf16))
    rows_s[...] = rows
    which = lax.broadcasted_iota(jnp.int32, (states, cols), 0)
    lane = lax.broadcasted_iota(jnp.int32, (states, cols), 1)
    mine = jnp.where(lane % states == which, 1.0, 0.0)
    row = lax.broadcasted_iota(jnp.int32, (cols, 2*cols), 0)
    col = lax.broadcasted_iota(jnp.int32, (cols, 2*cols), 1)
    wide = jnp.where((row % (2*states)) // states == col // cols, 1.0, 0.0).astype(bf16)
    def some(at, _):
        left = [(mine*jnp.broadcast_to(rows_s[pl.ds(at*CHUNK+t, 1), :], (states, cols))).astype(bf16) for t in range(CHUNK)]
        got = matmul(jnp.concatenate(left, 0), wide)
        here = pl.ds(pl.multiple_of(at*CHUNK*states, CHUNK*states), CHUNK*states)
        b_wide[here, :] = got[:, :cols]
        c_wide[here, :] = got[:, cols:]
        return 0
    lax.fori_loop(0, length//CHUNK, some, 0, unroll=4)

def tiles_of(values):
    return [values[:, at:at+128] for at in range(0, values.shape[1], 128)]

def fold(values, tmp, tt, states):
    for at, tile in enumerate(tiles_of(values)):
        total = tile[:8]
        for part in range(1, states//8):
            total = total + tile[part*8:(part+1)*8]
        tmp[at, pl.ds(tt//8*64 + tt%8, 8, stride=8), :] = total

def add_tiles(values):
    parts = tiles_of(values)
    total = parts[0]
    for part in parts[1:]:
        total = total + part
    return total

def unfold(tmp, out, base):
    for at in range(out.shape[1]//128):
        for part in range(CHUNK//8):
            acc = tmp[at, part*64:part*64+8, :]
            for row in range(1, 8):
                acc = acc + tmp[at, part*64+row*8:part*64+row*8+8, :]
            out[pl.ds(pl.multiple_of(base+part*8, 8), 8), at*128:(at+1)*128] = acc

def collect(acc, tmp, out, length, states):
    which = lax.broadcasted_iota(jnp.int32, (states, 128), 0)
    lane = lax.broadcasted_iota(jnp.int32, (states, 128), 1)
    mine = which == lane
    def some(at, _):
        base = pl.multiple_of(at*CHUNK, CHUNK)
        for tt in range(CHUNK):
            sums = jnp.sum(acc[pl.ds((base+tt)*states, states), :], axis=1, keepdims=True)
            fold(jnp.where(mine, sums, 0.0), tmp, tt, states)
        unfold(tmp, out, base)
        return 0
    lax.fori_loop(0, length//CHUNK, some, 0, unroll=4)

def fwd_kernel(states, flip_ref, dbl_ref, dtp_ref, vec_ref, rate2_ref, u_ref, z_ref, gg_ref,
               gated_ref, zg_ref, delta_ref, yg_ref, prior_ref, cout_ref,
               b_wide, c_wide, drive_s, y_s, y_tmp, c_acc, rows_s):
    step = pl.program_id(0)
    length, width = u_ref.shape
    rank = dtp_ref.shape[0]
    group = CHUNK*states
    chunks = length//CHUNK
    flip = flip_ref[0]
    @pl.when(step == 0)
    def _():
        spread(dbl_ref, rank, b_wide, c_wide, rows_s, states)
        c_acc[...] = jnp.zeros_like(c_acc)
    low = dbl_ref[:, :rank].astype(bf16)
    pre = matmul(low, dtp_ref[...]) + vec_ref[0:1, :]
    delta = jnp.maximum(pre, 0.0) + jnp.log1p(jnp.exp(-jnp.abs(pre)))
    delta_ref[...] = delta
    drive_s[...] = delta * u_ref[...].astype(f32)
    z = z_ref[...].astype(f32)
    yg_ref[...] = gg_ref[...].astype(f32) * (z * (0.5 + 0.5*jnp.tanh(0.5*z)))
    def run(flipped):
        def ahead(chunk, state):
            place = chunks-1-chunk if flipped else chunk
            base = pl.multiple_of(place*CHUNK, CHUNK)
            wide = pl.multiple_of(place*group, group)
            for at in range(CHUNK):
                tt = CHUNK-1-at if flipped else at
                t = base + tt
                here = pl.ds(wide + tt*states, states)
                d = jnp.broadcast_to(delta_ref[pl.ds(t,1),:], (states,width))
                x = jnp.broadcast_to(drive_s[pl.ds(t,1),:], (states,width))
                g = jnp.broadcast_to(yg_ref[pl.ds(t,1),:], (states,width))
                b = jnp.concatenate([b_wide[here,:]]*(width//128), axis=1)
                c = jnp.concatenate([c_wide[here,:]]*(width//128), axis=1)
                prior = jnp.exp2(d*rate2_ref[...])*state
                state = prior + x*b
                prior_ref[here,:] = prior.astype(bf16)
                fold(state*c, y_tmp, tt, states)
                c_acc[here,:] += add_tiles(state*g)
            unfold(y_tmp, y_s, base)
            return state
        lax.fori_loop(0, chunks, ahead, jnp.zeros((states,width), f32))
    pl.when(flip == 0)(lambda: run(False))
    pl.when(flip == 1)(lambda: run(True))
    u = u_ref[...].astype(f32)
    z = z_ref[...].astype(f32)
    sig = (0.5 + 0.5*jnp.tanh(0.5*z))
    y = y_s[...] + vec_ref[1:2,:]*u
    gated_ref[...] = (y*(z*sig)).astype(bf16)
    zg_ref[...] = (gg_ref[...].astype(f32)*y*(sig*(1.0+z*(1.0-sig)))).astype(bf16)
    @pl.when(step == pl.num_programs(0)-1)
    def _():
        collect(c_acc, y_tmp, rows_s, length, states)
        cout_ref[...] = rows_s[:, :states]

def bwd_kernel(states, flip_ref, dbl_ref, dtp_ref, vec_ref, rate2_ref, u_ref, delta_ref, yg_ref, prior_ref, cout_ref,
               us_ref, part_ref, packed_ref,
               b_wide, c_wide, drive_s, r_s, w_s, low_t, rank_s, r_tmp, w_tmp, b_acc, rows_s):
    step = pl.program_id(0)
    length, width = u_ref.shape
    rank = dtp_ref.shape[0]
    group = CHUNK*states
    chunks = length//CHUNK
    flip = flip_ref[0]
    @pl.when(step == 0)
    def _():
        low_t[...] = jnp.transpose(dbl_ref[...])[:rank,:].astype(bf16)
        spread(dbl_ref, rank, b_wide, c_wide, rows_s, states)
        b_acc[...] = jnp.zeros_like(b_acc)
        rank_s[...] = jnp.zeros_like(rank_s)
    u = u_ref[...].astype(f32)
    drive_s[...] = delta_ref[...]*u
    def run(flipped):
        def back(chunk, carry):
            carried, total = carry
            place = chunk if flipped else chunks-1-chunk
            base = pl.multiple_of(place*CHUNK, CHUNK)
            wide = pl.multiple_of(place*group, group)
            for at in range(CHUNK):
                tt = at if flipped else CHUNK-1-at
                t = base + tt
                here = pl.ds(wide + tt*states, states)
                d = jnp.broadcast_to(delta_ref[pl.ds(t,1),:], (states,width))
                x = jnp.broadcast_to(yg_ref[pl.ds(t,1),:], (states,width))
                e = jnp.broadcast_to(drive_s[pl.ds(t,1),:], (states,width))
                b = jnp.concatenate([b_wide[here,:]]*(width//128), axis=1)
                c = jnp.concatenate([c_wide[here,:]]*(width//128), axis=1)
                power = d*rate2_ref[...]
                adj = carried + x*c
                moved = (adj*prior_ref[here,:].astype(f32))*power
                total = total + moved
                fold(moved, w_tmp, tt, states)
                fold(adj*b, r_tmp, tt, states)
                b_acc[here,:] += add_tiles(adj*e)
                carried = jnp.exp2(power)*adj
            unfold(w_tmp, w_s, base)
            unfold(r_tmp, r_s, base)
            return carried, total
        zero = jnp.zeros((states,width), f32)
        _, total = lax.fori_loop(0, chunks, back, (zero, zero))
        packed_ref[rank:rank+states,:] = total*(1.0/LOG2E)
    pl.when(flip == 0)(lambda: run(False))
    pl.when(flip == 1)(lambda: run(True))
    yg = yg_ref[...]
    r = r_s[...]
    delta = delta_ref[...]
    us_ref[...] = delta*r + vec_ref[1:2,:]*yg
    low = dbl_ref[:, :rank].astype(bf16)
    pre = matmul(low, dtp_ref[...]) + vec_ref[0:1,:]
    sig = jnp.exp(pre-delta)
    ratio = jnp.where(delta > 1e-30, sig/jnp.maximum(delta, 1e-30), 1.0)
    pre_grad = w_s[...]*(1.0/LOG2E)*ratio + u*r*sig
    pre_low = pre_grad.astype(bf16)
    rank_s[...] += contract_cols(pre_low, dtp_ref[...])
    packed_ref[0:rank,:] = matmul(low_t[...], pre_low)
    packed_ref[rank+states:rank+states+1,:] = jnp.sum(pre_grad, axis=0, keepdims=True)
    packed_ref[rank+states+1:rank+states+2,:] = jnp.sum(yg*u, axis=0, keepdims=True)
    rest = packed_ref.shape[0]-rank-states-2
    packed_ref[rank+states+2:,:] = jnp.zeros((rest,width), f32)
    @pl.when(step == pl.num_programs(0)-1)
    def _():
        collect(b_acc, r_tmp, rows_s, length, states)
        part_ref[...] = jnp.concatenate([rank_s[...], rows_s[:, :states], cout_ref[...]], axis=1)


def scan_specs(length, channels, states, rank, cols, width):
    whole = lambda *shape: pl.BlockSpec(shape, lambda j: (0,) * len(shape))
    block = lambda count: pl.BlockSpec((count, width), lambda j: (0, j))
    out = lambda rows, kind: jax.ShapeDtypeStruct((rows, channels), kind)
    return whole, block, out


def forward_call(flip, dbl, dtproj, vec, rates2, u, z, gg, width):
    length, channels = u.shape
    states, rank, cols = rates2.shape[0], dtproj.shape[0], dbl.shape[1]
    whole, block, out = scan_specs(length, channels, states, rank, cols, width)
    return pl.pallas_call(
        functools.partial(fwd_kernel, states),
        grid=(channels // width,),
        in_specs=[
            pl.BlockSpec(memory_space=pltpu.SMEM),
            whole(length, cols),
            block(rank),
            block(2),
            block(states),
            block(length),
            block(length),
            block(length),
        ],
        out_specs=[block(length)] * 4 + [block(length * states), whole(length, states)],
        out_shape=[
            out(length, bf16),
            out(length, bf16),
            out(length, f32),
            out(length, f32),
            out(length * states, bf16),
            jax.ShapeDtypeStruct((length, states), f32),
        ],
        scratch_shapes=[
            pltpu.VMEM((length * states, 128), f32),
            pltpu.VMEM((length * states, 128), f32),
            pltpu.VMEM((length, width), f32),
            pltpu.VMEM((length, width), f32),
            pltpu.VMEM((width // 128, CHUNK * 8, 128), f32),
            pltpu.VMEM((length * states, 128), f32),
            pltpu.VMEM((length, cols), f32),
        ],
        compiler_params=pltpu.CompilerParams(vmem_limit_bytes=40 * 1024 * 1024),
        cost_estimate=pl.CostEstimate(
            flops=16000000000, bytes_accessed=20000000, transcendentals=7000000
        ),
        name="scan_forward",
    )(flip, dbl, dtproj, vec, rates2, u, z, gg)


def backward_call(flip, dbl, dtproj, vec, rates2, u, delta, yg, prior, cout, width):
    length, channels = u.shape
    states, rank, cols = rates2.shape[0], dtproj.shape[0], dbl.shape[1]
    rows = -(-(rank + states + 2) // 8) * 8
    whole, block, out = scan_specs(length, channels, states, rank, cols, width)
    return pl.pallas_call(
        functools.partial(bwd_kernel, states),
        grid=(channels // width,),
        in_specs=[
            pl.BlockSpec(memory_space=pltpu.SMEM),
            whole(length, cols),
            block(rank),
            block(2),
            block(states),
            block(length),
            block(length),
            block(length),
            block(length * states),
            whole(length, states),
        ],
        out_specs=[block(length), whole(length, cols), block(rows)],
        out_shape=[
            out(length, f32),
            jax.ShapeDtypeStruct((length, cols), f32),
            out(rows, f32),
        ],
        scratch_shapes=[
            pltpu.VMEM((length * states, 128), f32),
            pltpu.VMEM((length * states, 128), f32),
            pltpu.VMEM((length, width), f32),
            pltpu.VMEM((length, width), f32),
            pltpu.VMEM((length, width), f32),
            pltpu.VMEM((rank, length), bf16),
            pltpu.VMEM((length, rank), f32),
            pltpu.VMEM((width // 128, CHUNK * 8, 128), f32),
            pltpu.VMEM((width // 128, CHUNK * 8, 128), f32),
            pltpu.VMEM((length * states, 128), f32),
            pltpu.VMEM((length, cols), f32),
        ],
        compiler_params=pltpu.CompilerParams(vmem_limit_bytes=40 * 1024 * 1024),
        cost_estimate=pl.CostEstimate(
            flops=22000000000, bytes_accessed=20000000, transcendentals=7000000
        ),
        name="scan_backward",
    )(flip, dbl, dtproj, vec, rates2, u, delta, yg, prior, cout)


def local(
    tokens,
    cond,
    counts,
    valid,
    ada_weight,
    ada_bias,
    in_weight,
    conv_weight,
    conv_bias,
    xproj_weight,
    dtproj_weight,
    dt_bias,
    a_log,
    skip_gain,
    out_weight,
    cotangent,
):
    slot_count, shard_rows, model = tokens.shape
    dirs = lax.axis_size("dir")
    dps = lax.axis_size("dp")
    length = valid.shape[1]
    me = lax.axis_index("dir")
    dp_index = lax.axis_index("dp")
    core = me & 1
    chip = me >> 1
    half = in_weight.shape[1] // 2
    rank = dtproj_weight.shape[0]
    states = a_log.shape[1]
    flip = core.astype(jnp.int32).reshape(1)
    slots = range(slot_count)

    live_slots = (jnp.arange(slot_count) < counts[0]).astype(f32)
    full_mask = valid.astype(f32) * live_slots[:, None]
    mask_cols = full_mask[:, :, None]
    local_mask = lax.dynamic_slice_in_dim(full_mask, me * shard_rows, shard_rows, 1)

    def gather_rows(block):
        other = swap(block, "dir", 1)
        both = ordered(chip, block[None], other[None], 0)
        there = swap(both, "dir", 0)
        return ordered(core, both[:, None], there[:, None], 1).reshape(length, model)

    full_tokens = [gather_rows(tokens[slot]) for slot in slots]
    full_cot = [gather_rows(cotangent[slot]) for slot in slots]

    in_keep, in_send = halves(in_weight, core, 1)
    in_there = swap(in_send, "dir", 0)
    in_mixed = ordered(core, in_keep, in_there, 1)
    out_there = swap(out_weight, "dir", 0)
    out_pair = ordered(core, out_weight, out_there, 0)

    cond_act = jax.nn.silu(cond.astype(f32)).astype(bf16)
    modulation = matmul(cond_act, ada_weight) + ada_bias.astype(f32)[None, :]
    first, second = bit_orders("dp")
    act_all = gather_bits(cond_act, "dp", first)

    taps = jnp.concatenate(
        [jnp.transpose(conv_weight.astype(f32)), conv_bias.astype(f32)[None, :]], 0
    )
    vec = jnp.stack([dt_bias, skip_gain])
    rates2 = -jnp.exp(jnp.transpose(a_log)) * LOG2E

    def sum_rows(partial):
        blocks = partial.reshape(dirs // 2, 2, shard_rows, model)
        keep = lax.dynamic_index_in_dim(blocks, core, 1, keepdims=False)
        send = lax.dynamic_index_in_dim(blocks, 1 - core, 1, keepdims=False)
        pair = keep + swap(send, "dir", 0)
        mine = lax.dynamic_index_in_dim(pair, chip, 0, keepdims=False)
        theirs = lax.dynamic_index_in_dim(pair, 1 - chip, 0, keepdims=False)
        return mine + swap(theirs.astype(bf16), "dir", 1).astype(f32)

    def forward(slot):
        shift = modulation[slot, :model]
        scale = modulation[slot, model : 2 * model]
        gate = modulation[slot, 2 * model :]
        mask = mask_cols[slot]
        raw = full_tokens[slot].astype(f32)
        centred = raw - jnp.mean(raw, axis=1, keepdims=True)
        spread = jnp.mean(centred * centred, axis=1, keepdims=True)
        hat = centred * lax.rsqrt(spread + EPSILON)
        normed = (mask * (hat * (1.0 + scale[None, :]) + shift[None, :])).astype(bf16)
        own = matmul(normed, in_weight).astype(bf16)
        other = swap(own, "dir", 0)
        x = jnp.where(core == 0, own, other)
        z = jnp.where(core == 0, other, own)
        u, part = conv_call(flip, x, mask, taps, xproj_weight, half)
        dbl = part + swap(part, "dir", 1)
        branch_grad = (mask * full_cot[slot].astype(f32) * gate[None, :]).astype(bf16)
        gg = contract_cols(branch_grad, out_pair).astype(bf16)
        return normed, x, z, u, dbl, branch_grad, gg

    def sum_halves(values):
        keep, send = halves(values, core, 1)
        return (keep.astype(f32) + swap(send, "dir", 0).astype(f32)).astype(bf16)

    channels_block = 512 if dt_bias.shape[0] % 512 == 0 else 128

    kept = [forward(slot) for slot in slots]
    scanned = []
    for slot in slots:
        normed, x, z, u, dbl, branch_grad, gg = kept[slot]
        scanned.append(
            forward_call(flip, dbl, dtproj_weight, vec, rates2, u, z, gg, channels_block)
        )

    normed_all = jnp.concatenate([kept[slot][0] for slot in slots], 0)
    branch_all = jnp.concatenate([kept[slot][5] for slot in slots], 0)
    gate_sums = [sum_halves(scanned[slot][0]) for slot in slots]
    z_sums = [sum_halves(scanned[slot][1]) for slot in slots]
    out_part = Scatter(contract_rows(branch_all, jnp.concatenate(gate_sums, 0)), "dp", first)
    z_part = Scatter(contract_rows(normed_all, jnp.concatenate(z_sums, 0)), "dp", second)

    backs = []
    for slot in slots:
        normed, x, z, u, dbl, branch_grad, gg = kept[slot]
        gated, zg, delta, yg, prior, cout = scanned[slot]
        u, out_part.send, z_part.send = ahead_of(u, out_part.send, z_part.send)
        backs.append(
            backward_call(
                flip, dbl, dtproj_weight, vec, rates2, u, delta, yg, prior, cout, channels_block
            )
        )
        out_part.step()
        z_part.step()

    mixed, gate_grads, x_sums, conv_packs = [], [], [], []
    for slot in slots:
        normed, x, z, u, dbl, branch_grad, gg = kept[slot]
        us, part, packed = backs[slot]
        dg = (part + swap(part, "dir", 1)).astype(bf16)
        xg, conv_pack = conv_back_call(
            flip, x, u, mask_cols[slot], taps, xproj_weight, us, dg, half
        )
        conv_packs.append(conv_pack)
        x_sums.append(sum_halves(xg))
        branch = sum_rows(matmul(gate_sums[slot], out_weight))
        gate = modulation[slot, 2 * model :]
        mask = local_mask[slot][:, None]
        raw = tokens[slot].astype(f32)
        mixed.append(mask * (raw + gate[None, :] * branch))
        res_grad = mask * cotangent[slot].astype(f32)
        gate_grads.append(jnp.sum(res_grad * branch, axis=0))

    out_sum = jnp.transpose(out_part.finish())
    scan_pack = sum(backs[slot][2] for slot in slots)
    z_sum = z_part.finish()

    token_grads, mod_rows = [], []
    for slot in slots:
        scale = modulation[slot, model : 2 * model]
        mask = local_mask[slot][:, None]
        raw = tokens[slot].astype(f32)
        centred = raw - jnp.mean(raw, axis=1, keepdims=True)
        spread = jnp.mean(centred * centred, axis=1, keepdims=True)
        inverse = lax.rsqrt(spread + EPSILON)
        hat = centred * inverse
        proj_grad = jnp.concatenate([x_sums[slot], z_sums[slot]], 1)
        normed_grad = mask * sum_rows(contract_cols(proj_grad, in_mixed))
        scaled = normed_grad * hat
        q = normed_grad * (1.0 + scale[None, :])
        token_part = inverse * (
            q
            - jnp.mean(q, axis=1, keepdims=True)
            - hat * jnp.mean(q * hat, axis=1, keepdims=True)
        )
        res_grad = mask * cotangent[slot].astype(f32)
        token_grads.append(res_grad + token_part)
        mod_rows.append(
            jnp.concatenate(
                [jnp.sum(normed_grad, axis=0), jnp.sum(scaled, axis=0), gate_grads[slot]]
            )
        )

    x_part = contract_rows(normed_all, jnp.concatenate(x_sums, 0))
    split = half // 2
    x_sum = jnp.concatenate(
        [
            scatter_bits(x_part[:, :split], "dp", first),
            scatter_bits(x_part[:, split:], "dp", second),
        ],
        1,
    )
    keep_sum = jnp.where(core == 0, x_sum, z_sum)
    send_sum = jnp.where(core == 0, z_sum, x_sum)
    in_sum = ordered(core, keep_sum, swap(send_sum, "dir", 0), 1)

    pack = jnp.concatenate([sum(conv_packs), scan_pack], 0)
    pack = gather_bits(scatter_bits(pack, "dp", second).astype(bf16), "dp", second[::-1])
    pack = pack.reshape(-1, pack.shape[-1]).astype(f32)
    cols = xproj_weight.shape[1]
    tap_count = conv_weight.shape[1]
    base = conv_packs[0].shape[0]
    xproj_sum = jnp.transpose(pack[:cols])
    kernel_sum = jnp.transpose(pack[cols : cols + tap_count])
    offset_sum = pack[cols + tap_count]
    dtproj_sum = pack[base : base + rank]
    rate_sum = jnp.transpose(pack[base + rank : base + rank + states])
    step_bias_sum = pack[base + rank + states]
    skip_sum = pack[base + rank + states + 1]

    mod_part = jnp.stack(mod_rows)
    mod_pair = mod_part + swap(mod_part, "dir", 0)
    mod_total = mod_pair + swap(mod_pair, "dir", 1)
    mod_low = mod_total.astype(bf16)
    cond_value = cond.astype(f32)
    sig = jax.nn.sigmoid(cond_value)
    cond_grad = contract_cols(mod_low, ada_weight) * sig * (1.0 + cond_value * (1.0 - sig))
    columns = ada_weight.shape[1] // dirs
    mod_mine = lax.dynamic_slice_in_dim(mod_low, me * columns, columns, 1)
    mod_all = gather_bits(mod_mine, "dp", first).reshape(-1, columns)
    rows = ada_weight.shape[0] // dps
    act_mine = lax.dynamic_slice_in_dim(act_all.reshape(-1, model), dp_index * rows, rows, 1)
    ada_sum = contract_rows(act_mine, mod_all)
    bias_part = jnp.sum(mod_total, axis=0)
    bias_sum = bias_part
    bits = dps.bit_length() - 1
    bias_blocks = bias_part.reshape((2,) * bits + (-1,))
    left = list(range(bits - 1, -1, -1))
    for bit in first:
        at = left.index(bit)
        mine = (dp_index >> bit) & 1
        keep = lax.dynamic_index_in_dim(bias_blocks, mine, at, keepdims=False)
        send = lax.dynamic_index_in_dim(bias_blocks, 1 - mine, at, keepdims=False)
        bias_blocks = keep + swap(send, "dp", bit)
        left.pop(at)
    bias_sum = bias_blocks

    return (
        jnp.stack(mixed),
        jnp.stack(token_grads),
        cond_grad,
        ada_sum,
        bias_sum,
        in_sum,
        kernel_sum,
        offset_sum,
        xproj_sum,
        dtproj_sum,
        step_bias_sum,
        rate_sum,
        skip_sum,
        out_sum,
    )


def solution(mesh):
    in_specs = (
        P("dp", "dir", None),
        P("dp", None),
        P("dp"),
        P("dp", None),
        P(),
        P(),
        P(None, "dir"),
        P("dir", None),
        P("dir"),
        P("dir", None),
        P(None, "dir"),
        P("dir"),
        P("dir", None),
        P("dir"),
        P("dir", None),
        P("dp", "dir", None),
    )
    out_specs = (
        P("dp", "dir", None),
        P("dp", "dir", None),
        P("dp", None),
        P("dp", "dir"),
        P("dp"),
        P("dp", "dir"),
        P("dir", None),
        P("dir"),
        P("dir", None),
        P(None, "dir"),
        P("dir"),
        P("dir", None),
        P("dir"),
        P("dir", "dp"),
    )
    return jax.shard_map(local, mesh=mesh, in_specs=in_specs, out_specs=out_specs, check_vma=False)
```

```python
import functools

import jax
import jax.numpy as jnp
from jax import lax
from jax.experimental import pallas as pl
from jax.experimental.pallas import tpu as pltpu
from jax.sharding import PartitionSpec as P

EPSILON = 1e-06
LOG2E = 1.4426950408889634
CHUNK = 16
MARGIN = 8

bf16 = jnp.bfloat16
f32 = jnp.float32


def swap(block, axis, bit):
    count = lax.axis_size(axis)
    return lax.ppermute(block, axis, [(at, at ^ (1 << bit)) for at in range(count)])


def contract_rows(left, right):
    return lax.dot_general(
        left, right, (((0,), (0,)), ((), ())), preferred_element_type=f32
    )


def contract_cols(left, right):
    return lax.dot_general(
        left, right, (((1,), (1,)), ((), ())), preferred_element_type=f32
    )


def matmul(left, right):
    return jnp.dot(left, right, preferred_element_type=f32)


def ordered(bit, own, other, axis):
    return jnp.where(
        bit == 0,
        jnp.concatenate([own, other], axis),
        jnp.concatenate([other, own], axis),
    )


def halves(values, bit, axis):
    size = values.shape[axis] // 2
    keep = lax.dynamic_slice_in_dim(values, bit * size, size, axis)
    send = lax.dynamic_slice_in_dim(values, (1 - bit) * size, size, axis)
    return keep, send


class Scatter:
    def __init__(self, values, axis, order):
        self.axis, self.order = axis, list(order)
        bits = len(order)
        self.values = values.reshape((2,) * bits + (values.shape[0] >> bits,) + values.shape[1:])
        self.left = sorted(order, reverse=True)
        self.split()

    def split(self):
        if not self.order:
            return
        at = self.left.index(self.order[0])
        mine = (lax.axis_index(self.axis) >> self.order[0]) & 1
        self.keep = lax.dynamic_index_in_dim(self.values, mine, at, keepdims=False)
        send = lax.dynamic_index_in_dim(self.values, 1 - mine, at, keepdims=False)
        self.send = send.astype(bf16)

    def step(self, *earlier):
        bit = self.order.pop(0)
        self.left.remove(bit)
        arrived = after(swap(self.send, self.axis, bit), *earlier)
        self.values = self.keep.astype(f32) + arrived.astype(f32)
        self.split()


class SharedSum:
    def __init__(self, values, axis, order):
        self.axis = axis
        few = list(order[:2])
        self.plan = [("halve", bit) for bit in few] + [("add", bit) for bit in order[2:]]
        self.plan += [("join", bit) for bit in few[::-1]]
        self.values = values
        self.begin()

    def begin(self):
        kind, bit = self.plan[0] if self.plan else ("", 0)
        self.mine = (lax.axis_index(self.axis) >> bit) & 1
        if kind == "halve":
            self.keep, self.send = halves(self.values, self.mine, 0)
            self.send = self.send.astype(bf16)
        else:
            self.keep = self.send = self.values.astype(bf16)

    def step(self, *earlier):
        kind, bit = self.plan.pop(0)
        arrived = after(swap(self.send, self.axis, bit), *earlier)
        if kind == "join":
            self.values = ordered(self.mine, self.keep, arrived, 0)
        else:
            self.values = self.keep.astype(f32) + arrived.astype(f32)
        self.begin()


def after(values, *earlier):
    return lax.optimization_barrier((values, earlier))[0] if earlier else values


def gather_bit(values, axis, bit, have):
    at = len([other for other in have if other > bit])
    mine = (lax.axis_index(axis) >> bit) & 1
    arrived = swap(values, axis, bit)
    have.append(bit)
    return jnp.where(
        mine == 0, jnp.stack([values, arrived], at), jnp.stack([arrived, values], at)
    )


def gather_bits(values, axis, order):
    have = []
    for bit in order:
        values = gather_bit(values, axis, bit, have)
    return values.reshape((lax.axis_size(axis),) + values.shape[len(order) :])


def bit_orders(axis):
    bits = lax.axis_size(axis).bit_length() - 1
    first = list(range(bits))
    second = list(range(bits))
    if bits > 1:
        second[0], second[1] = 1, 0
    return first, second


def shifted(padded, length, by, flip):
    return jnp.where(
        flip == 1,
        padded[MARGIN + by : MARGIN + by + length, :],
        padded[MARGIN - by : MARGIN - by + length, :],
    )


def norm_kernel(me_ref, own_ref, over_ref, beside_ref, far_ref, mask_ref, mod_ref, weight_ref, normed_ref, proj_ref):
    rows = own_ref.shape[1]

    @pl.when(pl.program_id(0) == 0)
    def _():
        shift = mod_ref[0:1, :]
        scale = mod_ref[1:2, :]
        for code, block in ((0, own_ref), (2, over_ref), (1, beside_ref), (3, far_ref)):
            here = pl.ds(pl.multiple_of((me_ref[0] ^ code) * rows, rows), rows)
            raw = block[0].astype(f32)
            centred = raw - jnp.mean(raw, axis=1, keepdims=True)
            spread = jnp.mean(centred * centred, axis=1, keepdims=True)
            hat = centred * lax.rsqrt(spread + EPSILON)
            normed_ref[here, :] = (mask_ref[here, :] * (hat * (1.0 + scale) + shift)).astype(bf16)

    proj_ref[...] = matmul(normed_ref[...], weight_ref[...]).astype(bf16)


def norm_call(me, blocks, slot, mask, mod, weight, width):
    _, rows, model = blocks[0].shape
    length = mask.shape[0]
    channels = weight.shape[1]
    whole = lambda *shape: pl.BlockSpec(shape, lambda j: (0,) * len(shape))
    return pl.pallas_call(
        norm_kernel,
        grid=(channels // width,),
        in_specs=[pl.BlockSpec(memory_space=pltpu.SMEM)]
        + [pl.BlockSpec((1, rows, model), lambda j: (slot, 0, 0))] * 4
        + [whole(length, 1), whole(2, model), pl.BlockSpec((model, width), lambda j: (0, j))],
        out_specs=[whole(length, model), pl.BlockSpec((length, width), lambda j: (0, j))],
        out_shape=[
            jax.ShapeDtypeStruct((length, model), bf16),
            jax.ShapeDtypeStruct((length, channels), bf16),
        ],
        compiler_params=pltpu.CompilerParams(vmem_limit_bytes=12 * 1024 * 1024),
        cost_estimate=pl.CostEstimate(flops=1000, bytes_accessed=1000, transcendentals=0),
        name="norm_project",
    )(me, *blocks, mask, mod, weight)


def gate_kernel(
    chunk, me_ref, side_ref, own_ref, over_ref, beside_ref, far_ref, mask_ref, gate_ref, mine_ref,
    theirs_ref, keep_ref, give_ref, out_ref, grad_s
):
    rows = own_ref.shape[1]
    step = pl.program_id(0)

    @pl.when(step == 0)
    def _():
        for code, block in ((0, own_ref), (2, over_ref), (1, beside_ref), (3, far_ref)):
            here = pl.ds(pl.multiple_of((me_ref[0] ^ code) * rows, rows), rows)
            grad_s[here, :] = (mask_ref[here, :] * block[0].astype(f32) * gate_ref[...]).astype(bf16)
        for side in range(2):

            @pl.when(side_ref[0] == side)
            def _():
                for at, start in enumerate(range(0, grad_s.shape[1], 2 * chunk)):
                    to = slice(at * chunk, (at + 1) * chunk)
                    first = grad_s[:, start : start + chunk]
                    second = grad_s[:, start + chunk : start + 2 * chunk]
                    keep_ref[:, to] = second if side else first
                    give_ref[:, to] = first if side else second

    core = me_ref[0] & 1

    @pl.when(step == core)
    def _():
        out_ref[...] = contract_cols(grad_s[...], mine_ref[...]).astype(bf16)

    @pl.when(step != core)
    def _():
        out_ref[...] = contract_cols(grad_s[...], theirs_ref[...]).astype(bf16)


def gate_call(me, side, blocks, slot, mask, gate, mine, theirs, chunk):
    _, rows, model = blocks[0].shape
    length = mask.shape[0]
    quarter = mine.shape[0]
    whole = lambda *shape: pl.BlockSpec(shape, lambda j: (0,) * len(shape))
    return pl.pallas_call(
        functools.partial(gate_kernel, chunk),
        grid=(2,),
        in_specs=[pl.BlockSpec(memory_space=pltpu.SMEM)] * 2
        + [pl.BlockSpec((1, rows, model), lambda j: (slot, 0, 0))] * 4
        + [whole(length, 1), whole(1, model), whole(quarter, model), whole(quarter, model)],
        out_specs=[
            whole(length, model // 2),
            whole(length, model // 2),
            pl.BlockSpec((length, quarter), lambda j: (0, j)),
        ],
        out_shape=[
            jax.ShapeDtypeStruct((length, model // 2), bf16),
            jax.ShapeDtypeStruct((length, model // 2), bf16),
            jax.ShapeDtypeStruct((length, 2 * quarter), bf16),
        ],
        scratch_shapes=[pltpu.VMEM((length, model), bf16)],
        compiler_params=pltpu.CompilerParams(vmem_limit_bytes=16 * 1024 * 1024),
        cost_estimate=pl.CostEstimate(flops=1000, bytes_accessed=1000, transcendentals=0),
        name="gate_project",
    )(me, side, *blocks, mask, gate, mine, theirs)


def pick_rows(values_ref, parity, chips, rows):
    blocks = []
    for at in range(values_ref.shape[0] // rows // 2):
        start = pl.multiple_of((2 * at + parity) * rows, rows)
        blocks.append(values_ref[pl.ds(start, rows), :])
    return jnp.concatenate(blocks, 0)


def branch_kernel(rows, flip_ref, values_ref, weight_ref, keep_ref, send_ref):
    core = flip_ref[0]
    keep_ref[...] = matmul(pick_rows(values_ref, core, 2, rows), weight_ref[...])
    send_ref[...] = matmul(pick_rows(values_ref, 1 - core, 2, rows), weight_ref[...])


def branch_call(flip, values, weight, rows, width):
    count, depth = values.shape
    model = weight.shape[1]
    out = jax.ShapeDtypeStruct((count // 2, model), f32)
    return pl.pallas_call(
        functools.partial(branch_kernel, rows),
        grid=(model // width,),
        in_specs=[
            pl.BlockSpec(memory_space=pltpu.SMEM),
            pl.BlockSpec((count, depth), lambda j: (0, 0)),
            pl.BlockSpec((depth, width), lambda j: (0, j)),
        ],
        out_specs=[pl.BlockSpec((count // 2, width), lambda j: (0, j))] * 2,
        out_shape=[out, out],
        compiler_params=pltpu.CompilerParams(vmem_limit_bytes=10 * 1024 * 1024),
        cost_estimate=pl.CostEstimate(flops=1000, bytes_accessed=1000, transcendentals=0),
        name="branch_rows",
    )(flip, values, weight)


def proj_back_kernel(rows, flip_ref, x_ref, z_ref, first_ref, second_ref, keep_ref, send_ref, x_s, z_s):
    core = flip_ref[0]

    @pl.when(core == 0)
    def _():
        x_s[...] = x_ref[...]
        z_s[...] = z_ref[...]

    @pl.when(core == 1)
    def _():
        x_s[...] = z_ref[...]
        z_s[...] = x_ref[...]

    for parity, out_ref in ((core, keep_ref), (1 - core, send_ref)):
        out_ref[...] = contract_cols(pick_rows(x_s, parity, 2, rows), first_ref[...]) + contract_cols(
            pick_rows(z_s, parity, 2, rows), second_ref[...]
        )


def proj_back_call(flip, x, z, first, second, rows, width):
    count, depth = x.shape
    model = first.shape[0]
    out = jax.ShapeDtypeStruct((count // 2, model), f32)
    return pl.pallas_call(
        functools.partial(proj_back_kernel, rows),
        grid=(model // width,),
        in_specs=[
            pl.BlockSpec(memory_space=pltpu.SMEM),
            pl.BlockSpec((count, depth), lambda j: (0, 0)),
            pl.BlockSpec((count, depth), lambda j: (0, 0)),
            pl.BlockSpec((width, depth), lambda j: (j, 0)),
            pl.BlockSpec((width, depth), lambda j: (j, 0)),
        ],
        out_specs=[pl.BlockSpec((count // 2, width), lambda j: (0, j))] * 2,
        out_shape=[out, out],
        scratch_shapes=[pltpu.VMEM((count, depth), bf16)] * 2,
        compiler_params=pltpu.CompilerParams(vmem_limit_bytes=14 * 1024 * 1024),
        cost_estimate=pl.CostEstimate(flops=1000, bytes_accessed=1000, transcendentals=0),
        name="proj_back",
    )(flip, x, z, first, second)


def conv_kernel(
    flip_ref, own_ref, other_ref, mask_ref, taps_ref, xproj_ref, x_ref, z_ref, u_ref, dbl_ref, pad
):
    step = pl.program_id(0)
    length, width = own_ref.shape
    flip = flip_ref[0]

    @pl.when(flip == 0)
    def _():
        x_ref[...] = own_ref[...]
        z_ref[...] = other_ref[...]

    @pl.when(flip == 1)
    def _():
        x_ref[...] = other_ref[...]
        z_ref[...] = own_ref[...]

    pad[0:MARGIN, :] = jnp.zeros((MARGIN, width), f32)
    pad[MARGIN + length :, :] = jnp.zeros((MARGIN, width), f32)
    pad[MARGIN : MARGIN + length, :] = x_ref[...].astype(f32)
    taps = taps_ref.shape[0] - 1
    conv = taps_ref[taps : taps + 1, :] + pad[MARGIN : MARGIN + length, :] * taps_ref[taps - 1 : taps, :]
    for by in range(1, taps):
        conv = conv + shifted(pad, length, by, flip) * taps_ref[taps - 1 - by : taps - by, :]
    u = (mask_ref[...] * (conv * jax.nn.sigmoid(conv))).astype(bf16)
    u_ref[...] = u
    part = matmul(u, xproj_ref[...])

    @pl.when(step == 0)
    def _():
        dbl_ref[...] = part

    @pl.when(step > 0)
    def _():
        dbl_ref[...] += part


def conv_back_kernel(
    flip_ref, x_ref, u_ref, mask_ref, taps_ref, xproj_ref, us_ref, dg_ref, xg_ref, packed_ref, pad
):
    length, width = x_ref.shape
    flip = flip_ref[0]
    pad[0:MARGIN, :] = jnp.zeros((MARGIN, width), f32)
    pad[MARGIN + length :, :] = jnp.zeros((MARGIN, width), f32)
    pad[MARGIN : MARGIN + length, :] = x_ref[...].astype(f32)
    taps = taps_ref.shape[0] - 1
    conv = taps_ref[taps : taps + 1, :] + pad[MARGIN : MARGIN + length, :] * taps_ref[taps - 1 : taps, :]
    for by in range(1, taps):
        conv = conv + shifted(pad, length, by, flip) * taps_ref[taps - 1 - by : taps - by, :]
    sig = jax.nn.sigmoid(conv)
    dg = dg_ref[...]
    u_grad = us_ref[...] + contract_cols(dg, xproj_ref[...])
    conv_grad = u_grad * mask_ref[...] * (sig * (1.0 + conv * (1.0 - sig)))
    cols = dg.shape[1]
    packed_ref[0:cols, :] = matmul(jnp.transpose(dg.astype(f32)).astype(bf16), u_ref[...])
    for by in range(taps):
        moved = pad[MARGIN : MARGIN + length, :] if by == 0 else shifted(pad, length, by, flip)
        row = cols + taps - 1 - by
        packed_ref[row : row + 1, :] = jnp.sum(conv_grad * moved, axis=0, keepdims=True)
    packed_ref[cols + taps : cols + taps + 1, :] = jnp.sum(conv_grad, axis=0, keepdims=True)
    rest = packed_ref.shape[0] - cols - taps - 1
    packed_ref[cols + taps + 1 :, :] = jnp.zeros((rest, width), f32)
    pad[MARGIN : MARGIN + length, :] = conv_grad
    grad = conv_grad * taps_ref[taps - 1 : taps, :]
    for by in range(1, taps):
        grad = grad + shifted(pad, length, by, 1 - flip) * taps_ref[taps - 1 - by : taps - by, :]
    xg_ref[...] = grad.astype(bf16)


def conv_call(flip, own, other, mask, taps, xproj, width):
    length, channels = own.shape
    cols = xproj.shape[1]
    return pl.pallas_call(
        conv_kernel,
        grid=(channels // width,),
        in_specs=[
            pl.BlockSpec(memory_space=pltpu.SMEM),
            pl.BlockSpec((length, width), lambda j: (0, j)),
            pl.BlockSpec((length, width), lambda j: (0, j)),
            pl.BlockSpec((length, 1), lambda j: (0, 0)),
            pl.BlockSpec((taps.shape[0], width), lambda j: (0, j)),
            pl.BlockSpec((width, cols), lambda j: (j, 0)),
        ],
        out_specs=[
            pl.BlockSpec((length, width), lambda j: (0, j)),
            pl.BlockSpec((length, width), lambda j: (0, j)),
            pl.BlockSpec((length, width), lambda j: (0, j)),
            pl.BlockSpec((length, cols), lambda j: (0, 0)),
        ],
        out_shape=[
            jax.ShapeDtypeStruct((length, channels), bf16),
            jax.ShapeDtypeStruct((length, channels), bf16),
            jax.ShapeDtypeStruct((length, channels), bf16),
            jax.ShapeDtypeStruct((length, cols), f32),
        ],
        scratch_shapes=[pltpu.VMEM((length + 2 * MARGIN, width), f32)],
        compiler_params=pltpu.CompilerParams(vmem_limit_bytes=12 * 1024 * 1024),
        cost_estimate=pl.CostEstimate(flops=1000, bytes_accessed=1000, transcendentals=0),
        name="conv_forward",
    )(flip, own, other, mask, taps, xproj)


def conv_back_call(flip, x, u, mask, taps, xproj, us, dg, width):
    length, channels = x.shape
    cols = xproj.shape[1]
    rows = -(-(cols + taps.shape[0]) // 8) * 8
    return pl.pallas_call(
        conv_back_kernel,
        grid=(channels // width,),
        in_specs=[
            pl.BlockSpec(memory_space=pltpu.SMEM),
            pl.BlockSpec((length, width), lambda j: (0, j)),
            pl.BlockSpec((length, width), lambda j: (0, j)),
            pl.BlockSpec((length, 1), lambda j: (0, 0)),
            pl.BlockSpec((taps.shape[0], width), lambda j: (0, j)),
            pl.BlockSpec((width, cols), lambda j: (j, 0)),
            pl.BlockSpec((length, width), lambda j: (0, j)),
            pl.BlockSpec((length, cols), lambda j: (0, 0)),
        ],
        out_specs=[
            pl.BlockSpec((length, width), lambda j: (0, j)),
            pl.BlockSpec((rows, width), lambda j: (0, j)),
        ],
        out_shape=[
            jax.ShapeDtypeStruct((length, channels), bf16),
            jax.ShapeDtypeStruct((rows, channels), f32),
        ],
        scratch_shapes=[pltpu.VMEM((length + 2 * MARGIN, width), f32)],
        compiler_params=pltpu.CompilerParams(vmem_limit_bytes=14 * 1024 * 1024),
        cost_estimate=pl.CostEstimate(flops=1000, bytes_accessed=1000, transcendentals=0),
        name="conv_backward",
    )(flip, x, u, mask, taps, xproj, us, dg)


def spread(dbl_ref, first, b_wide, c_wide, rows_s, states):
    length, cols = dbl_ref.shape
    rest = dbl_ref[...]
    row = lax.broadcasted_iota(jnp.int32, (cols, cols), 0)
    col = lax.broadcasted_iota(jnp.int32, (cols, cols), 1)
    rows = jnp.zeros((length, cols), f32)
    for part in range(3):
        piece = rest.astype(bf16)
        rest = rest - piece.astype(f32)
        pick = ((row == first + col % (2*states)) & (col // (2*states) == part))
        rows = rows + matmul(piece, jnp.where(pick, 1.0, 0.0).astype(bf16))
    rows_s[...] = rows
    which = lax.broadcasted_iota(jnp.int32, (states, cols), 0)
    lane = lax.broadcasted_iota(jnp.int32, (states, cols), 1)
    mine = jnp.where(lane % states == which, 1.0, 0.0)
    row = lax.broadcasted_iota(jnp.int32, (cols, 2*cols), 0)
    col = lax.broadcasted_iota(jnp.int32, (cols, 2*cols), 1)
    wide = jnp.where((row % (2*states)) // states == col // cols, 1.0, 0.0).astype(bf16)
    def some(at, _):
        left = [(mine*jnp.broadcast_to(rows_s[pl.ds(at*CHUNK+t, 1), :], (states, cols))).astype(bf16) for t in range(CHUNK)]
        got = matmul(jnp.concatenate(left, 0), wide)
        here = pl.ds(pl.multiple_of(at*CHUNK*states, CHUNK*states), CHUNK*states)
        b_wide[here, :] = got[:, :cols]
        c_wide[here, :] = got[:, cols:]
        return 0
    lax.fori_loop(0, length//CHUNK, some, 0, unroll=4)

def tiles_of(values):
    return [values[:, at:at+128] for at in range(0, values.shape[1], 128)]

def fold(values, tmp, tt, states):
    for at, tile in enumerate(tiles_of(values)):
        total = tile[:8]
        for part in range(1, states//8):
            total = total + tile[part*8:(part+1)*8]
        tmp[at, pl.ds(tt//8*64 + tt%8, 8, stride=8), :] = total

def add_tiles(values):
    parts = tiles_of(values)
    total = parts[0]
    for part in parts[1:]:
        total = total + part
    return total

def unfold(tmp, out, base):
    for at in range(out.shape[1]//128):
        for part in range(CHUNK//8):
            acc = tmp[at, part*64:part*64+8, :]
            for row in range(1, 8):
                acc = acc + tmp[at, part*64+row*8:part*64+row*8+8, :]
            out[pl.ds(pl.multiple_of(base+part*8, 8), 8), at*128:(at+1)*128] = acc

def collect(acc, tmp, out, length, states):
    which = lax.broadcasted_iota(jnp.int32, (states, 128), 0)
    lane = lax.broadcasted_iota(jnp.int32, (states, 128), 1)
    mine = which == lane
    def some(at, _):
        base = pl.multiple_of(at*CHUNK, CHUNK)
        for tt in range(CHUNK):
            sums = jnp.sum(acc[pl.ds((base+tt)*states, states), :], axis=1, keepdims=True)
            fold(jnp.where(mine, sums, 0.0), tmp, tt, states)
        unfold(tmp, out, base)
        return 0
    lax.fori_loop(0, length//CHUNK, some, 0, unroll=4)

def fwd_kernel(states, flip_ref, dbl_ref, dtp_ref, vec_ref, rate2_ref, u_ref, z_ref, gg_ref,
               gated_ref, zg_ref, delta_ref, yg_ref, prior_ref, cout_ref,
               b_wide, c_wide, drive_s, y_s, y_tmp, c_acc, rows_s):
    step = pl.program_id(0)
    length, width = u_ref.shape
    rank = dtp_ref.shape[0]
    group = CHUNK*states
    chunks = length//CHUNK
    flip = flip_ref[0]
    @pl.when(step == 0)
    def _():
        spread(dbl_ref, rank, b_wide, c_wide, rows_s, states)
        c_acc[...] = jnp.zeros_like(c_acc)
    low = dbl_ref[:, :rank].astype(bf16)
    pre = matmul(low, dtp_ref[...]) + vec_ref[0:1, :]
    delta = jnp.maximum(pre, 0.0) + jnp.log1p(jnp.exp(-jnp.abs(pre)))
    delta_ref[...] = delta
    drive_s[...] = delta * u_ref[...].astype(f32)
    z = z_ref[...].astype(f32)
    yg_ref[...] = gg_ref[...].astype(f32) * (z * (0.5 + 0.5*jnp.tanh(0.5*z)))
    def run(flipped):
        def ahead(chunk, state):
            place = chunks-1-chunk if flipped else chunk
            base = pl.multiple_of(place*CHUNK, CHUNK)
            wide = pl.multiple_of(place*group, group)
            for at in range(CHUNK):
                tt = CHUNK-1-at if flipped else at
                t = base + tt
                here = pl.ds(wide + tt*states, states)
                d = jnp.broadcast_to(delta_ref[pl.ds(t,1),:], (states,width))
                x = jnp.broadcast_to(drive_s[pl.ds(t,1),:], (states,width))
                g = jnp.broadcast_to(yg_ref[pl.ds(t,1),:], (states,width))
                b = jnp.concatenate([b_wide[here,:]]*(width//128), axis=1)
                c = jnp.concatenate([c_wide[here,:]]*(width//128), axis=1)
                prior = jnp.exp2(d*rate2_ref[...])*state
                state = prior + x*b
                prior_ref[here,:] = prior.astype(bf16)
                fold(state*c, y_tmp, tt, states)
                c_acc[here,:] += add_tiles(state*g)
            unfold(y_tmp, y_s, base)
            return state
        lax.fori_loop(0, chunks, ahead, jnp.zeros((states,width), f32))
    pl.when(flip == 0)(lambda: run(False))
    pl.when(flip == 1)(lambda: run(True))
    u = u_ref[...].astype(f32)
    z = z_ref[...].astype(f32)
    sig = (0.5 + 0.5*jnp.tanh(0.5*z))
    y = y_s[...] + vec_ref[1:2,:]*u
    gated_ref[...] = (y*(z*sig)).astype(bf16)
    zg_ref[...] = (gg_ref[...].astype(f32)*y*(sig*(1.0+z*(1.0-sig)))).astype(bf16)
    @pl.when(step == pl.num_programs(0)-1)
    def _():
        collect(c_acc, y_tmp, rows_s, length, states)
        cout_ref[...] = rows_s[:, :states]

def bwd_kernel(states, flip_ref, dbl_ref, dtp_ref, vec_ref, rate2_ref, u_ref, delta_ref, yg_ref, prior_ref, cout_ref,
               us_ref, part_ref, packed_ref,
               b_wide, c_wide, drive_s, r_s, w_s, low_t, rank_s, r_tmp, w_tmp, b_acc, rows_s):
    step = pl.program_id(0)
    length, width = u_ref.shape
    rank = dtp_ref.shape[0]
    group = CHUNK*states
    chunks = length//CHUNK
    flip = flip_ref[0]
    @pl.when(step == 0)
    def _():
        low_t[...] = jnp.transpose(dbl_ref[...])[:rank,:].astype(bf16)
        spread(dbl_ref, rank, b_wide, c_wide, rows_s, states)
        b_acc[...] = jnp.zeros_like(b_acc)
        rank_s[...] = jnp.zeros_like(rank_s)
    u = u_ref[...].astype(f32)
    drive_s[...] = delta_ref[...]*u
    def run(flipped):
        def back(chunk, carry):
            carried, total = carry
            place = chunk if flipped else chunks-1-chunk
            base = pl.multiple_of(place*CHUNK, CHUNK)
            wide = pl.multiple_of(place*group, group)
            for at in range(CHUNK):
                tt = at if flipped else CHUNK-1-at
                t = base + tt
                here = pl.ds(wide + tt*states, states)
                d = jnp.broadcast_to(delta_ref[pl.ds(t,1),:], (states,width))
                x = jnp.broadcast_to(yg_ref[pl.ds(t,1),:], (states,width))
                e = jnp.broadcast_to(drive_s[pl.ds(t,1),:], (states,width))
                b = jnp.concatenate([b_wide[here,:]]*(width//128), axis=1)
                c = jnp.concatenate([c_wide[here,:]]*(width//128), axis=1)
                power = d*rate2_ref[...]
                adj = carried + x*c
                moved = (adj*prior_ref[here,:].astype(f32))*power
                total = total + moved
                fold(moved, w_tmp, tt, states)
                fold(adj*b, r_tmp, tt, states)
                b_acc[here,:] += add_tiles(adj*e)
                carried = jnp.exp2(power)*adj
            unfold(w_tmp, w_s, base)
            unfold(r_tmp, r_s, base)
            return carried, total
        zero = jnp.zeros((states,width), f32)
        _, total = lax.fori_loop(0, chunks, back, (zero, zero))
        packed_ref[rank:rank+states,:] = total*(1.0/LOG2E)
    pl.when(flip == 0)(lambda: run(False))
    pl.when(flip == 1)(lambda: run(True))
    yg = yg_ref[...]
    r = r_s[...]
    delta = delta_ref[...]
    us_ref[...] = delta*r + vec_ref[1:2,:]*yg
    low = dbl_ref[:, :rank].astype(bf16)
    pre = matmul(low, dtp_ref[...]) + vec_ref[0:1,:]
    sig = jnp.exp(pre-delta)
    ratio = jnp.where(delta > 1e-30, sig/jnp.maximum(delta, 1e-30), 1.0)
    pre_grad = w_s[...]*(1.0/LOG2E)*ratio + u*r*sig
    pre_low = pre_grad.astype(bf16)
    rank_s[...] += contract_cols(pre_low, dtp_ref[...])
    packed_ref[0:rank,:] = matmul(low_t[...], pre_low)
    packed_ref[rank+states:rank+states+1,:] = jnp.sum(pre_grad, axis=0, keepdims=True)
    packed_ref[rank+states+1:rank+states+2,:] = jnp.sum(yg*u, axis=0, keepdims=True)
    rest = packed_ref.shape[0]-rank-states-2
    packed_ref[rank+states+2:,:] = jnp.zeros((rest,width), f32)
    @pl.when(step == pl.num_programs(0)-1)
    def _():
        collect(b_acc, r_tmp, rows_s, length, states)
        part_ref[...] = jnp.concatenate([rank_s[...], rows_s[:, :states], cout_ref[...]], axis=1)


def scan_specs(length, channels, states, rank, cols, width):
    whole = lambda *shape: pl.BlockSpec(shape, lambda j: (0,) * len(shape))
    block = lambda count: pl.BlockSpec((count, width), lambda j: (0, j))
    out = lambda rows, kind: jax.ShapeDtypeStruct((rows, channels), kind)
    return whole, block, out


def forward_call(flip, dbl, dtproj, vec, rates2, u, z, gg, width):
    length, channels = u.shape
    states, rank, cols = rates2.shape[0], dtproj.shape[0], dbl.shape[1]
    whole, block, out = scan_specs(length, channels, states, rank, cols, width)
    return pl.pallas_call(
        functools.partial(fwd_kernel, states),
        grid=(channels // width,),
        in_specs=[
            pl.BlockSpec(memory_space=pltpu.SMEM),
            whole(length, cols),
            block(rank),
            block(2),
            block(states),
            block(length),
            block(length),
            block(length),
        ],
        out_specs=[block(length)] * 4 + [block(length * states), whole(length, states)],
        out_shape=[
            out(length, bf16),
            out(length, bf16),
            out(length, f32),
            out(length, f32),
            out(length * states, bf16),
            jax.ShapeDtypeStruct((length, states), f32),
        ],
        scratch_shapes=[
            pltpu.VMEM((length * states, 128), f32),
            pltpu.VMEM((length * states, 128), f32),
            pltpu.VMEM((length, width), f32),
            pltpu.VMEM((length, width), f32),
            pltpu.VMEM((width // 128, CHUNK * 8, 128), f32),
            pltpu.VMEM((length * states, 128), f32),
            pltpu.VMEM((length, cols), f32),
        ],
        compiler_params=pltpu.CompilerParams(vmem_limit_bytes=40 * 1024 * 1024),
        cost_estimate=pl.CostEstimate(
            flops=16000000000, bytes_accessed=20000000, transcendentals=7000000
        ),
        name="scan_forward",
    )(flip, dbl, dtproj, vec, rates2, u, z, gg)


def backward_call(flip, dbl, dtproj, vec, rates2, u, delta, yg, prior, cout, width):
    length, channels = u.shape
    states, rank, cols = rates2.shape[0], dtproj.shape[0], dbl.shape[1]
    rows = -(-(rank + states + 2) // 8) * 8
    whole, block, out = scan_specs(length, channels, states, rank, cols, width)
    return pl.pallas_call(
        functools.partial(bwd_kernel, states),
        grid=(channels // width,),
        in_specs=[
            pl.BlockSpec(memory_space=pltpu.SMEM),
            whole(length, cols),
            block(rank),
            block(2),
            block(states),
            block(length),
            block(length),
            block(length),
            block(length * states),
            whole(length, states),
        ],
        out_specs=[block(length), whole(length, cols), block(rows)],
        out_shape=[
            out(length, f32),
            jax.ShapeDtypeStruct((length, cols), f32),
            out(rows, f32),
        ],
        scratch_shapes=[
            pltpu.VMEM((length * states, 128), f32),
            pltpu.VMEM((length * states, 128), f32),
            pltpu.VMEM((length, width), f32),
            pltpu.VMEM((length, width), f32),
            pltpu.VMEM((length, width), f32),
            pltpu.VMEM((rank, length), bf16),
            pltpu.VMEM((length, rank), f32),
            pltpu.VMEM((width // 128, CHUNK * 8, 128), f32),
            pltpu.VMEM((width // 128, CHUNK * 8, 128), f32),
            pltpu.VMEM((length * states, 128), f32),
            pltpu.VMEM((length, cols), f32),
        ],
        compiler_params=pltpu.CompilerParams(vmem_limit_bytes=40 * 1024 * 1024),
        cost_estimate=pl.CostEstimate(
            flops=22000000000, bytes_accessed=20000000, transcendentals=7000000
        ),
        name="scan_backward",
    )(flip, dbl, dtproj, vec, rates2, u, delta, yg, prior, cout)


def local(
    tokens,
    cond,
    counts,
    valid,
    ada_weight,
    ada_bias,
    in_weight,
    conv_weight,
    conv_bias,
    xproj_weight,
    dtproj_weight,
    dt_bias,
    a_log,
    skip_gain,
    out_weight,
    cotangent,
):
    slot_count, shard_rows, model = tokens.shape
    dirs = lax.axis_size("dir")
    dps = lax.axis_size("dp")
    length = valid.shape[1]
    me = lax.axis_index("dir")
    dp_index = lax.axis_index("dp")
    core = me & 1
    chip = me >> 1
    half = in_weight.shape[1] // 2
    rank = dtproj_weight.shape[0]
    states = a_log.shape[1]
    flip = core.astype(jnp.int32).reshape(1)
    slots = range(slot_count)

    live_slots = (jnp.arange(slot_count) < counts[0]).astype(f32)
    full_mask = valid.astype(f32) * live_slots[:, None]
    mask_cols = full_mask[:, :, None]
    me_ref = me.astype(jnp.int32).reshape(1)
    first, second = bit_orders("dp")

    def gather_rows(block):
        over = swap(block, "dir", 1)
        return block, over, swap(block, "dir", 0), swap(over, "dir", 0)

    token_blocks = gather_rows(tokens)
    cond_act = jax.nn.silu(cond.astype(f32)).astype(bf16)
    modulation = matmul(cond_act, ada_weight) + ada_bias.astype(f32)[None, :]
    cot_blocks = gather_rows(after(cotangent, token_blocks[0]))
    in_keep, in_send = halves(after(in_weight, modulation), core, 1)
    in_there = swap(in_send, "dir", 0)
    out_there = swap(out_weight, "dir", 0)

    taps = jnp.concatenate(
        [jnp.transpose(conv_weight.astype(f32)), conv_bias.astype(f32)[None, :]], 0
    )
    vec = jnp.stack([dt_bias, skip_gain])
    rates2 = -jnp.exp(jnp.transpose(a_log)) * LOG2E
    width = 512 if dt_bias.shape[0] % 512 == 0 else 128

    def sum_halves(values):
        keep, send = halves(values, core, 1)
        return (keep.astype(f32) + swap(send, "dir", 0).astype(f32)).astype(bf16)

    mods = [modulation[slot].reshape(3, model) for slot in slots]
    normed, x, z, u, part, part_there, branch_grad, gg = ([None] * slot_count for _ in range(8))
    owns = []
    for slot in slots:
        normed[slot], own = norm_call(
            me_ref, token_blocks, slot, mask_cols[slot], mods[slot][:2], in_weight, width
        )
        owns.append((own, swap(own, "dir", 0)))
    for slot in slots:
        own, other = owns[slot]
        x[slot], z[slot], u[slot], part[slot] = conv_call(
            flip, own, other, mask_cols[slot], taps, xproj_weight, half
        )
        part_there[slot] = swap(part[slot], "dir", 1)

    pair_bit = second[0]
    rest_bits = [bit for bit in first if bit != pair_bit]
    mine = (dp_index >> pair_bit) & 1
    normed_all = jnp.concatenate(normed, 0)
    left = after(normed_all, u[-1])
    chunk = model // dps << pair_bit

    def columns_of(bit_value):
        return jnp.concatenate(
            [
                lax.dynamic_slice_in_dim(left, start + bit_value * chunk, chunk, 1)
                for start in range(0, model, 2 * chunk)
            ],
            1,
        )

    left_sent = columns_of(1 - mine)
    left_mine = columns_of(mine)
    left_there = swap(left_sent, "dp", pair_bit)

    out_bit = first[0]
    out_side = (dp_index >> out_bit) & 1
    side_ref = out_side.astype(jnp.int32).reshape(1)
    branch_keep, branch_there, gate_sums, z_sums, gate_there, z_there = ([] for _ in range(6))
    scanned, dbl = [], []
    tie = (left_sent,)
    for slot in slots:
        keep, give, gg[slot] = gate_call(
            me_ref,
            side_ref,
            cot_blocks,
            slot,
            mask_cols[slot],
            after(mods[slot][2:], *tie),
            out_weight,
            out_there,
            model // dps << out_bit,
        )
        branch_keep.append(keep)
        branch_there.append(swap(give, "dp", out_bit))
        dbl.append(part[slot] + after(part_there[slot], gg[slot]))
        scanned.append(
            forward_call(
                flip, dbl[slot], dtproj_weight, vec, rates2, u[slot], z[slot], gg[slot], width
            )
        )
        gated, zg = scanned[slot][:2]
        if slot + 1 == slot_count:
            gated, zg = after((gated, zg), left_there, *branch_there[:-1], *gate_there, *z_there)
        gate_sums.append(sum_halves(gated))
        z_sums.append(sum_halves(zg))
        gate_there.append(swap(gate_sums[-1], "dp", out_bit))
        z_there.append(swap(z_sums[-1], "dp", pair_bit))
        tie = (scanned[slot][5], gate_sums[slot], z_sums[slot])
    z_all, gate_all = jnp.concatenate(z_sums, 0), jnp.concatenate(gate_sums, 0)

    backs, part_back, dgs = [], [], []
    u_tied = after(u[0], z_all, gate_all)
    for slot in slots:
        backs.append(
            backward_call(
                flip, dbl[slot], dtproj_weight, vec, rates2, u_tied, *scanned[slot][2:], width
            )
        )
        part_back.append(swap(backs[-1][1], "dir", 1))
        if slot == 0:
            first_end = backs[0][1]
            z_part = Scatter(
                contract_rows(left_mine, after(z_all, first_end))
                + contract_rows(left_there, after(jnp.concatenate(z_there, 0), first_end)),
                "dp",
                rest_bits,
            )
            out_part = Scatter(
                contract_rows(jnp.concatenate(branch_keep, 0), after(gate_all, first_end))
                + contract_rows(
                    jnp.concatenate(branch_there, 0),
                    after(jnp.concatenate(gate_there, 0), first_end),
                ),
                "dp",
                [bit for bit in first if bit != out_bit],
            )
            rows_keep, rows_give = branch_call(
                flip, after(gate_all, z_part.send, out_part.send), out_weight, shard_rows, width
            )
            rows_there = swap(rows_give, "dir", 0)
            dgs.append((backs[0][1] + after(part_back[0], rows_give)).astype(bf16))
            u_tied, z_part.send, out_part.send = after(
                (u[1], z_part.send, out_part.send), dgs[0]
            )
        else:
            dgs.append(None)
    z_part.step(backs[-1][1])
    out_part.step(backs[-1][1])

    end = backs[-1][1]
    x_grads, conv_packs = [], []
    for slot in slots:
        dg = dgs[slot]
        if dg is None:
            dg = (backs[slot][1] + after(part_back[slot], x_grads[0])).astype(bf16)
        else:
            dg = after(dg, z_part.send, out_part.send)
        xg, conv_pack = conv_back_call(
            flip, x[slot], u[slot], mask_cols[slot], taps, xproj_weight, backs[slot][0], dg, half
        )
        conv_packs.append(conv_pack)
        x_grads.append(xg)
    pairs = [halves(xg, core, 1) for xg in x_grads]
    pairs = [(keep, swap(send, "dir", 0)) for keep, send in pairs]
    x_all = jnp.concatenate(
        [(keep.astype(f32) + there.astype(f32)).astype(bf16) for keep, there in pairs], 0
    )
    x_there = swap(x_all, "dp", pair_bit)

    pack = jnp.concatenate([sum(conv_packs), sum(backs[slot][2] for slot in slots)], 0)
    shared = SharedSum(after(pack, x_all), "dp", first)
    norm_keep, norm_give = proj_back_call(
        flip, after(x_all, shared.send), z_all, in_keep, in_there, shard_rows, width
    )
    norm_there = swap(norm_give, "dir", 0)

    def fold_chip(keep, there):
        keep = keep.reshape(slot_count, dirs // 2, shard_rows, model)
        there = there.reshape(slot_count, dirs // 2, shard_rows, model)

        def of(which):
            return lax.dynamic_index_in_dim(keep, which, 1, keepdims=False) + lax.dynamic_index_in_dim(
                there, which, 1, keepdims=False
            )

        return of(chip), of(1 - chip).astype(bf16)

    rows_mine, branch_sent = fold_chip(rows_keep, after(rows_there, norm_give))
    branch_far = swap(branch_sent, "dir", 1)
    norm_mine, norm_sent = fold_chip(norm_keep, after(norm_there, branch_sent))
    norm_far = swap(norm_sent, "dir", 1)
    shared.step(norm_sent)

    x_part = contract_rows(left_mine, after(x_all, shared.send)) + contract_rows(
        left_there, after(x_there, shared.send)
    )
    x_part = Scatter(x_part, "dp", rest_bits)

    raw = after(tokens, x_part.send).astype(f32)
    local_mask = lax.dynamic_slice_in_dim(full_mask, me * shard_rows, shard_rows, 1)[:, :, None]
    scale = modulation[:, None, model : 2 * model]
    gate = modulation[:, None, 2 * model :]
    branch = rows_mine + after(branch_far, x_part.send).astype(f32)
    mixed = local_mask * (raw + gate * branch)
    res_grad = local_mask * cotangent.astype(f32)
    gate_grad = jnp.sum(res_grad * branch, axis=1)
    centred = raw - jnp.mean(raw, axis=2, keepdims=True)
    spread = jnp.mean(centred * centred, axis=2, keepdims=True)
    inverse = lax.rsqrt(spread + EPSILON)
    hat = centred * inverse
    normed_grad = local_mask * (norm_mine + after(norm_far, x_part.send).astype(f32))
    shift_grad = jnp.sum(normed_grad, axis=1)
    scale_grad = jnp.sum(normed_grad * hat, axis=1)
    q = normed_grad * (1.0 + scale)
    token_grads = res_grad + inverse * (
        q - jnp.mean(q, axis=2, keepdims=True) - hat * jnp.mean(q * hat, axis=2, keepdims=True)
    )
    mod_part = jnp.concatenate([shift_grad, scale_grad, gate_grad], 1)
    mod_pair = mod_part + swap(mod_part, "dir", 0)
    mod_far = swap(mod_pair, "dir", 1)
    shared.step(mod_pair)
    out_part.step(shared.send)
    z_part.step(shared.send)
    mod_total = mod_pair + after(mod_far, out_part.values, z_part.values)
    mod_low = mod_total.astype(bf16)
    have = []
    sides = jnp.concatenate([mod_low, after(cond_act, end)], 1)
    x_part.step(sides)
    sides = gather_bit(after(sides, x_part.send), "dp", first[0], have)
    shared.step(sides)
    for bit in first[1:-1]:
        sides = gather_bit(after(sides, shared.send), "dp", bit, have)
    cond_value = cond.astype(f32)
    sig = jax.nn.sigmoid(cond_value)
    cond_grad = (
        contract_cols(after(mod_low, sides), ada_weight)
        * sig
        * (1.0 + cond_value * (1.0 - sig))
    )
    while len(shared.plan) > 1:
        shared.step(cond_grad)
    sides = gather_bit(sides, "dp", first[-1], have)
    sides = sides.reshape(dps * slot_count, -1)
    columns = ada_weight.shape[1] // dirs
    rows = ada_weight.shape[0] // dps
    total_columns = ada_weight.shape[1]
    mod_all = lax.dynamic_slice_in_dim(sides, me * columns, columns, 1)
    act_mine = lax.dynamic_slice_in_dim(sides, total_columns + dp_index * rows, rows, 1)
    ada_sum = contract_rows(act_mine, mod_all)
    portion = total_columns // dps
    bias_part = lax.dynamic_slice_in_dim(sides, dp_index * portion, portion, 1)
    bias_sum = jnp.sum(bias_part.astype(f32), axis=0)

    cols = xproj_weight.shape[1]
    tap_count = conv_weight.shape[1]
    shared.step(sides)
    pack = shared.values.astype(f32)
    base = conv_packs[0].shape[0]
    conv_rows, scan_rows = pack[:base], pack[base:]
    xproj_sum = jnp.transpose(conv_rows[:cols])
    kernel_sum = jnp.transpose(conv_rows[cols : cols + tap_count])
    offset_sum = conv_rows[cols + tap_count]
    dtproj_sum = scan_rows[:rank]
    rate_sum = jnp.transpose(scan_rows[rank : rank + states])
    step_bias_sum = scan_rows[rank + states]
    skip_sum = scan_rows[rank + states + 1]

    while x_part.order:
        x_part.step(sides)
    while z_part.order:
        z_part.step(sides)
    while out_part.order:
        out_part.step(sides)
    x_sum = x_part.values
    z_sum = z_part.values
    out_sum = jnp.transpose(out_part.values)
    keep_sum = jnp.where(core == 0, x_sum, z_sum)
    send_sum = jnp.where(core == 0, z_sum, x_sum)
    in_sum = ordered(core, keep_sum, swap(send_sum, "dir", 0), 1)

    return (
        mixed,
        token_grads,
        cond_grad,
        ada_sum,
        bias_sum,
        in_sum,
        kernel_sum,
        offset_sum,
        xproj_sum,
        dtproj_sum,
        step_bias_sum,
        rate_sum,
        skip_sum,
        out_sum,
    )


def solution(mesh):
    in_specs = (
        P("dp", "dir", None),
        P("dp", None),
        P("dp"),
        P("dp", None),
        P(),
        P(),
        P(None, "dir"),
        P("dir", None),
        P("dir"),
        P("dir", None),
        P(None, "dir"),
        P("dir"),
        P("dir", None),
        P("dir"),
        P("dir", None),
        P("dp", "dir", None),
    )
    out_specs = (
        P("dp", "dir", None),
        P("dp", "dir", None),
        P("dp", None),
        P("dp", "dir"),
        P("dp"),
        P("dp", "dir"),
        P("dir", None),
        P("dir"),
        P("dir", None),
        P(None, "dir"),
        P("dir"),
        P("dir", None),
        P("dir"),
        P("dir", "dp"),
    )
    return jax.shard_map(local, mesh=mesh, in_specs=in_specs, out_specs=out_specs, check_vma=False)
```

```python
import functools

import jax
import jax.numpy as jnp
from jax import lax
from jax.experimental import pallas as pl
from jax.experimental.pallas import tpu as pltpu
from jax.sharding import PartitionSpec as P

EPSILON = 1e-06
LOG2E = 1.4426950408889634
CHUNK = 16
MARGIN = 8

bf16 = jnp.bfloat16
f32 = jnp.float32


def swap(block, axis, bit):
    count = lax.axis_size(axis)
    return lax.ppermute(block, axis, [(at, at ^ (1 << bit)) for at in range(count)])


def contract_rows(left, right):
    return lax.dot_general(
        left, right, (((0,), (0,)), ((), ())), preferred_element_type=f32
    )


def contract_cols(left, right):
    return lax.dot_general(
        left, right, (((1,), (1,)), ((), ())), preferred_element_type=f32
    )


def matmul(left, right):
    return jnp.dot(left, right, preferred_element_type=f32)


def ordered(bit, own, other, axis):
    return jnp.where(
        bit == 0,
        jnp.concatenate([own, other], axis),
        jnp.concatenate([other, own], axis),
    )


def halves(values, bit, axis):
    size = values.shape[axis] // 2
    keep = lax.dynamic_slice_in_dim(values, bit * size, size, axis)
    send = lax.dynamic_slice_in_dim(values, (1 - bit) * size, size, axis)
    return keep, send


class Scatter:
    def __init__(self, values, axis, order):
        self.axis, self.order = axis, list(order)
        bits = len(order)
        self.values = values.reshape((2,) * bits + (values.shape[0] >> bits,) + values.shape[1:])
        self.left = sorted(order, reverse=True)
        self.split()

    def split(self):
        if not self.order:
            return
        at = self.left.index(self.order[0])
        mine = (lax.axis_index(self.axis) >> self.order[0]) & 1
        self.keep = lax.dynamic_index_in_dim(self.values, mine, at, keepdims=False)
        send = lax.dynamic_index_in_dim(self.values, 1 - mine, at, keepdims=False)
        self.send = send.astype(bf16)

    def step(self, *earlier):
        bit = self.order.pop(0)
        self.left.remove(bit)
        arrived = after(swap(self.send, self.axis, bit), *earlier)
        self.values = self.keep.astype(f32) + arrived.astype(f32)
        self.split()


class SharedSum:
    def __init__(self, values, axis, order):
        self.axis = axis
        few = list(order[:2])
        self.plan = [("halve", bit) for bit in few] + [("add", bit) for bit in order[2:]]
        self.plan += [("join", bit) for bit in few[::-1]]
        self.start(*values)

    def start(self, keep, send):
        self.keep, self.send = keep, send

    def begin(self):
        kind, bit = self.plan[0] if self.plan else ("", 0)
        self.mine = (lax.axis_index(self.axis) >> bit) & 1
        if kind == "halve":
            self.keep, self.send = halves(self.values, self.mine, 0)
            self.send = self.send.astype(bf16)
        else:
            self.keep = self.send = self.values.astype(bf16)

    def step(self, *earlier):
        kind, bit = self.plan.pop(0)
        arrived = after(swap(self.send, self.axis, bit), *earlier)
        if kind == "join":
            self.values = ordered(self.mine, self.keep, arrived, 0)
        else:
            self.values = self.keep.astype(f32) + arrived.astype(f32)
        self.begin()

    def last(self, *earlier):
        _, bit = self.plan.pop(0)
        return self.keep, after(swap(self.send, self.axis, bit), *earlier)


def after(values, *earlier):
    return lax.optimization_barrier((values, earlier))[0] if earlier else values


def gather_bit(values, axis, bit, have, *earlier):
    at = len([other for other in have if other > bit])
    mine = (lax.axis_index(axis) >> bit) & 1
    arrived = after(swap(values, axis, bit), *earlier)
    have.append(bit)
    return jnp.where(
        mine == 0, jnp.stack([values, arrived], at), jnp.stack([arrived, values], at)
    )


def bit_orders(axis):
    bits = lax.axis_size(axis).bit_length() - 1
    first = list(range(bits))
    second = list(range(bits))
    if bits > 1:
        second[0], second[1] = 1, 0
    return first, second


def shifted(padded, length, by, flip):
    return jnp.where(
        flip == 1,
        padded[MARGIN + by : MARGIN + by + length, :],
        padded[MARGIN - by : MARGIN - by + length, :],
    )


def kernel_params(megabytes):
    return pltpu.CompilerParams(vmem_limit_bytes=megabytes * 1024 * 1024)


LIGHT = pl.CostEstimate(flops=1000, bytes_accessed=1000, transcendentals=0)


def whole(*shape):
    return pl.BlockSpec(shape, lambda *at: (0,) * len(shape))


def scalars():
    return pl.BlockSpec(memory_space=pltpu.SMEM)


def shaped(shape, kind):
    return jax.ShapeDtypeStruct(shape, kind)


def outer(shape, kind):
    return pltpu.HBM(shape, kind)


def held(values):
    return pltpu.with_memory_space_constraint(values, pltpu.HBM)


def split_columns(values_ref, side_ref, chunk, keep_ref, give_ref):
    for side in range(2):

        @pl.when(side_ref[0] == side)
        def _():
            for at, start in enumerate(range(0, values_ref.shape[1], 2 * chunk)):
                to = slice(at * chunk, (at + 1) * chunk)
                first = values_ref[:, start : start + chunk]
                second = values_ref[:, start + chunk : start + 2 * chunk]
                keep_ref[:, to] = second if side else first
                give_ref[:, to] = first if side else second


def norm_kernel(
    chunk, me_ref, side_ref, own_ref, over_ref, beside_ref, far_ref, mask_ref, mod_ref, weight_ref,
    keep_ref, give_ref, proj_ref, normed_s
):
    slots, rows, _ = own_ref.shape
    length = mask_ref.shape[1]

    @pl.when(pl.program_id(0) == 0)
    def _():
        for slot in range(slots):
            shift = mod_ref[slot, 0:1, :]
            scale = mod_ref[slot, 1:2, :]
            for code, block in ((0, own_ref), (2, over_ref), (1, beside_ref), (3, far_ref)):
                start = pl.multiple_of((me_ref[0] ^ code) * rows, rows)
                raw = block[slot].astype(f32)
                centred = raw - jnp.mean(raw, axis=1, keepdims=True)
                spread = jnp.mean(centred * centred, axis=1, keepdims=True)
                hat = centred * lax.rsqrt(spread + EPSILON)
                mask = mask_ref[slot, pl.ds(start, rows), :]
                normed_s[pl.ds(slot * length + start, rows), :] = (
                    mask * (hat * (1.0 + scale) + shift)
                ).astype(bf16)
        split_columns(normed_s, side_ref, chunk, keep_ref, give_ref)

    proj_ref[...] = matmul(normed_s[...], weight_ref[...]).astype(bf16)


def norm_call(me, side, blocks, mask, mods, weight, width, chunk):
    slots, rows, model = blocks[0].shape
    count = slots * mask.shape[1]
    channels = weight.shape[1]
    return pl.pallas_call(
        functools.partial(norm_kernel, chunk),
        grid=(channels // width,),
        in_specs=[scalars(), scalars()]
        + [whole(slots, rows, model)] * 4
        + [whole(*mask.shape), whole(slots, 3, model), pl.BlockSpec((model, width), lambda j: (0, j))],
        out_specs=[
            whole(count, model // 2),
            whole(count, model // 2),
            pl.BlockSpec((count, width), lambda j: (0, j)),
        ],
        out_shape=[
            shaped((count, model // 2), bf16),
            shaped((count, model // 2), bf16),
            shaped((count, channels), bf16),
        ],
        scratch_shapes=[pltpu.VMEM((count, model), bf16)],
        compiler_params=kernel_params(20),
        cost_estimate=LIGHT,
        name="norm_project",
    )(me, side, *blocks, mask, mods, held(weight))


def gate_kernel(
    chunk, me_ref, side_ref, own_ref, over_ref, beside_ref, far_ref, mask_ref, mod_ref, mine_ref,
    theirs_ref, keep_ref, give_ref, out_ref, grad_s
):
    slots, rows, _ = own_ref.shape
    length = mask_ref.shape[1]
    step = pl.program_id(0)

    @pl.when(step == 0)
    def _():
        for slot in range(slots):
            gate = mod_ref[slot, 2:3, :]
            for code, block in ((0, own_ref), (2, over_ref), (1, beside_ref), (3, far_ref)):
                start = pl.multiple_of((me_ref[0] ^ code) * rows, rows)
                mask = mask_ref[slot, pl.ds(start, rows), :]
                grad_s[pl.ds(slot * length + start, rows), :] = (
                    mask * block[slot].astype(f32) * gate
                ).astype(bf16)
        split_columns(grad_s, side_ref, chunk, keep_ref, give_ref)

    @pl.when(step < pl.num_programs(0) // 2)
    def _():
        out_ref[...] = contract_cols(grad_s[...], mine_ref[...]).astype(bf16)

    @pl.when(step >= pl.num_programs(0) // 2)
    def _():
        out_ref[...] = contract_cols(grad_s[...], theirs_ref[...]).astype(bf16)


def gate_call(me, side, blocks, mask, mods, mine, theirs, chunk):
    slots, rows, model = blocks[0].shape
    count = slots * mask.shape[1]
    quarter = mine.shape[0]
    parts = 2
    width = quarter // parts

    def out_at(j, me_ref, side_ref):
        return (0, ((me_ref[0] & 1) ^ (j // parts)) * parts + j % parts)

    fixed = lambda *shape: pl.BlockSpec(shape, lambda j, *refs: (0,) * len(shape))
    return pl.pallas_call(
        functools.partial(gate_kernel, chunk),
        grid_spec=pltpu.PrefetchScalarGridSpec(
            num_scalar_prefetch=2,
            grid=(2 * parts,),
            in_specs=[fixed(slots, rows, model)] * 4
            + [
                fixed(*mask.shape),
                fixed(slots, 3, model),
                pl.BlockSpec((width, model), lambda j, *refs: (jnp.minimum(j, parts - 1), 0)),
                pl.BlockSpec((width, model), lambda j, *refs: (jnp.maximum(j - parts, 0), 0)),
            ],
            out_specs=[
                fixed(count, model // 2),
                fixed(count, model // 2),
                pl.BlockSpec((count, width), out_at),
            ],
            scratch_shapes=[pltpu.VMEM((count, model), bf16)],
        ),
        out_shape=[
            shaped((count, model // 2), bf16),
            shaped((count, model // 2), bf16),
            outer((count, 2 * quarter), bf16),
        ],
        compiler_params=kernel_params(20),
        cost_estimate=LIGHT,
        name="gate_project",
    )(me, side, *blocks, mask, mods, held(mine), held(theirs))


def pair_kernel(first_ref, second_ref, third_ref, fourth_ref, left_ref, right_ref):
    left_ref[...] = (first_ref[...].astype(f32) + second_ref[...].astype(f32)).astype(bf16)
    right_ref[...] = (third_ref[...].astype(f32) + fourth_ref[...].astype(f32)).astype(bf16)


def pair_call(first, second, third, fourth, blocks):
    rows, cols = first.shape
    block = pl.BlockSpec((rows // blocks, cols), lambda i: (i, 0))
    return pl.pallas_call(
        pair_kernel,
        grid=(blocks,),
        in_specs=[block] * 4,
        out_specs=[block] * 2,
        out_shape=[shaped((rows, cols), bf16)] * 2,
        compiler_params=kernel_params(10),
        cost_estimate=LIGHT,
        name="pair_sums",
    )(held(first), held(second), held(third), held(fourth))


def join_kernel(*refs):
    out_ref = refs[-1]
    rows = refs[0].shape[0]
    for at in range(len(refs) // 2):
        total = refs[2 * at][...].astype(f32) + refs[2 * at + 1][...].astype(f32)
        out_ref[at * rows : (at + 1) * rows, :] = total.astype(bf16)


def join_call(pairs):
    rows, cols = pairs[0][0].shape
    return pl.pallas_call(
        join_kernel,
        out_shape=shaped((len(pairs) * rows, cols), bf16),
        compiler_params=kernel_params(10),
        cost_estimate=LIGHT,
        name="join_sums",
    )(*[part for pair in pairs for part in pair])


def pack_kernel(side_ref, conv_ref, scan_ref, keep_ref, send_ref, total):
    count = conv_ref.shape[0]
    rows = keep_ref.shape[0]
    total[0:count, :] = conv_ref[...]
    total[count:, :] = scan_ref[...]
    side = side_ref[0]
    keep_ref[...] = total[pl.ds(pl.multiple_of(side * rows, rows), rows), :]
    send_ref[...] = total[pl.ds(pl.multiple_of((1 - side) * rows, rows), rows), :].astype(bf16)


def pack_call(side, conv, scan):
    cols = conv.shape[1]
    rows = (conv.shape[0] + scan.shape[0]) // 2
    return pl.pallas_call(
        pack_kernel,
        in_specs=[scalars(), whole(*conv.shape), whole(*scan.shape)],
        out_specs=[whole(rows, cols)] * 2,
        grid=(1,),
        out_shape=[shaped((rows, cols), f32), shaped((rows, cols), bf16)],
        scratch_shapes=[pltpu.VMEM((2 * rows, cols), f32)],
        compiler_params=kernel_params(14),
        cost_estimate=LIGHT,
        name="pack_sums",
    )(side, conv, scan)


def unpack_kernel(spots, side_ref, keep_ref, there_ref, xproj_ref, taps_ref, dtproj_ref, rates_ref, vec_ref, total):
    rows = keep_ref.shape[0]
    cols, tap_count, base, rank, states = spots
    side = side_ref[0]
    total[pl.ds(pl.multiple_of(side * rows, rows), rows), :] = keep_ref[...].astype(f32)
    total[pl.ds(pl.multiple_of((1 - side) * rows, rows), rows), :] = there_ref[...].astype(f32)
    dtproj_ref[...] = total[base : base + rank, :]
    vec_ref[...] = jnp.zeros_like(vec_ref)
    vec_ref[0:1, :] = total[cols + tap_count : cols + tap_count + 1, :]
    vec_ref[1:3, :] = total[base + rank + states : base + rank + states + 2, :]
    for at in range(0, total.shape[1], 128):
        here = slice(at, at + 128)
        xproj_ref[here, :] = jnp.transpose(total[0:cols, here])
        turned = jnp.transpose(total[cols : cols + 128, here])
        taps_ref[here, :] = turned[:, 0:tap_count]
        first = base + rank - cols
        rates_ref[here, :] = turned[:, first : first + states]


def unpack_call(side, keep, there, cols, tap_count, base, rank, states):
    rows, channels = keep.shape
    shapes = [(channels, cols), (channels, tap_count), (rank, channels), (channels, states), (8, channels)]
    return pl.pallas_call(
        functools.partial(unpack_kernel, (cols, tap_count, base, rank, states)),
        grid=(1,),
        in_specs=[scalars(), whole(rows, channels), whole(rows, channels)],
        out_specs=[whole(*shape) for shape in shapes],
        out_shape=[shaped(shape, f32) for shape in shapes],
        scratch_shapes=[pltpu.VMEM((2 * rows, channels), f32)],
        compiler_params=kernel_params(16),
        cost_estimate=LIGHT,
        name="unpack_sums",
    )(side, keep, there)


def fold_kernel(slots, rows, me_ref, keep_ref, there_ref, mine_ref, sent_ref):
    chip = me_ref[0] >> 1
    for slot in range(slots):
        for which, out_ref in ((chip, mine_ref), (1 - chip, sent_ref)):
            here = pl.ds(pl.multiple_of((2 * slot + which) * rows, rows), rows)
            out_ref[slot] = (keep_ref[here, :] + there_ref[here, :].astype(f32)).astype(out_ref.dtype)


def fold_call(me, keep, there, slots):
    count, model = keep.shape
    rows = count // slots // 2
    return pl.pallas_call(
        functools.partial(fold_kernel, slots, rows),
        grid=(1,),
        in_specs=[scalars(), whole(count, model), whole(count, model)],
        out_specs=[whole(slots, rows, model)] * 2,
        out_shape=[shaped((slots, rows, model), f32), shaped((slots, rows, model), bf16)],
        compiler_params=kernel_params(14),
        cost_estimate=LIGHT,
        name="fold_rows",
    )(me, keep, there)


def rows_kernel(
    tokens_ref, cot_ref, mask_ref, mod_ref, branch_ref, branch_far_ref, norm_ref, norm_far_ref,
    mixed_ref, grad_ref, mod_grad_ref
):
    raw = tokens_ref[...].astype(f32)
    mask = mask_ref[...]
    gate = mod_ref[2:3, :]
    branch = branch_ref[...] + branch_far_ref[...].astype(f32)
    mixed_ref[...] = mask * (raw + gate * branch)
    res_grad = mask * cot_ref[...].astype(f32)
    centred = raw - jnp.mean(raw, axis=1, keepdims=True)
    spread = jnp.mean(centred * centred, axis=1, keepdims=True)
    inverse = lax.rsqrt(spread + EPSILON)
    hat = centred * inverse
    normed_grad = mask * (norm_ref[...] + norm_far_ref[...].astype(f32))
    q = normed_grad * (1.0 + mod_ref[1:2, :])
    grad_ref[...] = res_grad + inverse * (
        q - jnp.mean(q, axis=1, keepdims=True) - hat * jnp.mean(q * hat, axis=1, keepdims=True)
    )
    mod_grad_ref[0:1, :] = jnp.sum(normed_grad, axis=0, keepdims=True)
    mod_grad_ref[1:2, :] = jnp.sum(normed_grad * hat, axis=0, keepdims=True)
    mod_grad_ref[2:3, :] = jnp.sum(res_grad * branch, axis=0, keepdims=True)


def rows_call(tokens, cot, mask, mods, branch, branch_far, norm, norm_far):
    slots, rows, model = tokens.shape
    row = pl.BlockSpec((None, rows, model), lambda i: (i, 0, 0))
    mod = pl.BlockSpec((None, 3, model), lambda i: (i, 0, 0))
    return pl.pallas_call(
        rows_kernel,
        grid=(slots,),
        in_specs=[row, row, pl.BlockSpec((None, rows, 1), lambda i: (i, 0, 0)), mod, row, row, row, row],
        out_specs=[row, row, mod],
        out_shape=[
            shaped((slots, rows, model), f32),
            shaped((slots, rows, model), f32),
            shaped((slots, 3, model), f32),
        ],
        compiler_params=kernel_params(14),
        cost_estimate=LIGHT,
        name="owned_rows",
    )(tokens, cot, mask, mods, branch, branch_far, norm, norm_far)


def pick_rows(values_ref, parity, chips, rows):
    blocks = []
    for at in range(values_ref.shape[0] // rows // 2):
        start = pl.multiple_of((2 * at + parity) * rows, rows)
        blocks.append(values_ref[pl.ds(start, rows), :])
    return jnp.concatenate(blocks, 0)


def branch_kernel(rows, flip_ref, values_ref, weight_ref, keep_ref, send_ref):
    core = flip_ref[0]
    keep_ref[...] = matmul(pick_rows(values_ref, core, 2, rows), weight_ref[...])
    send_ref[...] = matmul(pick_rows(values_ref, 1 - core, 2, rows), weight_ref[...]).astype(bf16)


def branch_call(flip, values, weight, rows, width):
    count, depth = values.shape
    model = weight.shape[1]
    out = [shaped((count // 2, model), f32), shaped((count // 2, model), bf16)]
    return pl.pallas_call(
        functools.partial(branch_kernel, rows),
        grid=(model // width,),
        in_specs=[
            pl.BlockSpec(memory_space=pltpu.SMEM),
            pl.BlockSpec((count, depth), lambda j: (0, 0)),
            pl.BlockSpec((depth, width), lambda j: (0, j)),
        ],
        out_specs=[pl.BlockSpec((count // 2, width), lambda j: (0, j))] * 2,
        out_shape=out,
        compiler_params=kernel_params(10),
        cost_estimate=pl.CostEstimate(flops=1000, bytes_accessed=1000, transcendentals=0),
        name="branch_rows",
    )(flip, values, weight)


def proj_back_kernel(rows, flip_ref, x_ref, z_ref, weight_ref, there_ref, keep_ref, send_ref, x_s, z_s, mine_s):
    core = flip_ref[0]
    half = there_ref.shape[1]

    @pl.when(core == 0)
    def _():
        x_s[...] = x_ref[...]
        z_s[...] = z_ref[...]
        mine_s[...] = weight_ref[:, :half]

    @pl.when(core == 1)
    def _():
        x_s[...] = z_ref[...]
        z_s[...] = x_ref[...]
        mine_s[...] = weight_ref[:, half:]

    for parity, out_ref in ((core, keep_ref), (1 - core, send_ref)):
        total = contract_cols(pick_rows(x_s, parity, 2, rows), mine_s[...]) + contract_cols(
            pick_rows(z_s, parity, 2, rows), there_ref[...]
        )
        out_ref[...] = total.astype(out_ref.dtype)


def proj_back_call(flip, x, z, weight, there, rows, width):
    count, depth = x.shape
    model = there.shape[0]
    out = [shaped((count // 2, model), f32), shaped((count // 2, model), bf16)]
    return pl.pallas_call(
        functools.partial(proj_back_kernel, rows),
        grid=(model // width,),
        in_specs=[
            scalars(),
            whole(count, depth),
            whole(count, depth),
            pl.BlockSpec((width, 2 * depth), lambda j: (j, 0)),
            pl.BlockSpec((width, depth), lambda j: (j, 0)),
        ],
        out_specs=[pl.BlockSpec((count // 2, width), lambda j: (0, j))] * 2,
        out_shape=out,
        scratch_shapes=[pltpu.VMEM((count, depth), bf16)] * 2 + [pltpu.VMEM((width, depth), bf16)],
        compiler_params=kernel_params(18),
        cost_estimate=LIGHT,
        name="proj_back",
    )(flip, x, z, held(weight), held(there))


def cond_kernel(mod_ref, weight_ref, cond_ref, out_ref):
    value = cond_ref[...].astype(f32)
    sig = jax.nn.sigmoid(value)
    out_ref[...] = contract_cols(mod_ref[...], weight_ref[...]) * sig * (1.0 + value * (1.0 - sig))


def cond_call(mods, weight, cond):
    slots, columns = mods.shape
    model = weight.shape[0]
    width = 256 if model % 256 == 0 else 128
    return pl.pallas_call(
        cond_kernel,
        grid=(model // width,),
        in_specs=[
            whole(slots, columns),
            pl.BlockSpec((width, columns), lambda j: (j, 0)),
            pl.BlockSpec((slots, width), lambda j: (0, j)),
        ],
        out_specs=pl.BlockSpec((slots, width), lambda j: (0, j)),
        out_shape=shaped((slots, model), f32),
        compiler_params=kernel_params(14),
        cost_estimate=LIGHT,
        name="cond_rows",
    )(mods, held(weight), cond)


def conv_kernel(
    flip_ref, own_ref, other_ref, mask_ref, taps_ref, xproj_ref, x_ref, z_ref, u_ref, dbl_ref, pad
):
    step = pl.program_id(1)
    length, width = own_ref.shape
    flip = flip_ref[0]

    @pl.when(flip == 0)
    def _():
        x_ref[...] = own_ref[...]
        z_ref[...] = other_ref[...]

    @pl.when(flip == 1)
    def _():
        x_ref[...] = other_ref[...]
        z_ref[...] = own_ref[...]

    pad[0:MARGIN, :] = jnp.zeros((MARGIN, width), f32)
    pad[MARGIN + length :, :] = jnp.zeros((MARGIN, width), f32)
    pad[MARGIN : MARGIN + length, :] = x_ref[...].astype(f32)
    taps = taps_ref.shape[0] - 1
    conv = taps_ref[taps : taps + 1, :] + pad[MARGIN : MARGIN + length, :] * taps_ref[taps - 1 : taps, :]
    for by in range(1, taps):
        conv = conv + shifted(pad, length, by, flip) * taps_ref[taps - 1 - by : taps - by, :]
    u = (mask_ref[...] * (conv * jax.nn.sigmoid(conv))).astype(bf16)
    u_ref[...] = u
    part = matmul(u, xproj_ref[...])

    @pl.when(step == 0)
    def _():
        dbl_ref[...] = part

    @pl.when(step > 0)
    def _():
        dbl_ref[...] += part


def conv_back_kernel(
    flip_ref, x_ref, u_ref, mask_ref, taps_ref, xproj_ref, us_ref, dg_ref, prev_ref, keep_ref, send_ref,
    packed_ref, pad
):
    length, width = x_ref.shape
    flip = flip_ref[0]
    pad[0:MARGIN, :] = jnp.zeros((MARGIN, width), f32)
    pad[MARGIN + length :, :] = jnp.zeros((MARGIN, width), f32)
    pad[MARGIN : MARGIN + length, :] = x_ref[...].astype(f32)
    taps = taps_ref.shape[0] - 1
    conv = taps_ref[taps : taps + 1, :] + pad[MARGIN : MARGIN + length, :] * taps_ref[taps - 1 : taps, :]
    for by in range(1, taps):
        conv = conv + shifted(pad, length, by, flip) * taps_ref[taps - 1 - by : taps - by, :]
    sig = jax.nn.sigmoid(conv)
    dg = dg_ref[...]
    u_grad = us_ref[...] + contract_cols(dg, xproj_ref[...])
    conv_grad = u_grad * mask_ref[...] * (sig * (1.0 + conv * (1.0 - sig)))
    cols = dg.shape[1]
    packed_ref[0:cols, :] = prev_ref[0:cols, :] + matmul(jnp.transpose(dg.astype(f32)).astype(bf16), u_ref[...])
    for by in range(taps):
        moved = pad[MARGIN : MARGIN + length, :] if by == 0 else shifted(pad, length, by, flip)
        row = cols + taps - 1 - by
        packed_ref[row : row + 1, :] = prev_ref[row : row + 1, :] + jnp.sum(conv_grad * moved, axis=0, keepdims=True)
    row = cols + taps
    packed_ref[row : row + 1, :] = prev_ref[row : row + 1, :] + jnp.sum(conv_grad, axis=0, keepdims=True)
    rest = packed_ref.shape[0] - cols - taps - 1
    packed_ref[cols + taps + 1 :, :] = jnp.zeros((rest, width), f32)
    pad[MARGIN : MARGIN + length, :] = conv_grad
    grad = conv_grad * taps_ref[taps - 1 : taps, :]
    for by in range(1, taps):
        grad = grad + shifted(pad, length, by, 1 - flip) * taps_ref[taps - 1 - by : taps - by, :]
    grad = grad.astype(bf16)

    @pl.when(pl.program_id(0) == flip)
    def _():
        keep_ref[...] = grad

    @pl.when(pl.program_id(0) != flip)
    def _():
        send_ref[...] = grad


def conv_call(flip, own, other, mask, taps, xproj, width):
    slots, length = mask.shape[:2]
    channels = own.shape[1]
    cols = xproj.shape[1]
    block = pl.BlockSpec((length, width), lambda i, j: (i, j))
    return pl.pallas_call(
        conv_kernel,
        grid=(slots, channels // width),
        in_specs=[
            scalars(),
            block,
            block,
            pl.BlockSpec((None, length, 1), lambda i, j: (i, 0, 0)),
            pl.BlockSpec((taps.shape[0], width), lambda i, j: (0, j)),
            pl.BlockSpec((width, cols), lambda i, j: (j, 0)),
        ],
        out_specs=[block, block, block, pl.BlockSpec((length, cols), lambda i, j: (i, 0))],
        out_shape=[outer((slots * length, channels), bf16)] * 3
        + [shaped((slots * length, cols), f32)],
        scratch_shapes=[pltpu.VMEM((length + 2 * MARGIN, width), f32)],
        compiler_params=kernel_params(12),
        cost_estimate=LIGHT,
        name="conv_forward",
    )(flip, own, other, mask, taps, xproj)


def conv_back_call(flip, slot, x, u, mask, taps, xproj, us, dg, prev):
    length = mask.shape[1]
    channels = x.shape[1]
    cols = xproj.shape[1]
    width = channels // 2
    rows = prev.shape[0]
    item = pl.BlockSpec((length, width), lambda j: (slot, j))
    return pl.pallas_call(
        conv_back_kernel,
        grid=(2,),
        in_specs=[
            scalars(),
            item,
            item,
            pl.BlockSpec((None, length, 1), lambda j: (slot, 0, 0)),
            pl.BlockSpec((taps.shape[0], width), lambda j: (0, j)),
            pl.BlockSpec((width, cols), lambda j: (j, 0)),
            pl.BlockSpec((length, width), lambda j: (0, j)),
            whole(length, cols),
            pl.BlockSpec((rows, width), lambda j: (0, j)),
        ],
        out_specs=[
            whole(length, width),
            whole(length, width),
            pl.BlockSpec((rows, width), lambda j: (0, j)),
        ],
        out_shape=[
            shaped((length, width), bf16),
            shaped((length, width), bf16),
            shaped((rows, channels), f32),
        ],
        scratch_shapes=[pltpu.VMEM((length + 2 * MARGIN, width), f32)],
        compiler_params=kernel_params(16),
        cost_estimate=LIGHT,
        name="conv_backward",
    )(flip, held(x), held(u), mask, taps, xproj, held(us), dg, prev)


def spread(dbl_ref, first, b_wide, c_wide, rows_s, states):
    length, cols = dbl_ref.shape
    rest = dbl_ref[...]
    row = lax.broadcasted_iota(jnp.int32, (cols, cols), 0)
    col = lax.broadcasted_iota(jnp.int32, (cols, cols), 1)
    rows = jnp.zeros((length, cols), f32)
    for part in range(3):
        piece = rest.astype(bf16)
        rest = rest - piece.astype(f32)
        pick = ((row == first + col % (2*states)) & (col // (2*states) == part))
        rows = rows + matmul(piece, jnp.where(pick, 1.0, 0.0).astype(bf16))
    rows_s[...] = rows
    which = lax.broadcasted_iota(jnp.int32, (states, cols), 0)
    lane = lax.broadcasted_iota(jnp.int32, (states, cols), 1)
    mine = jnp.where(lane % states == which, 1.0, 0.0)
    row = lax.broadcasted_iota(jnp.int32, (cols, 2*cols), 0)
    col = lax.broadcasted_iota(jnp.int32, (cols, 2*cols), 1)
    wide = jnp.where((row % (2*states)) // states == col // cols, 1.0, 0.0).astype(bf16)
    def some(at, _):
        left = [(mine*jnp.broadcast_to(rows_s[pl.ds(at*CHUNK+t, 1), :], (states, cols))).astype(bf16) for t in range(CHUNK)]
        got = matmul(jnp.concatenate(left, 0), wide)
        here = pl.ds(pl.multiple_of(at*CHUNK*states, CHUNK*states), CHUNK*states)
        b_wide[here, :] = got[:, :cols]
        c_wide[here, :] = got[:, cols:]
        return 0
    lax.fori_loop(0, length//CHUNK, some, 0, unroll=4)

def tiles_of(values):
    return [values[:, at:at+128] for at in range(0, values.shape[1], 128)]

def fold(values, tmp, tt, states):
    for at, tile in enumerate(tiles_of(values)):
        total = tile[:8]
        for part in range(1, states//8):
            total = total + tile[part*8:(part+1)*8]
        tmp[at, pl.ds(tt//8*64 + tt%8, 8, stride=8), :] = total

def add_tiles(values):
    parts = tiles_of(values)
    total = parts[0]
    for part in parts[1:]:
        total = total + part
    return total

def unfold(tmp, out, base):
    for at in range(out.shape[1]//128):
        for part in range(CHUNK//8):
            acc = tmp[at, part*64:part*64+8, :]
            for row in range(1, 8):
                acc = acc + tmp[at, part*64+row*8:part*64+row*8+8, :]
            out[pl.ds(pl.multiple_of(base+part*8, 8), 8), at*128:(at+1)*128] = acc

def collect(acc, tmp, out, length, states):
    which = lax.broadcasted_iota(jnp.int32, (states, 128), 0)
    lane = lax.broadcasted_iota(jnp.int32, (states, 128), 1)
    mine = which == lane
    def some(at, _):
        base = pl.multiple_of(at*CHUNK, CHUNK)
        for tt in range(CHUNK):
            sums = jnp.sum(acc[pl.ds((base+tt)*states, states), :], axis=1, keepdims=True)
            fold(jnp.where(mine, sums, 0.0), tmp, tt, states)
        unfold(tmp, out, base)
        return 0
    lax.fori_loop(0, length//CHUNK, some, 0, unroll=4)

def fwd_kernel(states, flip_ref, dbl_ref, dtp_ref, vec_ref, rate2_ref, u_ref, z_ref, gg_ref,
               gate_keep, gate_send, z_keep, z_send, delta_ref, yg_ref, prior_ref, cout_ref,
               b_wide, c_wide, drive_s, y_s, y_tmp, c_acc, rows_s):
    step = pl.program_id(1)
    length, width = u_ref.shape
    rank = dtp_ref.shape[0]
    group = CHUNK*states
    chunks = length//CHUNK
    flip = flip_ref[0]
    @pl.when(step == 0)
    def _():
        spread(dbl_ref, rank, b_wide, c_wide, rows_s, states)
        c_acc[...] = jnp.zeros_like(c_acc)
    low = dbl_ref[:, :rank].astype(bf16)
    pre = matmul(low, dtp_ref[...]) + vec_ref[0:1, :]
    delta = jnp.maximum(pre, 0.0) + jnp.log1p(jnp.exp(-jnp.abs(pre)))
    delta_ref[...] = delta
    drive_s[...] = delta * u_ref[...].astype(f32)
    z = z_ref[...].astype(f32)
    yg_ref[...] = gg_ref[...].astype(f32) * (z * (0.5 + 0.5*jnp.tanh(0.5*z)))
    def run(flipped):
        def ahead(chunk, state):
            place = chunks-1-chunk if flipped else chunk
            base = pl.multiple_of(place*CHUNK, CHUNK)
            wide = pl.multiple_of(place*group, group)
            for at in range(CHUNK):
                tt = CHUNK-1-at if flipped else at
                t = base + tt
                here = pl.ds(wide + tt*states, states)
                d = jnp.broadcast_to(delta_ref[pl.ds(t,1),:], (states,width))
                x = jnp.broadcast_to(drive_s[pl.ds(t,1),:], (states,width))
                g = jnp.broadcast_to(yg_ref[pl.ds(t,1),:], (states,width))
                b = jnp.concatenate([b_wide[here,:]]*(width//128), axis=1)
                c = jnp.concatenate([c_wide[here,:]]*(width//128), axis=1)
                prior = jnp.exp2(d*rate2_ref[...])*state
                state = prior + x*b
                prior_ref[here,:] = prior.astype(bf16)
                fold(state*c, y_tmp, tt, states)
                c_acc[here,:] += add_tiles(state*g)
            unfold(y_tmp, y_s, base)
            return state
        lax.fori_loop(0, chunks, ahead, jnp.zeros((states,width), f32))
    pl.when(flip == 0)(lambda: run(False))
    pl.when(flip == 1)(lambda: run(True))
    u = u_ref[...].astype(f32)
    z = z_ref[...].astype(f32)
    sig = (0.5 + 0.5*jnp.tanh(0.5*z))
    y = y_s[...] + vec_ref[1:2,:]*u
    gated = (y*(z*sig)).astype(bf16)
    zg = (gg_ref[...].astype(f32)*y*(sig*(1.0+z*(1.0-sig)))).astype(bf16)
    half = gate_keep.shape[1]
    for at in range(2*half//width):
        for core in range(2):
            def put(at=at, core=core):
                for side in range(2):
                    low, high = max(at*width, side*half), min((at+1)*width, (side+1)*half)
                    if low < high:
                        to = slice(low-side*half, high-side*half)
                        of = slice(low-at*width, high-at*width)
                        (gate_keep if side == core else gate_send)[:, to] = gated[:, of]
                        (z_keep if side == core else z_send)[:, to] = zg[:, of]
            pl.when((step == at) & (flip == core))(put)
    @pl.when(step == pl.num_programs(1)-1)
    def _():
        collect(c_acc, y_tmp, rows_s, length, states)
        cout_ref[...] = rows_s[:, :states]

def bwd_kernel(states, flip_ref, dbl_ref, dtp_ref, vec_ref, rate2_ref, u_ref, delta_ref, yg_ref, prior_ref, cout_ref, prev_ref,
               us_ref, part_ref, packed_ref,
               b_wide, c_wide, drive_s, r_s, w_s, low_t, rank_s, r_tmp, w_tmp, b_acc, rows_s):
    step = pl.program_id(0)
    length, width = u_ref.shape
    rank = dtp_ref.shape[0]
    group = CHUNK*states
    chunks = length//CHUNK
    flip = flip_ref[0]
    @pl.when(step == 0)
    def _():
        low_t[...] = jnp.transpose(dbl_ref[...])[:rank,:].astype(bf16)
        spread(dbl_ref, rank, b_wide, c_wide, rows_s, states)
        b_acc[...] = jnp.zeros_like(b_acc)
        rank_s[...] = jnp.zeros_like(rank_s)
    u = u_ref[...].astype(f32)
    drive_s[...] = delta_ref[...]*u
    def run(flipped):
        def back(chunk, carry):
            carried, total = carry
            place = chunk if flipped else chunks-1-chunk
            base = pl.multiple_of(place*CHUNK, CHUNK)
            wide = pl.multiple_of(place*group, group)
            for at in range(CHUNK):
                tt = at if flipped else CHUNK-1-at
                t = base + tt
                here = pl.ds(wide + tt*states, states)
                d = jnp.broadcast_to(delta_ref[pl.ds(t,1),:], (states,width))
                x = jnp.broadcast_to(yg_ref[pl.ds(t,1),:], (states,width))
                e = jnp.broadcast_to(drive_s[pl.ds(t,1),:], (states,width))
                b = jnp.concatenate([b_wide[here,:]]*(width//128), axis=1)
                c = jnp.concatenate([c_wide[here,:]]*(width//128), axis=1)
                power = d*rate2_ref[...]
                adj = carried + x*c
                moved = (adj*prior_ref[here,:].astype(f32))*power
                total = total + moved
                fold(moved, w_tmp, tt, states)
                fold(adj*b, r_tmp, tt, states)
                b_acc[here,:] += add_tiles(adj*e)
                carried = jnp.exp2(power)*adj
            unfold(w_tmp, w_s, base)
            unfold(r_tmp, r_s, base)
            return carried, total
        zero = jnp.zeros((states,width), f32)
        _, total = lax.fori_loop(0, chunks, back, (zero, zero))
        packed_ref[rank:rank+states,:] = prev_ref[rank:rank+states,:] + total*(1.0/LOG2E)
    pl.when(flip == 0)(lambda: run(False))
    pl.when(flip == 1)(lambda: run(True))
    yg = yg_ref[...]
    r = r_s[...]
    delta = delta_ref[...]
    us_ref[...] = delta*r + vec_ref[1:2,:]*yg
    low = dbl_ref[:, :rank].astype(bf16)
    pre = matmul(low, dtp_ref[...]) + vec_ref[0:1,:]
    sig = jnp.exp(pre-delta)
    ratio = jnp.where(delta > 1e-30, sig/jnp.maximum(delta, 1e-30), 1.0)
    pre_grad = w_s[...]*(1.0/LOG2E)*ratio + u*r*sig
    pre_low = pre_grad.astype(bf16)
    rank_s[...] += contract_cols(pre_low, dtp_ref[...])
    packed_ref[0:rank,:] = prev_ref[0:rank,:] + matmul(low_t[...], pre_low)
    packed_ref[rank+states:rank+states+1,:] = prev_ref[rank+states:rank+states+1,:] + jnp.sum(pre_grad, axis=0, keepdims=True)
    packed_ref[rank+states+1:rank+states+2,:] = prev_ref[rank+states+1:rank+states+2,:] + jnp.sum(yg*u, axis=0, keepdims=True)
    rest = packed_ref.shape[0]-rank-states-2
    packed_ref[rank+states+2:,:] = jnp.zeros((rest,width), f32)
    @pl.when(step == pl.num_programs(0)-1)
    def _():
        collect(b_acc, r_tmp, rows_s, length, states)
        part_ref[...] = jnp.concatenate([rank_s[...], rows_s[:, :states], cout_ref[...]], axis=1)


def forward_call(flip, dbl, dtproj, vec, rates2, u, z, gg, slots, width):
    count, channels = u.shape
    length = count // slots
    half = channels // 2
    states, rank, cols = rates2.shape[0], dtproj.shape[0], dbl.shape[1]
    weight = lambda rows: pl.BlockSpec((rows, width), lambda i, j: (0, j))
    block = lambda rows: pl.BlockSpec((rows, width), lambda i, j: (i, j))
    item = lambda wide: pl.BlockSpec((length, wide), lambda i, j: (i, 0))
    return pl.pallas_call(
        functools.partial(fwd_kernel, states),
        grid=(slots, channels // width),
        in_specs=[scalars(), item(cols), weight(rank), weight(2), weight(states)] + [block(length)] * 3,
        out_specs=[item(half)] * 4 + [block(length)] * 2 + [block(length * states), item(states)],
        out_shape=[outer((count, half), bf16)] * 4
        + [outer((count, channels), f32)] * 2
        + [outer((count * states, channels), bf16), shaped((count, states), f32)],
        scratch_shapes=[
            pltpu.VMEM((length * states, 128), f32),
            pltpu.VMEM((length * states, 128), f32),
            pltpu.VMEM((length, width), f32),
            pltpu.VMEM((length, width), f32),
            pltpu.VMEM((width // 128, CHUNK * 8, 128), f32),
            pltpu.VMEM((length * states, 128), f32),
            pltpu.VMEM((length, cols), f32),
        ],
        compiler_params=kernel_params(40),
        cost_estimate=pl.CostEstimate(
            flops=32000000000, bytes_accessed=40000000, transcendentals=14000000
        ),
        name="scan_forward",
    )(flip, dbl, dtproj, vec, rates2, held(u), held(z), held(gg))


def backward_call(flip, slot, slots, dbl, dtproj, vec, rates2, u, delta, yg, prior, cout, prev, width):
    count, channels = u.shape
    length = count // slots
    states, rank, cols = rates2.shape[0], dtproj.shape[0], dbl.shape[1]
    rows = prev.shape[0]
    weight = lambda rows: pl.BlockSpec((rows, width), lambda j: (0, j))
    block = lambda rows: pl.BlockSpec((rows, width), lambda j: (slot, j))
    item = lambda wide: pl.BlockSpec((length, wide), lambda j: (slot, 0))
    return pl.pallas_call(
        functools.partial(bwd_kernel, states),
        grid=(channels // width,),
        in_specs=[scalars(), item(cols), weight(rank), weight(2), weight(states)]
        + [block(length)] * 3
        + [block(length * states), item(states), weight(rows)],
        out_specs=[weight(length), whole(length, cols), weight(rows)],
        out_shape=[
            outer((length, channels), f32),
            shaped((length, cols), f32),
            shaped((rows, channels), f32),
        ],
        scratch_shapes=[
            pltpu.VMEM((length * states, 128), f32),
            pltpu.VMEM((length * states, 128), f32),
            pltpu.VMEM((length, width), f32),
            pltpu.VMEM((length, width), f32),
            pltpu.VMEM((length, width), f32),
            pltpu.VMEM((rank, length), bf16),
            pltpu.VMEM((length, rank), f32),
            pltpu.VMEM((width // 128, CHUNK * 8, 128), f32),
            pltpu.VMEM((width // 128, CHUNK * 8, 128), f32),
            pltpu.VMEM((length * states, 128), f32),
            pltpu.VMEM((length, cols), f32),
        ],
        compiler_params=kernel_params(40),
        cost_estimate=pl.CostEstimate(
            flops=22000000000, bytes_accessed=20000000, transcendentals=7000000
        ),
        name="scan_backward",
    )(flip, dbl, dtproj, vec, rates2, held(u), held(delta), held(yg), held(prior), cout, prev)


def local(
    tokens,
    cond,
    counts,
    valid,
    ada_weight,
    ada_bias,
    in_weight,
    conv_weight,
    conv_bias,
    xproj_weight,
    dtproj_weight,
    dt_bias,
    a_log,
    skip_gain,
    out_weight,
    cotangent,
):
    slot_count, shard_rows, model = tokens.shape
    dirs = lax.axis_size("dir")
    dps = lax.axis_size("dp")
    me = lax.axis_index("dir")
    dp_index = lax.axis_index("dp")
    core = me & 1
    half = in_weight.shape[1] // 2
    rank = dtproj_weight.shape[0]
    states = a_log.shape[1]
    tap_count = conv_weight.shape[1]
    cols = xproj_weight.shape[1]
    slots = range(slot_count)
    width = 512 if dt_bias.shape[0] % 512 == 0 else 128
    first, second = bit_orders("dp")
    z_bit, out_bit = first[0], second[0]
    scalar = lambda value: value.astype(jnp.int32).reshape(1)
    flip, me_ref = scalar(core), scalar(me)
    z_side, out_side = scalar((dp_index >> z_bit) & 1), scalar((dp_index >> out_bit) & 1)

    live_slots = (jnp.arange(slot_count) < counts[0]).astype(f32)
    full_mask = valid.astype(f32) * live_slots[:, None]
    mask_cols = full_mask[:, :, None]
    local_mask = lax.dynamic_slice_in_dim(full_mask, me * shard_rows, shard_rows, 1)[:, :, None]

    def gather_rows(block, *earlier):
        over = after(swap(block, "dir", 1), *earlier)
        return block, over, swap(block, "dir", 0), swap(over, "dir", 0)

    in_send = lax.dynamic_slice_in_dim(in_weight, (1 - core) * half, half, 1)
    in_there = swap(in_send, "dir", 0)
    cond_act = jax.nn.silu(cond.astype(f32)).astype(bf16)
    modulation = matmul(after(cond_act, in_send), ada_weight) + ada_bias.astype(f32)[None, :]
    mods = modulation.reshape(slot_count, 3, model)
    token_blocks = gather_rows(tokens, modulation)
    cot_blocks = gather_rows(cotangent, token_blocks[1])
    out_there = swap(out_weight, "dir", 0)

    taps = jnp.concatenate(
        [jnp.transpose(conv_weight.astype(f32)), conv_bias.astype(f32)[None, :]], 0
    )
    vec = jnp.stack([dt_bias, skip_gain])
    rates2 = -jnp.exp(jnp.transpose(a_log)) * LOG2E

    left_mine, left_give, own = norm_call(
        me_ref,
        z_side,
        token_blocks,
        mask_cols,
        after(mods, cot_blocks[1]),
        in_weight,
        width,
        model // dps << z_bit,
    )
    other = swap(own, "dir", 0)
    x, z, u, part = conv_call(flip, own, other, mask_cols, taps, xproj_weight, half)
    part_there = swap(part, "dir", 1)
    branch_mine, branch_give, gg = gate_call(
        me_ref,
        out_side,
        cot_blocks,
        mask_cols,
        after(mods, part),
        out_weight,
        out_there,
        model // dps << out_bit,
    )
    left_there = swap(left_give, "dp", z_bit)
    branch_there = swap(branch_give, "dp", out_bit)
    dbl = part + after(part_there, gg)
    gate_keep, gate_send, z_keep, z_send, *saved = forward_call(
        flip, dbl, dtproj_weight, vec, rates2, u, z, gg, slot_count, width
    )
    gate_send, z_send = after((gate_send, z_send), left_there, branch_there)
    gate_all, z_all = pair_call(
        gate_keep, swap(gate_send, "dir", 0), z_keep, swap(z_send, "dir", 0), slot_count
    )
    gate_there = swap(gate_all, "dp", out_bit)
    z_there = swap(z_all, "dp", z_bit)

    rest = lambda out: [bit for bit in first if bit != out]
    scan_rows = -(-(rank + states + 2) // 8) * 8
    packed = jnp.zeros((scan_rows, dt_bias.shape[0]), f32)
    backs, dgs = [], []
    u_tied = after(u, z_all, gate_all)
    for slot in slots:
        us, part_back, packed = backward_call(
            flip, slot, slot_count, dbl, dtproj_weight, vec, rates2, u_tied, *saved, packed, width
        )
        there = swap(part_back, "dir", 1)
        backs.append((us, part_back, there))
        if slot == 0:
            z_part = Scatter(
                contract_rows(left_mine, after(z_all, part_back))
                + contract_rows(left_there, after(z_there, part_back)),
                "dp",
                rest(z_bit),
            )
            out_part = Scatter(
                contract_rows(branch_mine, after(gate_all, part_back))
                + contract_rows(branch_there, after(gate_there, part_back)),
                "dp",
                rest(out_bit),
            )
            dgs.append((part_back + after(there, z_part.send, out_part.send)).astype(bf16))
            u_tied, z_part.send, out_part.send = after((u, z_part.send, out_part.send), dgs[0])
    end = backs[-1][1]
    z_part.step(end)
    out_part.step(end)

    conv_rows = -(-(cols + tap_count + 1) // 8) * 8
    conv_packed = jnp.zeros((conv_rows, dt_bias.shape[0]), f32)
    pairs = []
    for slot in slots:
        us, part_back, there = backs[slot]
        if slot == 0:
            dg = after(dgs[0], z_part.send, out_part.send)
        else:
            dg = (part_back + after(there, pairs[-1][0])).astype(bf16)
        keep, send, conv_packed = conv_back_call(
            flip, slot, x, u, mask_cols, taps, xproj_weight, us, dg, conv_packed
        )
        pairs.append((keep, send))
    z_part.step(pairs[-1][1])
    pairs = [(keep, swap(after(send, z_part.values), "dir", 0)) for keep, send in pairs]
    x_all = join_call(pairs)
    x_there = swap(x_all, "dp", z_bit)
    shared = SharedSum(pack_call(out_side, after(conv_packed, x_all), packed), "dp", second)
    norm_keep, norm_give = proj_back_call(
        flip, after(x_all, shared.send), z_all, in_weight, in_there, shard_rows, width
    )
    rows_keep, rows_give = branch_call(
        flip, after(gate_all, norm_give), out_weight, shard_rows, width
    )
    out_part.step(rows_give)
    shared.step(out_part.values)
    x_part = contract_rows(left_mine, after(x_all, shared.send)) + contract_rows(
        left_there, after(x_there, shared.send)
    )
    x_part = Scatter(x_part, "dp", rest(z_bit))
    norm_there = swap(after(norm_give, x_part.send), "dir", 0)
    rows_there = swap(after(rows_give, x_part.send), "dir", 0)
    norm_mine, norm_sent = fold_call(me_ref, norm_keep, norm_there, slot_count)
    norm_far = swap(norm_sent, "dir", 1)
    rows_mine, branch_sent = fold_call(me_ref, rows_keep, after(rows_there, norm_sent), slot_count)
    branch_far = swap(branch_sent, "dir", 1)
    shared.step(branch_sent)

    mixed, token_grads, mod_part = rows_call(
        tokens,
        cotangent,
        local_mask,
        mods,
        rows_mine,
        after(branch_far, shared.send),
        norm_mine,
        after(norm_far, shared.send),
    )
    mod_there = swap(mod_part, "dir", 0)
    shared.step(mod_part)
    x_part.step(shared.send)
    mod_pair = mod_part + after(mod_there, x_part.send)
    mod_far = swap(mod_pair, "dir", 1)
    shared.step(mod_pair)
    mod_total = mod_pair + after(mod_far, shared.send)
    mod_low = mod_total.astype(bf16).reshape(slot_count, 3 * model)
    cond_grad = cond_call(mod_low, ada_weight, cond)
    have = []
    sides = jnp.concatenate([mod_low, after(cond_act, end)], 1)
    sides = gather_bit(sides, "dp", first[0], have, cond_grad)
    while len(shared.plan) > 1:
        shared.step(sides)
    keep, there = shared.last(sides)
    for bit in first[1:-1]:
        sides = gather_bit(sides, "dp", bit, have)
    sides = gather_bit(sides, "dp", first[-1], have)
    sides = sides.reshape(dps * slot_count, -1)
    total_columns = ada_weight.shape[1]
    columns = total_columns // dirs
    rows = ada_weight.shape[0] // dps
    mod_all = lax.dynamic_slice_in_dim(sides, me * columns, columns, 1)
    act_mine = lax.dynamic_slice_in_dim(sides, total_columns + dp_index * rows, rows, 1)
    ada_sum = contract_rows(act_mine, mod_all)
    portion = total_columns // dps
    bias_part = lax.dynamic_slice_in_dim(sides, dp_index * portion, portion, 1)
    bias_sum = jnp.sum(bias_part.astype(f32), axis=0)

    xproj_sum, kernel_sum, dtproj_sum, rate_sum, vec_sum = unpack_call(
        out_side, keep, there, cols, tap_count, conv_rows, rank, states
    )
    while x_part.order:
        x_part.step(xproj_sum)
    while z_part.order:
        z_part.step(xproj_sum)
    while out_part.order:
        out_part.step(xproj_sum)
    x_sum = x_part.values
    z_sum = z_part.values
    out_sum = jnp.transpose(out_part.values)
    keep_sum = jnp.where(core == 0, x_sum, z_sum)
    send_sum = jnp.where(core == 0, z_sum, x_sum)
    in_sum = ordered(core, keep_sum, swap(send_sum, "dir", 0), 1)

    return (
        mixed,
        token_grads,
        cond_grad,
        ada_sum,
        bias_sum,
        in_sum,
        kernel_sum,
        vec_sum[0],
        xproj_sum,
        dtproj_sum,
        vec_sum[1],
        rate_sum,
        vec_sum[2],
        out_sum,
    )


def solution(mesh):
    in_specs = (
        P("dp", "dir", None),
        P("dp", None),
        P("dp"),
        P("dp", None),
        P(),
        P(),
        P(None, "dir"),
        P("dir", None),
        P("dir"),
        P("dir", None),
        P(None, "dir"),
        P("dir"),
        P("dir", None),
        P("dir"),
        P("dir", None),
        P("dp", "dir", None),
    )
    out_specs = (
        P("dp", "dir", None),
        P("dp", "dir", None),
        P("dp", None),
        P("dp", "dir"),
        P("dp"),
        P("dp", "dir"),
        P("dir", None),
        P("dir"),
        P("dir", None),
        P(None, "dir"),
        P("dir"),
        P("dir", None),
        P("dir"),
        P("dir", "dp"),
    )
    return jax.shard_map(local, mesh=mesh, in_specs=in_specs, out_specs=out_specs, check_vma=False)
```

```python
import functools

import jax
import jax.numpy as jnp
from jax import lax
from jax.experimental import pallas as pl
from jax.experimental.pallas import tpu as pltpu
from jax.sharding import PartitionSpec as P

EPSILON = 1e-06
LOG2E = 1.4426950408889634
CHUNK = 16
MARGIN = 8

bf16 = jnp.bfloat16
f32 = jnp.float32


def swap(block, axis, bit):
    count = lax.axis_size(axis)
    return lax.ppermute(block, axis, [(at, at ^ (1 << bit)) for at in range(count)])


def contract_rows(left, right):
    return lax.dot_general(
        left, right, (((0,), (0,)), ((), ())), preferred_element_type=f32
    )


def contract_cols(left, right):
    return lax.dot_general(
        left, right, (((1,), (1,)), ((), ())), preferred_element_type=f32
    )


def matmul(left, right):
    return jnp.dot(left, right, preferred_element_type=f32)


def ordered(bit, own, other, axis):
    return jnp.where(
        bit == 0,
        jnp.concatenate([own, other], axis),
        jnp.concatenate([other, own], axis),
    )


def halves(values, bit, axis):
    size = values.shape[axis] // 2
    keep = lax.dynamic_slice_in_dim(values, bit * size, size, axis)
    send = lax.dynamic_slice_in_dim(values, (1 - bit) * size, size, axis)
    return keep, send


class Scatter:
    def __init__(self, values, axis, order):
        self.axis, self.order = axis, list(order)
        bits = len(order)
        self.values = values.reshape((2,) * bits + (values.shape[0] >> bits,) + values.shape[1:])
        self.left = sorted(order, reverse=True)
        self.split()

    def split(self):
        if not self.order:
            return
        at = self.left.index(self.order[0])
        mine = (lax.axis_index(self.axis) >> self.order[0]) & 1
        self.keep = lax.dynamic_index_in_dim(self.values, mine, at, keepdims=False)
        send = lax.dynamic_index_in_dim(self.values, 1 - mine, at, keepdims=False)
        self.send = send.astype(bf16)

    def step(self, *earlier):
        bit = self.order.pop(0)
        self.left.remove(bit)
        arrived = after(swap(self.send, self.axis, bit), *earlier)
        self.values = self.keep.astype(f32) + arrived.astype(f32)
        self.split()


class SharedSum:
    def __init__(self, values, axis, order):
        self.axis = axis
        few = list(order[:2])
        self.plan = [("halve", bit) for bit in few] + [("add", bit) for bit in order[2:]]
        self.plan += [("join", bit) for bit in few[::-1]]
        self.start(*values)

    def start(self, keep, send):
        self.keep, self.send = keep, send

    def begin(self):
        kind, bit = self.plan[0] if self.plan else ("", 0)
        self.mine = (lax.axis_index(self.axis) >> bit) & 1
        if kind == "halve":
            self.keep, self.send = halves(self.values, self.mine, 0)
            self.send = self.send.astype(bf16)
        else:
            self.keep = self.send = self.values.astype(bf16)

    def step(self, *earlier):
        kind, bit = self.plan.pop(0)
        arrived = after(swap(self.send, self.axis, bit), *earlier)
        if kind == "join":
            self.values = ordered(self.mine, self.keep, arrived, 0)
        else:
            self.values = self.keep.astype(f32) + arrived.astype(f32)
        self.begin()

    def last(self, *earlier):
        _, bit = self.plan.pop(0)
        return self.keep, after(swap(self.send, self.axis, bit), *earlier)


def after(values, *earlier):
    return lax.optimization_barrier((values, earlier))[0] if earlier else values


def gather_bit(values, axis, bit, have, *earlier):
    at = len([other for other in have if other > bit])
    mine = (lax.axis_index(axis) >> bit) & 1
    arrived = after(swap(values, axis, bit), *earlier)
    have.append(bit)
    return jnp.where(
        mine == 0, jnp.stack([values, arrived], at), jnp.stack([arrived, values], at)
    )


def gather_rest(values, axis, bits, *earlier):
    codes = [code << bits[0] for code in range(1 << len(bits))]
    got = [values] + [
        lax.ppermute(values, axis, [(at, at ^ code) for at in range(lax.axis_size(axis))])
        for code in codes[1:]
    ]
    got = after(got, *earlier)
    mine = lax.axis_index(axis) >> bits[0]
    stacked = jnp.stack(got)
    return jnp.take(stacked, jnp.arange(len(codes)) ^ mine, axis=0)


def bit_orders(axis):
    bits = lax.axis_size(axis).bit_length() - 1
    first = list(range(bits))
    second = list(range(bits))
    if bits > 1:
        second[0], second[1] = 1, 0
    return first, second


def kernel_params(megabytes):
    return pltpu.CompilerParams(vmem_limit_bytes=megabytes * 1024 * 1024)


LIGHT = pl.CostEstimate(flops=1000, bytes_accessed=1000, transcendentals=0)


def whole(*shape):
    return pl.BlockSpec(shape, lambda *at: (0,) * len(shape))


def scalars():
    return pl.BlockSpec(memory_space=pltpu.SMEM)


def shaped(shape, kind):
    return jax.ShapeDtypeStruct(shape, kind)


def outer(shape, kind):
    return pltpu.HBM(shape, kind)


def held(values):
    return pltpu.with_memory_space_constraint(values, pltpu.HBM)


def split_columns(values_ref, side_ref, chunk, keep_ref, give_ref):
    for side in range(2):

        @pl.when(side_ref[0] == side)
        def _():
            for at, start in enumerate(range(0, values_ref.shape[1], 2 * chunk)):
                to = slice(at * chunk, (at + 1) * chunk)
                first = values_ref[:, start : start + chunk]
                second = values_ref[:, start + chunk : start + 2 * chunk]
                keep_ref[:, to] = second if side else first
                give_ref[:, to] = first if side else second


def norm_kernel(
    chunk, me_ref, side_ref, own_ref, over_ref, beside_ref, far_ref, mask_ref, mod_ref, weight_ref,
    keep_ref, give_ref, proj_ref, normed_s
):
    slots, rows, _ = own_ref.shape
    length = mask_ref.shape[1]

    @pl.when(pl.program_id(0) == 0)
    def _():
        for slot in range(slots):
            shift = mod_ref[slot, 0:1, :]
            scale = mod_ref[slot, 1:2, :]
            for code, block in ((0, own_ref), (2, over_ref), (1, beside_ref), (3, far_ref)):
                start = pl.multiple_of((me_ref[0] ^ code) * rows, rows)
                raw = block[slot].astype(f32)
                centred = raw - jnp.mean(raw, axis=1, keepdims=True)
                spread = jnp.mean(centred * centred, axis=1, keepdims=True)
                hat = centred * lax.rsqrt(spread + EPSILON)
                mask = mask_ref[slot, pl.ds(start, rows), :]
                normed_s[pl.ds(slot * length + start, rows), :] = (
                    mask * (hat * (1.0 + scale) + shift)
                ).astype(bf16)
        split_columns(normed_s, side_ref, chunk, keep_ref, give_ref)

    proj_ref[...] = matmul(normed_s[...], weight_ref[...]).astype(bf16)


def norm_call(me, side, blocks, mask, mods, weight, width, chunk):
    slots, rows, model = blocks[0].shape
    count = slots * mask.shape[1]
    channels = weight.shape[1]
    return pl.pallas_call(
        functools.partial(norm_kernel, chunk),
        grid=(channels // width,),
        in_specs=[scalars(), scalars()]
        + [whole(slots, rows, model)] * 4
        + [whole(*mask.shape), whole(slots, 3, model), pl.BlockSpec((model, width), lambda j: (0, j))],
        out_specs=[
            whole(count, model // 2),
            whole(count, model // 2),
            pl.BlockSpec((count, width), lambda j: (0, j)),
        ],
        out_shape=[
            shaped((count, model // 2), bf16),
            shaped((count, model // 2), bf16),
            shaped((count, channels), bf16),
        ],
        scratch_shapes=[pltpu.VMEM((count, model), bf16)],
        compiler_params=kernel_params(20),
        cost_estimate=LIGHT,
        name="norm_project",
    )(me, side, *blocks, mask, mods, held(weight))


def gate_kernel(
    chunk, me_ref, side_ref, own_ref, over_ref, beside_ref, far_ref, mask_ref, mod_ref, mine_ref,
    theirs_ref, keep_ref, give_ref, out_ref, grad_s
):
    slots, rows, _ = own_ref.shape
    length = mask_ref.shape[1]
    step = pl.program_id(0)

    @pl.when(step == 0)
    def _():
        for slot in range(slots):
            gate = mod_ref[slot, 2:3, :]
            for code, block in ((0, own_ref), (2, over_ref), (1, beside_ref), (3, far_ref)):
                start = pl.multiple_of((me_ref[0] ^ code) * rows, rows)
                mask = mask_ref[slot, pl.ds(start, rows), :]
                grad_s[pl.ds(slot * length + start, rows), :] = (
                    mask * block[slot].astype(f32) * gate
                ).astype(bf16)
        split_columns(grad_s, side_ref, chunk, keep_ref, give_ref)

    @pl.when(step < pl.num_programs(0) // 2)
    def _():
        out_ref[...] = contract_cols(grad_s[...], mine_ref[...]).astype(bf16)

    @pl.when(step >= pl.num_programs(0) // 2)
    def _():
        out_ref[...] = contract_cols(grad_s[...], theirs_ref[...]).astype(bf16)


def gate_call(me, side, blocks, mask, mods, mine, theirs, chunk):
    slots, rows, model = blocks[0].shape
    count = slots * mask.shape[1]
    quarter = mine.shape[0]
    parts = 2
    width = quarter // parts

    def out_at(j, me_ref, side_ref):
        return (0, ((me_ref[0] & 1) ^ (j // parts)) * parts + j % parts)

    fixed = lambda *shape: pl.BlockSpec(shape, lambda j, *refs: (0,) * len(shape))
    return pl.pallas_call(
        functools.partial(gate_kernel, chunk),
        grid_spec=pltpu.PrefetchScalarGridSpec(
            num_scalar_prefetch=2,
            grid=(2 * parts,),
            in_specs=[fixed(slots, rows, model)] * 4
            + [
                fixed(*mask.shape),
                fixed(slots, 3, model),
                pl.BlockSpec((width, model), lambda j, *refs: (jnp.minimum(j, parts - 1), 0)),
                pl.BlockSpec((width, model), lambda j, *refs: (jnp.maximum(j - parts, 0), 0)),
            ],
            out_specs=[
                fixed(count, model // 2),
                fixed(count, model // 2),
                pl.BlockSpec((count, width), out_at),
            ],
            scratch_shapes=[pltpu.VMEM((count, model), bf16)],
        ),
        out_shape=[
            shaped((count, model // 2), bf16),
            shaped((count, model // 2), bf16),
            outer((count, 2 * quarter), bf16),
        ],
        compiler_params=kernel_params(20),
        cost_estimate=LIGHT,
        name="gate_project",
    )(me, side, *blocks, mask, mods, held(mine), held(theirs))


def pair_kernel(first_ref, second_ref, third_ref, fourth_ref, left_ref, right_ref):
    left_ref[...] = (first_ref[...].astype(f32) + second_ref[...].astype(f32)).astype(bf16)
    right_ref[...] = (third_ref[...].astype(f32) + fourth_ref[...].astype(f32)).astype(bf16)


def pair_call(first, second, third, fourth, blocks):
    rows, cols = first.shape
    block = pl.BlockSpec((rows // blocks, cols), lambda i: (i, 0))
    return pl.pallas_call(
        pair_kernel,
        grid=(blocks,),
        in_specs=[block] * 4,
        out_specs=[block] * 2,
        out_shape=[shaped((rows, cols), bf16)] * 2,
        compiler_params=kernel_params(10),
        cost_estimate=LIGHT,
        name="pair_sums",
    )(held(first), held(second), held(third), held(fourth))


def join_kernel(keep_ref, there_ref, out_ref):
    out_ref[...] = (keep_ref[...].astype(f32) + there_ref[...].astype(f32)).astype(bf16)


def join_call(keep, there):
    return pl.pallas_call(
        join_kernel,
        out_shape=shaped(keep.shape, bf16),
        compiler_params=kernel_params(8),
        cost_estimate=LIGHT,
        name="join_sums",
    )(keep, there)


def pack_kernel(side_ref, conv_ref, scan_ref, keep_ref, send_ref, total):
    count = conv_ref.shape[0]
    rows = keep_ref.shape[0]
    total[0:count, :] = conv_ref[...]
    total[count:, :] = scan_ref[...]
    side = side_ref[0]
    keep_ref[...] = total[pl.ds(pl.multiple_of(side * rows, rows), rows), :]
    send_ref[...] = total[pl.ds(pl.multiple_of((1 - side) * rows, rows), rows), :].astype(bf16)


def pack_call(side, conv, scan):
    cols = conv.shape[1]
    rows = (conv.shape[0] + scan.shape[0]) // 2
    return pl.pallas_call(
        pack_kernel,
        in_specs=[scalars(), whole(*conv.shape), whole(*scan.shape)],
        out_specs=[whole(rows, cols)] * 2,
        grid=(1,),
        out_shape=[shaped((rows, cols), f32), shaped((rows, cols), bf16)],
        scratch_shapes=[pltpu.VMEM((2 * rows, cols), f32)],
        compiler_params=kernel_params(14),
        cost_estimate=LIGHT,
        name="pack_sums",
    )(side, conv, scan)


def unpack_kernel(
    spots, side_ref, keep_ref, there_ref, xproj_ref, taps_ref, dtproj_ref, rates_ref, vec_ref, total
):
    rows = keep_ref.shape[0]
    cols, tap_count, base, rank, states = spots
    side = side_ref[0]
    total[pl.ds(pl.multiple_of(side * rows, rows), rows), :] = keep_ref[...].astype(f32)
    total[pl.ds(pl.multiple_of((1 - side) * rows, rows), rows), :] = there_ref[...].astype(f32)
    dtproj_ref[...] = total[base : base + rank, :]
    taps_ref[...] = total[cols : cols + tap_count, :]
    first = base + rank
    rates_ref[...] = total[first : first + states, :]
    vec_ref[...] = jnp.zeros_like(vec_ref)
    vec_ref[0:1, :] = total[cols + tap_count : cols + tap_count + 1, :]
    vec_ref[1:3, :] = total[first + states : first + states + 2, :]
    for at in range(0, total.shape[1], 128):
        here = slice(at, at + 128)
        xproj_ref[here, :] = jnp.transpose(total[0:cols, here])


def unpack_call(side, keep, there, cols, tap_count, base, rank, states):
    rows, channels = keep.shape
    shapes = [(channels, cols), (tap_count, channels), (rank, channels), (states, channels)]
    shapes += [(8, channels)]
    return pl.pallas_call(
        functools.partial(unpack_kernel, (cols, tap_count, base, rank, states)),
        grid=(1,),
        in_specs=[scalars(), whole(rows, channels), whole(rows, channels)],
        out_specs=[whole(*shape) for shape in shapes],
        out_shape=[shaped(shape, f32) for shape in shapes],
        scratch_shapes=[pltpu.VMEM((2 * rows, channels), f32)],
        compiler_params=kernel_params(16),
        cost_estimate=LIGHT,
        name="unpack_sums",
    )(side, keep, there)


def fold_kernel(rows, me_ref, *refs):
    mine_ref, sent_ref = refs[-2:]
    count = len(refs) // 2 - 1
    items = refs[0].shape[0] // rows // 2
    chip = me_ref[0] >> 1
    for at in range(count):
        keep_ref, there_ref = refs[at], refs[count + at]
        for item in range(items):
            for which, out_ref in ((chip, mine_ref), (1 - chip, sent_ref)):
                here = pl.ds(pl.multiple_of((2 * item + which) * rows, rows), rows)
                total = keep_ref[here, :] + there_ref[here, :].astype(f32)
                out_ref[at * items + item] = total.astype(out_ref.dtype)


def fold_call(me, keeps, theres, rows):
    count, model = keeps[0].shape
    slots = len(keeps) * count // rows // 2
    return pl.pallas_call(
        functools.partial(fold_kernel, rows),
        grid=(1,),
        in_specs=[scalars()] + [whole(count, model)] * (2 * len(keeps)),
        out_specs=[whole(slots, rows, model)] * 2,
        out_shape=[shaped((slots, rows, model), f32), shaped((slots, rows, model), bf16)],
        compiler_params=kernel_params(14),
        cost_estimate=LIGHT,
        name="fold_rows",
    )(me, *keeps, *theres)


def rows_kernel(
    tokens_ref, cot_ref, mask_ref, mod_ref, branch_ref, branch_far_ref, norm_ref, norm_far_ref,
    mixed_ref, grad_ref, mod_grad_ref
):
    raw = tokens_ref[...].astype(f32)
    mask = mask_ref[...]
    gate = mod_ref[2:3, :]
    branch = branch_ref[...] + branch_far_ref[...].astype(f32)
    mixed_ref[...] = mask * (raw + gate * branch)
    res_grad = mask * cot_ref[...].astype(f32)
    centred = raw - jnp.mean(raw, axis=1, keepdims=True)
    spread = jnp.mean(centred * centred, axis=1, keepdims=True)
    inverse = lax.rsqrt(spread + EPSILON)
    hat = centred * inverse
    normed_grad = mask * (norm_ref[...] + norm_far_ref[...].astype(f32))
    q = normed_grad * (1.0 + mod_ref[1:2, :])
    grad_ref[...] = res_grad + inverse * (
        q - jnp.mean(q, axis=1, keepdims=True) - hat * jnp.mean(q * hat, axis=1, keepdims=True)
    )
    mod_grad_ref[0:1, :] = jnp.sum(normed_grad, axis=0, keepdims=True)
    mod_grad_ref[1:2, :] = jnp.sum(normed_grad * hat, axis=0, keepdims=True)
    mod_grad_ref[2:3, :] = jnp.sum(res_grad * branch, axis=0, keepdims=True)


def rows_call(tokens, cot, mask, mods, branch, branch_far, norm, norm_far):
    slots, rows, model = tokens.shape
    row = pl.BlockSpec((None, rows, model), lambda i: (i, 0, 0))
    mod = pl.BlockSpec((None, 3, model), lambda i: (i, 0, 0))
    return pl.pallas_call(
        rows_kernel,
        grid=(slots,),
        in_specs=[row, row, pl.BlockSpec((None, rows, 1), lambda i: (i, 0, 0)), mod, row, row, row, row],
        out_specs=[row, row, mod],
        out_shape=[
            shaped((slots, rows, model), f32),
            shaped((slots, rows, model), f32),
            shaped((slots, 3, model), f32),
        ],
        compiler_params=kernel_params(14),
        cost_estimate=LIGHT,
        name="owned_rows",
    )(tokens, cot, mask, mods, branch, branch_far, norm, norm_far)


def pick_rows(values_ref, parity, chips, rows):
    blocks = []
    for at in range(values_ref.shape[0] // rows // 2):
        start = pl.multiple_of((2 * at + parity) * rows, rows)
        blocks.append(values_ref[pl.ds(start, rows), :])
    return jnp.concatenate(blocks, 0)


def branch_kernel(rows, flip_ref, values_ref, weight_ref, keep_ref, send_ref):
    core = flip_ref[0]
    keep_ref[...] = matmul(pick_rows(values_ref, core, 2, rows), weight_ref[...])
    send_ref[...] = matmul(pick_rows(values_ref, 1 - core, 2, rows), weight_ref[...]).astype(bf16)


def branch_call(flip, values, weight, rows, width):
    count, depth = values.shape
    model = weight.shape[1]
    out = [shaped((count // 2, model), f32), shaped((count // 2, model), bf16)]
    return pl.pallas_call(
        functools.partial(branch_kernel, rows),
        grid=(model // width,),
        in_specs=[
            pl.BlockSpec(memory_space=pltpu.SMEM),
            pl.BlockSpec((count, depth), lambda j: (0, 0)),
            pl.BlockSpec((depth, width), lambda j: (0, j)),
        ],
        out_specs=[pl.BlockSpec((count // 2, width), lambda j: (0, j))] * 2,
        out_shape=out,
        compiler_params=kernel_params(10),
        cost_estimate=pl.CostEstimate(flops=1000, bytes_accessed=1000, transcendentals=0),
        name="branch_rows",
    )(flip, values, weight)


def proj_back_kernel(rows, slots, flip_ref, *refs):
    x_refs = refs[:slots]
    z_ref, weight_ref, there_ref, keep_ref, send_ref, x_s, z_s, mine_s = refs[slots:]
    core = flip_ref[0]
    half = there_ref.shape[1]
    length = x_refs[0].shape[0]

    def place(x_to, z_to, mine):
        for slot in range(slots):
            x_to[slot * length : (slot + 1) * length, :] = x_refs[slot][...]
        z_to[...] = z_ref[...]
        mine_s[...] = mine

    pl.when(core == 0)(lambda: place(x_s, z_s, weight_ref[:, :half]))
    pl.when(core == 1)(lambda: place(z_s, x_s, weight_ref[:, half:]))
    for parity, out_ref in ((core, keep_ref), (1 - core, send_ref)):
        total = contract_cols(pick_rows(x_s, parity, 2, rows), mine_s[...]) + contract_cols(
            pick_rows(z_s, parity, 2, rows), there_ref[...]
        )
        out_ref[...] = total.astype(out_ref.dtype)


def proj_back_call(flip, xs, z, weight, there, rows, width):
    length, depth = xs[0].shape
    count = z.shape[0]
    model = there.shape[0]
    return pl.pallas_call(
        functools.partial(proj_back_kernel, rows, len(xs)),
        grid=(model // width,),
        in_specs=[scalars()]
        + [whole(length, depth)] * len(xs)
        + [
            whole(count, depth),
            pl.BlockSpec((width, 2 * depth), lambda j: (j, 0)),
            pl.BlockSpec((width, depth), lambda j: (j, 0)),
        ],
        out_specs=[pl.BlockSpec((count // 2, width), lambda j: (0, j))] * 2,
        out_shape=[shaped((count // 2, model), f32), shaped((count // 2, model), bf16)],
        scratch_shapes=[pltpu.VMEM((count, depth), bf16)] * 2 + [pltpu.VMEM((width, depth), bf16)],
        compiler_params=kernel_params(18),
        cost_estimate=LIGHT,
        name="proj_back",
    )(flip, *xs, z, held(weight), held(there))


def cond_kernel(mod_ref, weight_ref, cond_ref, out_ref):
    value = cond_ref[...].astype(f32)
    sig = jax.nn.sigmoid(value)
    out_ref[...] = contract_cols(mod_ref[...], weight_ref[...]) * sig * (1.0 + value * (1.0 - sig))


def cond_call(mods, weight, cond, start, count):
    slots, columns = mods.shape
    width = 256 if count % 256 == 0 else 128
    first = start // width
    return pl.pallas_call(
        cond_kernel,
        grid=(count // width,),
        in_specs=[
            whole(slots, columns),
            pl.BlockSpec((width, columns), lambda j: (first + j, 0)),
            pl.BlockSpec((slots, width), lambda j: (0, first + j)),
        ],
        out_specs=pl.BlockSpec((slots, width), lambda j: (0, j)),
        out_shape=shaped((slots, count), f32),
        compiler_params=kernel_params(14),
        cost_estimate=LIGHT,
        name="cond_rows",
    )(mods, held(weight), cond)


def tap_sum(pad, taps_ref, here, sign, length):
    taps = taps_ref.shape[0] - 1
    total = pad[MARGIN : MARGIN + length, :] * taps_ref[taps - 1 : taps, here]
    for by in range(1, taps):
        start = MARGIN - sign * by
        total = total + pad[start : start + length, :] * taps_ref[taps - 1 - by : taps - by, here]
    return total


def conv_kernel(
    flip_ref, own_ref, other_ref, mask_ref, taps_ref, xproj_ref, x_ref, z_ref, u_ref, slope_ref,
    dbl_ref, pads
):
    step = pl.program_id(1)
    length, width = own_ref.shape
    taps = taps_ref.shape[0] - 1
    flip = flip_ref[0]

    def run(flipped):
        x_from, z_from = (other_ref, own_ref) if flipped else (own_ref, other_ref)
        x_ref[...] = x_from[...]
        z_ref[...] = z_from[...]
        mask = jnp.broadcast_to(mask_ref[...], (length, 128))
        for tile in range(width // 128):
            here = slice(tile * 128, (tile + 1) * 128)
            pad = pads.at[tile]
            pad[0:MARGIN, :] = jnp.zeros((MARGIN, 128), f32)
            pad[MARGIN + length :, :] = jnp.zeros((MARGIN, 128), f32)
            pad[MARGIN : MARGIN + length, :] = x_from[:, here].astype(f32)
            conv = taps_ref[taps : taps + 1, here] + tap_sum(pad, taps_ref, here, -1 if flipped else 1, length)
            sig = 0.5 + 0.5 * jnp.tanh(0.5 * conv)
            u_ref[:, here] = (mask * (conv * sig)).astype(bf16)
            slope_ref[:, here] = mask * (sig * (1.0 + conv * (1.0 - sig)))

    pl.when(flip == 0)(lambda: run(False))
    pl.when(flip == 1)(lambda: run(True))
    part = matmul(u_ref[...], xproj_ref[...])

    @pl.when(step == 0)
    def _():
        dbl_ref[...] = part

    @pl.when(step > 0)
    def _():
        dbl_ref[...] += part


def conv_back_kernel(
    flip_ref, x_ref, u_ref, slope_ref, taps_ref, xproj_ref, us_ref, dg_ref, prev_ref, keep_ref,
    send_ref, packed_ref, grad_s, pads, grad_pads
):
    length, width = x_ref.shape
    flip = flip_ref[0]
    taps = taps_ref.shape[0] - 1
    dg = dg_ref[...]
    cols = dg.shape[1]
    grad_s[...] = (us_ref[...] + contract_cols(dg, xproj_ref[...])) * slope_ref[...]
    packed_ref[0:cols, :] = prev_ref[0:cols, :] + matmul(
        jnp.transpose(dg.astype(f32)).astype(bf16), u_ref[...]
    )
    rest = packed_ref.shape[0] - cols - taps - 1
    packed_ref[cols + taps + 1 :, :] = jnp.zeros((rest, width), f32)

    def run(flipped, out_ref):
        sign = -1 if flipped else 1
        for tile in range(width // 128):
            here = slice(tile * 128, (tile + 1) * 128)
            pad, grad_pad = pads.at[tile], grad_pads.at[tile]
            for ref in (pad, grad_pad):
                ref[0:MARGIN, :] = jnp.zeros((MARGIN, 128), f32)
                ref[MARGIN + length :, :] = jnp.zeros((MARGIN, 128), f32)
            conv_grad = grad_s[:, here]
            pad[MARGIN : MARGIN + length, :] = x_ref[:, here].astype(f32)
            grad_pad[MARGIN : MARGIN + length, :] = conv_grad
            for by in range(taps):
                start = MARGIN - sign * by
                row = cols + taps - 1 - by
                packed_ref[row : row + 1, here] = prev_ref[row : row + 1, here] + jnp.sum(
                    conv_grad * pad[start : start + length, :], axis=0, keepdims=True
                )
            row = cols + taps
            packed_ref[row : row + 1, here] = prev_ref[row : row + 1, here] + jnp.sum(
                conv_grad, axis=0, keepdims=True
            )
            out_ref[:, here] = tap_sum(grad_pad, taps_ref, here, -sign, length).astype(bf16)

    for flipped in (False, True):
        for block in range(2):
            out_ref = keep_ref if block == int(flipped) else send_ref
            pl.when((flip == int(flipped)) & (pl.program_id(0) == block))(
                functools.partial(run, flipped, out_ref)
            )


def conv_call(flip, own, other, mask, taps, xproj, width):
    slots, length = mask.shape[:2]
    channels = own.shape[1]
    cols = xproj.shape[1]
    block = pl.BlockSpec((length, width), lambda i, j: (i, j))
    return pl.pallas_call(
        conv_kernel,
        grid=(slots, channels // width),
        in_specs=[
            scalars(),
            block,
            block,
            pl.BlockSpec((None, length, 1), lambda i, j: (i, 0, 0)),
            pl.BlockSpec((taps.shape[0], width), lambda i, j: (0, j)),
            pl.BlockSpec((width, cols), lambda i, j: (j, 0)),
        ],
        out_specs=[block] * 4 + [pl.BlockSpec((length, cols), lambda i, j: (i, 0))],
        out_shape=[outer((slots * length, channels), bf16)] * 3
        + [outer((slots * length, channels), f32), shaped((slots * length, cols), f32)],
        scratch_shapes=[pltpu.VMEM((width // 128, length + 2 * MARGIN, 128), f32)],
        compiler_params=kernel_params(16),
        cost_estimate=LIGHT,
        name="conv_forward",
    )(flip, own, other, mask, taps, xproj)


def conv_back_call(flip, slot, length, x, u, slope, taps, xproj, us, dg, prev):
    channels = x.shape[1]
    cols = xproj.shape[1]
    width = channels // 2
    rows = prev.shape[0]
    item = pl.BlockSpec((length, width), lambda j: (slot, j))
    pads = pltpu.VMEM((width // 128, length + 2 * MARGIN, 128), f32)
    return pl.pallas_call(
        conv_back_kernel,
        grid=(2,),
        in_specs=[
            scalars(),
            item,
            item,
            item,
            pl.BlockSpec((taps.shape[0], width), lambda j: (0, j)),
            pl.BlockSpec((width, cols), lambda j: (j, 0)),
            pl.BlockSpec((length, width), lambda j: (0, j)),
            whole(length, cols),
            pl.BlockSpec((rows, width), lambda j: (0, j)),
        ],
        out_specs=[
            whole(length, width),
            whole(length, width),
            pl.BlockSpec((rows, width), lambda j: (0, j)),
        ],
        out_shape=[
            shaped((length, width), bf16),
            shaped((length, width), bf16),
            shaped((rows, channels), f32),
        ],
        scratch_shapes=[pltpu.VMEM((length, width), f32), pads, pads],
        compiler_params=kernel_params(18),
        cost_estimate=LIGHT,
        name="conv_backward",
    )(flip, held(x), held(u), held(slope), taps, xproj, held(us), dg, prev)


def spread(dbl_ref, first, b_wide, c_wide, rows_s, states):
    length, cols = dbl_ref.shape
    rest = dbl_ref[...]
    row = lax.broadcasted_iota(jnp.int32, (cols, cols), 0)
    col = lax.broadcasted_iota(jnp.int32, (cols, cols), 1)
    rows = jnp.zeros((length, cols), f32)
    for part in range(3):
        piece = rest.astype(bf16)
        rest = rest - piece.astype(f32)
        pick = ((row == first + col % (2*states)) & (col // (2*states) == part))
        rows = rows + matmul(piece, jnp.where(pick, 1.0, 0.0).astype(bf16))
    rows_s[...] = rows
    which = lax.broadcasted_iota(jnp.int32, (states, cols), 0)
    lane = lax.broadcasted_iota(jnp.int32, (states, cols), 1)
    mine = jnp.where(lane % states == which, 1.0, 0.0)
    row = lax.broadcasted_iota(jnp.int32, (cols, 2*cols), 0)
    col = lax.broadcasted_iota(jnp.int32, (cols, 2*cols), 1)
    wide = jnp.where((row % (2*states)) // states == col // cols, 1.0, 0.0).astype(bf16)
    def some(at, _):
        left = [(mine*jnp.broadcast_to(rows_s[pl.ds(at*CHUNK+t, 1), :], (states, cols))).astype(bf16) for t in range(CHUNK)]
        got = matmul(jnp.concatenate(left, 0), wide)
        here = pl.ds(pl.multiple_of(at*CHUNK*states, CHUNK*states), CHUNK*states)
        b_wide[here, :] = got[:, :cols]
        c_wide[here, :] = got[:, cols:]
        return 0
    lax.fori_loop(0, length//CHUNK, some, 0, unroll=4)

def tiles_of(values):
    return [values[:, at:at+128] for at in range(0, values.shape[1], 128)]

def fold(values, tmp, tt, states):
    for at, tile in enumerate(tiles_of(values)):
        total = tile[:8]
        for part in range(1, states//8):
            total = total + tile[part*8:(part+1)*8]
        tmp[at, pl.ds(tt//8*64 + tt%8, 8, stride=8), :] = total

def add_tiles(values):
    parts = tiles_of(values)
    total = parts[0]
    for part in parts[1:]:
        total = total + part
    return total

def unfold(tmp, out, base):
    for at in range(out.shape[1]//128):
        for part in range(CHUNK//8):
            acc = tmp[at, part*64:part*64+8, :]
            for row in range(1, 8):
                acc = acc + tmp[at, part*64+row*8:part*64+row*8+8, :]
            out[pl.ds(pl.multiple_of(base+part*8, 8), 8), at*128:(at+1)*128] = acc

def collect(acc, tmp, out, length, states):
    which = lax.broadcasted_iota(jnp.int32, (states, 128), 0)
    lane = lax.broadcasted_iota(jnp.int32, (states, 128), 1)
    mine = which == lane
    def some(at, _):
        base = pl.multiple_of(at*CHUNK, CHUNK)
        for tt in range(CHUNK):
            sums = jnp.sum(acc[pl.ds((base+tt)*states, states), :], axis=1, keepdims=True)
            fold(jnp.where(mine, sums, 0.0), tmp, tt, states)
        unfold(tmp, out, base)
        return 0
    lax.fori_loop(0, length//CHUNK, some, 0, unroll=4)

def fwd_kernel(states, flip_ref, dbl_ref, dtp_ref, vec_ref, rate2_ref, u_ref, z_ref, gg_ref,
               gate_keep, gate_send, z_keep, z_send, delta_ref, yg_ref, prior_ref, cout_ref,
               b_wide, c_wide, drive_s, y_s, y_tmp, c_acc, rows_s):
    step = pl.program_id(1)
    length, width = u_ref.shape
    rank = dtp_ref.shape[0]
    group = CHUNK*states
    chunks = length//CHUNK
    flip = flip_ref[0]
    @pl.when(step == 0)
    def _():
        spread(dbl_ref, rank, b_wide, c_wide, rows_s, states)
        c_acc[...] = jnp.zeros_like(c_acc)
    low = dbl_ref[:, :rank].astype(bf16)
    pre = matmul(low, dtp_ref[...]) + vec_ref[0:1, :]
    delta = jnp.maximum(pre, 0.0) + jnp.log1p(jnp.exp(-jnp.abs(pre)))
    delta_ref[...] = delta
    drive_s[...] = delta * u_ref[...].astype(f32)
    z = z_ref[...].astype(f32)
    yg_ref[...] = gg_ref[...].astype(f32) * (z * (0.5 + 0.5*jnp.tanh(0.5*z)))
    def run(flipped):
        def ahead(chunk, state):
            place = chunks-1-chunk if flipped else chunk
            base = pl.multiple_of(place*CHUNK, CHUNK)
            wide = pl.multiple_of(place*group, group)
            for at in range(CHUNK):
                tt = CHUNK-1-at if flipped else at
                t = base + tt
                here = pl.ds(wide + tt*states, states)
                d = jnp.broadcast_to(delta_ref[pl.ds(t,1),:], (states,width))
                x = jnp.broadcast_to(drive_s[pl.ds(t,1),:], (states,width))
                g = jnp.broadcast_to(yg_ref[pl.ds(t,1),:], (states,width))
                b = jnp.concatenate([b_wide[here,:]]*(width//128), axis=1)
                c = jnp.concatenate([c_wide[here,:]]*(width//128), axis=1)
                prior = jnp.exp2(d*rate2_ref[...])*state
                state = prior + x*b
                prior_ref[here,:] = prior.astype(bf16)
                fold(state*c, y_tmp, tt, states)
                c_acc[here,:] += add_tiles(state*g)
            unfold(y_tmp, y_s, base)
            return state
        lax.fori_loop(0, chunks, ahead, jnp.zeros((states,width), f32))
    pl.when(flip == 0)(lambda: run(False))
    pl.when(flip == 1)(lambda: run(True))
    u = u_ref[...].astype(f32)
    z = z_ref[...].astype(f32)
    sig = (0.5 + 0.5*jnp.tanh(0.5*z))
    y = y_s[...] + vec_ref[1:2,:]*u
    gated = (y*(z*sig)).astype(bf16)
    zg = (gg_ref[...].astype(f32)*y*(sig*(1.0+z*(1.0-sig)))).astype(bf16)
    half = gate_keep.shape[1]
    for at in range(2*half//width):
        for core in range(2):
            def put(at=at, core=core):
                for side in range(2):
                    low, high = max(at*width, side*half), min((at+1)*width, (side+1)*half)
                    if low < high:
                        to = slice(low-side*half, high-side*half)
                        of = slice(low-at*width, high-at*width)
                        (gate_keep if side == core else gate_send)[:, to] = gated[:, of]
                        (z_keep if side == core else z_send)[:, to] = zg[:, of]
            pl.when((step == at) & (flip == core))(put)
    @pl.when(step == pl.num_programs(1)-1)
    def _():
        collect(c_acc, y_tmp, rows_s, length, states)
        cout_ref[...] = rows_s[:, :states]

def bwd_kernel(states, flip_ref, dbl_ref, dtp_ref, vec_ref, rate2_ref, u_ref, delta_ref, yg_ref, prior_ref, cout_ref, prev_ref,
               us_ref, part_ref, packed_ref,
               b_wide, c_wide, drive_s, r_s, w_s, low_t, rank_s, r_tmp, w_tmp, b_acc, rows_s):
    step = pl.program_id(0)
    length, width = u_ref.shape
    rank = dtp_ref.shape[0]
    group = CHUNK*states
    chunks = length//CHUNK
    flip = flip_ref[0]
    @pl.when(step == 0)
    def _():
        low_t[...] = jnp.transpose(dbl_ref[...])[:rank,:].astype(bf16)
        spread(dbl_ref, rank, b_wide, c_wide, rows_s, states)
        b_acc[...] = jnp.zeros_like(b_acc)
        rank_s[...] = jnp.zeros_like(rank_s)
    u = u_ref[...].astype(f32)
    drive_s[...] = delta_ref[...]*u
    def run(flipped):
        def back(chunk, carry):
            carried, total = carry
            place = chunk if flipped else chunks-1-chunk
            base = pl.multiple_of(place*CHUNK, CHUNK)
            wide = pl.multiple_of(place*group, group)
            for at in range(CHUNK):
                tt = at if flipped else CHUNK-1-at
                t = base + tt
                here = pl.ds(wide + tt*states, states)
                d = jnp.broadcast_to(delta_ref[pl.ds(t,1),:], (states,width))
                x = jnp.broadcast_to(yg_ref[pl.ds(t,1),:], (states,width))
                e = jnp.broadcast_to(drive_s[pl.ds(t,1),:], (states,width))
                b = jnp.concatenate([b_wide[here,:]]*(width//128), axis=1)
                c = jnp.concatenate([c_wide[here,:]]*(width//128), axis=1)
                power = d*rate2_ref[...]
                adj = carried + x*c
                moved = (adj*prior_ref[here,:].astype(f32))*power
                total = total + moved
                fold(moved, w_tmp, tt, states)
                fold(adj*b, r_tmp, tt, states)
                b_acc[here,:] += add_tiles(adj*e)
                carried = jnp.exp2(power)*adj
            unfold(w_tmp, w_s, base)
            unfold(r_tmp, r_s, base)
            return carried, total
        zero = jnp.zeros((states,width), f32)
        _, total = lax.fori_loop(0, chunks, back, (zero, zero))
        packed_ref[rank:rank+states,:] = prev_ref[rank:rank+states,:] + total*(1.0/LOG2E)
    pl.when(flip == 0)(lambda: run(False))
    pl.when(flip == 1)(lambda: run(True))
    yg = yg_ref[...]
    r = r_s[...]
    delta = delta_ref[...]
    us_ref[...] = delta*r + vec_ref[1:2,:]*yg
    low = dbl_ref[:, :rank].astype(bf16)
    pre = matmul(low, dtp_ref[...]) + vec_ref[0:1,:]
    sig = jnp.exp(pre-delta)
    ratio = jnp.where(delta > 1e-30, sig/jnp.maximum(delta, 1e-30), 1.0)
    pre_grad = w_s[...]*(1.0/LOG2E)*ratio + u*r*sig
    pre_low = pre_grad.astype(bf16)
    rank_s[...] += contract_cols(pre_low, dtp_ref[...])
    packed_ref[0:rank,:] = prev_ref[0:rank,:] + matmul(low_t[...], pre_low)
    packed_ref[rank+states:rank+states+1,:] = prev_ref[rank+states:rank+states+1,:] + jnp.sum(pre_grad, axis=0, keepdims=True)
    packed_ref[rank+states+1:rank+states+2,:] = prev_ref[rank+states+1:rank+states+2,:] + jnp.sum(yg*u, axis=0, keepdims=True)
    rest = packed_ref.shape[0]-rank-states-2
    packed_ref[rank+states+2:,:] = jnp.zeros((rest,width), f32)
    @pl.when(step == pl.num_programs(0)-1)
    def _():
        collect(b_acc, r_tmp, rows_s, length, states)
        part_ref[...] = jnp.concatenate([rank_s[...], rows_s[:, :states], cout_ref[...]], axis=1)


def forward_call(flip, dbl, dtproj, vec, rates2, u, z, gg, slots, width):
    count, channels = u.shape
    length = count // slots
    half = channels // 2
    states, rank, cols = rates2.shape[0], dtproj.shape[0], dbl.shape[1]
    weight = lambda rows: pl.BlockSpec((rows, width), lambda i, j: (0, j))
    block = lambda rows: pl.BlockSpec((rows, width), lambda i, j: (i, j))
    item = lambda wide: pl.BlockSpec((length, wide), lambda i, j: (i, 0))
    return pl.pallas_call(
        functools.partial(fwd_kernel, states),
        grid=(slots, channels // width),
        in_specs=[scalars(), item(cols), weight(rank), weight(2), weight(states)] + [block(length)] * 3,
        out_specs=[item(half)] * 4 + [block(length)] * 2 + [block(length * states), item(states)],
        out_shape=[outer((count, half), bf16)] * 4
        + [outer((count, channels), f32)] * 2
        + [outer((count * states, channels), bf16), shaped((count, states), f32)],
        scratch_shapes=[
            pltpu.VMEM((length * states, 128), f32),
            pltpu.VMEM((length * states, 128), f32),
            pltpu.VMEM((length, width), f32),
            pltpu.VMEM((length, width), f32),
            pltpu.VMEM((width // 128, CHUNK * 8, 128), f32),
            pltpu.VMEM((length * states, 128), f32),
            pltpu.VMEM((length, cols), f32),
        ],
        compiler_params=kernel_params(40),
        cost_estimate=pl.CostEstimate(
            flops=32000000000, bytes_accessed=40000000, transcendentals=14000000
        ),
        name="scan_forward",
    )(flip, dbl, dtproj, vec, rates2, held(u), held(z), held(gg))


def backward_call(flip, slot, slots, dbl, dtproj, vec, rates2, u, delta, yg, prior, cout, prev, width):
    count, channels = u.shape
    length = count // slots
    states, rank, cols = rates2.shape[0], dtproj.shape[0], dbl.shape[1]
    rows = prev.shape[0]
    weight = lambda rows: pl.BlockSpec((rows, width), lambda j: (0, j))
    block = lambda rows: pl.BlockSpec((rows, width), lambda j: (slot, j))
    item = lambda wide: pl.BlockSpec((length, wide), lambda j: (slot, 0))
    return pl.pallas_call(
        functools.partial(bwd_kernel, states),
        grid=(channels // width,),
        in_specs=[scalars(), item(cols), weight(rank), weight(2), weight(states)]
        + [block(length)] * 3
        + [block(length * states), item(states), weight(rows)],
        out_specs=[weight(length), whole(length, cols), weight(rows)],
        out_shape=[
            outer((length, channels), f32),
            shaped((length, cols), f32),
            shaped((rows, channels), f32),
        ],
        scratch_shapes=[
            pltpu.VMEM((length * states, 128), f32),
            pltpu.VMEM((length * states, 128), f32),
            pltpu.VMEM((length, width), f32),
            pltpu.VMEM((length, width), f32),
            pltpu.VMEM((length, width), f32),
            pltpu.VMEM((rank, length), bf16),
            pltpu.VMEM((length, rank), f32),
            pltpu.VMEM((width // 128, CHUNK * 8, 128), f32),
            pltpu.VMEM((width // 128, CHUNK * 8, 128), f32),
            pltpu.VMEM((length * states, 128), f32),
            pltpu.VMEM((length, cols), f32),
        ],
        compiler_params=kernel_params(40),
        cost_estimate=pl.CostEstimate(
            flops=22000000000, bytes_accessed=20000000, transcendentals=7000000
        ),
        name="scan_backward",
    )(flip, dbl, dtproj, vec, rates2, held(u), held(delta), held(yg), held(prior), cout, prev)


def local(
    tokens,
    cond,
    counts,
    valid,
    ada_weight,
    ada_bias,
    in_weight,
    conv_weight,
    conv_bias,
    xproj_weight,
    dtproj_weight,
    dt_bias,
    a_log,
    skip_gain,
    out_weight,
    cotangent,
):
    slot_count, shard_rows, model = tokens.shape
    dirs = lax.axis_size("dir")
    dps = lax.axis_size("dp")
    me = lax.axis_index("dir")
    dp_index = lax.axis_index("dp")
    core = me & 1
    half = in_weight.shape[1] // 2
    rank = dtproj_weight.shape[0]
    states = a_log.shape[1]
    tap_count = conv_weight.shape[1]
    cols = xproj_weight.shape[1]
    slots = range(slot_count)
    width = 512 if dt_bias.shape[0] % 512 == 0 else 128
    first, second = bit_orders("dp")
    z_bit, out_bit = first[0], second[0]
    scalar = lambda value: value.astype(jnp.int32).reshape(1)
    flip, me_ref = scalar(core), scalar(me)
    z_side, out_side = scalar((dp_index >> z_bit) & 1), scalar((dp_index >> out_bit) & 1)

    live_slots = (jnp.arange(slot_count) < counts[0]).astype(f32)
    full_mask = valid.astype(f32) * live_slots[:, None]
    mask_cols = full_mask[:, :, None]
    local_mask = lax.dynamic_slice_in_dim(full_mask, me * shard_rows, shard_rows, 1)[:, :, None]

    def gather_rows(block, *earlier):
        over = after(swap(block, "dir", 1), *earlier)
        return block, over, swap(block, "dir", 0), swap(over, "dir", 0)

    cond_act = jax.nn.silu(cond.astype(f32)).astype(bf16)
    modulation = matmul(cond_act, ada_weight) + ada_bias.astype(f32)[None, :]
    mods = modulation.reshape(slot_count, 3, model)
    token_blocks = gather_rows(tokens, modulation)
    out_there = swap(out_weight, "dir", 0)

    taps = jnp.concatenate(
        [jnp.transpose(conv_weight.astype(f32)), conv_bias.astype(f32)[None, :]], 0
    )
    vec = jnp.stack([dt_bias, skip_gain])
    rates2 = -jnp.exp(jnp.transpose(a_log)) * LOG2E

    left_mine, left_give, own = norm_call(
        me_ref,
        z_side,
        token_blocks,
        mask_cols,
        mods,
        in_weight,
        width,
        model // dps << z_bit,
    )
    in_send = lax.dynamic_slice_in_dim(after(in_weight, left_mine), (1 - core) * half, half, 1)
    in_there = swap(in_send, "dir", 0)
    other = after(swap(own, "dir", 0), in_send)
    x, z, u, slope, part = conv_call(flip, own, other, mask_cols, taps, xproj_weight, half)
    part_there = swap(part, "dir", 1)
    cot_blocks = gather_rows(cotangent, part)
    branch_mine, branch_give, gg = gate_call(
        me_ref,
        out_side,
        cot_blocks,
        mask_cols,
        after(mods, part),
        out_weight,
        out_there,
        model // dps << out_bit,
    )
    left_there = swap(left_give, "dp", z_bit)
    branch_there = swap(branch_give, "dp", out_bit)
    dbl = part + after(part_there, gg)
    gate_keep, gate_send, z_keep, z_send, *saved = forward_call(
        flip, dbl, dtproj_weight, vec, rates2, u, z, gg, slot_count, width
    )
    gate_send, z_send = after((gate_send, z_send), left_there, branch_there)
    gate_all, z_all = pair_call(
        gate_keep, swap(gate_send, "dir", 0), z_keep, swap(z_send, "dir", 0), slot_count
    )
    gate_there = swap(gate_all, "dp", out_bit)
    z_there = swap(z_all, "dp", z_bit)

    rows_keep, rows_give = branch_call(flip, gate_all, out_weight, shard_rows, width)
    rows_there = swap(rows_give, "dir", 0)

    rest = lambda out: [bit for bit in first if bit != out]
    scan_rows = -(-(rank + states + 2) // 8) * 8
    packed = jnp.zeros((scan_rows, dt_bias.shape[0]), f32)
    conv_rows = -(-(cols + tap_count + 1) // 8) * 8
    conv_packed = jnp.zeros((conv_rows, dt_bias.shape[0]), f32)
    length = mask_cols.shape[1]

    def back_conv(slot, us, dg, conv_packed):
        return conv_back_call(
            flip, slot, length, x, u, slope, taps, xproj_weight, us, dg, conv_packed
        )

    x_sums, x_theres = [], []
    u_tied = after(u, z_all, rows_give)
    for slot in slots:
        us, part_back, packed = backward_call(
            flip, slot, slot_count, dbl, dtproj_weight, vec, rates2, u_tied, *saved, packed, width
        )
        there = swap(part_back, "dir", 1)
        if slot == 0:
            z_part = Scatter(
                contract_rows(left_mine, after(z_all, part_back))
                + contract_rows(left_there, after(z_there, part_back)),
                "dp",
                rest(z_bit),
            )
            out_part = Scatter(
                contract_rows(branch_mine, after(gate_all, part_back))
                + contract_rows(branch_there, after(gate_there, part_back)),
                "dp",
                rest(out_bit),
            )
        if slot + 1 < slot_count:
            dg = (part_back + after(there, z_part.send, out_part.send)).astype(bf16)
            keep, send, conv_packed = back_conv(slot, us, dg, conv_packed)
            send_there = swap(send, "dir", 0)
            if slot == 0:
                rows_mine, branch_sent = fold_call(
                    me_ref, [rows_keep], [after(rows_there, send)], shard_rows
                )
                branch_far = swap(branch_sent, "dir", 1)
            x_sums.append(join_call(keep, after(send_there, branch_sent)))
            x_theres.append(swap(x_sums[-1], "dp", z_bit))
            u_tied, z_part.send, out_part.send = after((u, z_part.send, out_part.send), x_sums[-1])

    z_part.step(part_back, branch_far, *x_theres)
    out_part.step(part_back)
    dg = (part_back + after(there, z_part.send, out_part.send)).astype(bf16)
    keep, send, conv_packed = back_conv(slot_count - 1, us, dg, conv_packed)
    shared = SharedSum(pack_call(out_side, conv_packed, packed), "dp", second)
    send_there = swap(after(send, shared.send), "dir", 0)
    x_sums.append(join_call(keep, send_there))
    x_there = swap(x_sums[-1], "dp", z_bit)
    norm_keep, norm_give = proj_back_call(
        flip, x_sums, z_all, in_weight, in_there, shard_rows, width
    )
    z_part.step(norm_give)
    out_part.step(norm_give)
    shared.step(z_part.values, out_part.values)
    x_theres.append(after(x_there, shared.send))
    norm_there = swap(norm_give, "dir", 0)
    norm_mine, norm_sent = fold_call(
        me_ref, [norm_keep], [after(norm_there, x_theres[-1])], shard_rows
    )
    norm_far = swap(norm_sent, "dir", 1)
    x_part = contract_rows(left_mine, jnp.concatenate(after(x_sums, norm_sent), 0)) + contract_rows(
        left_there, jnp.concatenate(after(x_theres, norm_sent), 0)
    )
    x_part = Scatter(x_part, "dp", rest(z_bit))
    shared.step(x_part.send)

    mixed, token_grads, mod_part = rows_call(
        tokens,
        cotangent,
        local_mask,
        mods,
        rows_mine,
        branch_far,
        norm_mine,
        after(norm_far, shared.send),
    )
    mod_there = swap(mod_part, "dir", 0)
    shared.step(mod_part)
    x_part.step(shared.send)
    mod_pair = mod_part + after(mod_there, x_part.send)
    mod_far = swap(mod_pair, "dir", 1)
    shared.step(mod_pair)
    mod_total = mod_pair + after(mod_far, shared.send)
    mod_low = mod_total.astype(bf16).reshape(slot_count, 3 * model)
    half_model = model // 2
    cond_low = cond_call(mod_low, ada_weight, cond, 0, half_model)
    have = []
    sides = jnp.concatenate([mod_low, cond_act], 1)
    sides = gather_bit(sides, "dp", first[0], have, cond_low)
    while len(shared.plan) > 1:
        shared.step(sides)
    keep, there = shared.last(sides)
    cond_high = cond_call(after(mod_low, sides), ada_weight, cond, half_model, half_model)
    cond_grad = jnp.concatenate([cond_low, cond_high], 1)
    sides = gather_rest(sides, "dp", first[1:], cond_high)
    sides = sides.reshape(dps * slot_count, -1)
    total_columns = ada_weight.shape[1]
    columns = total_columns // dirs
    rows = ada_weight.shape[0] // dps
    mod_all = lax.dynamic_slice_in_dim(sides, me * columns, columns, 1)
    act_mine = lax.dynamic_slice_in_dim(sides, total_columns + dp_index * rows, rows, 1)
    ada_sum = contract_rows(act_mine, mod_all)
    portion = total_columns // dps
    bias_part = lax.dynamic_slice_in_dim(sides, dp_index * portion, portion, 1)
    bias_sum = jnp.sum(bias_part.astype(f32), axis=0)

    xproj_sum, kernel_sum, dtproj_sum, rate_sum, vec_sum = unpack_call(
        out_side, keep, there, cols, tap_count, conv_rows, rank, states
    )
    while x_part.order:
        x_part.step(xproj_sum)
    while z_part.order:
        z_part.step(xproj_sum)
    while out_part.order:
        out_part.step(xproj_sum)
    x_sum = x_part.values
    z_sum = z_part.values
    out_sum = jnp.transpose(out_part.values)
    keep_sum = jnp.where(core == 0, x_sum, z_sum)
    send_sum = jnp.where(core == 0, z_sum, x_sum)
    in_sum = ordered(core, keep_sum, swap(send_sum, "dir", 0), 1)

    return (
        mixed,
        token_grads,
        cond_grad,
        ada_sum,
        bias_sum,
        in_sum,
        jnp.transpose(kernel_sum),
        vec_sum[0],
        xproj_sum,
        dtproj_sum,
        vec_sum[1],
        jnp.transpose(rate_sum),
        vec_sum[2],
        out_sum,
    )


def solution(mesh):
    in_specs = (
        P("dp", "dir", None),
        P("dp", None),
        P("dp"),
        P("dp", None),
        P(),
        P(),
        P(None, "dir"),
        P("dir", None),
        P("dir"),
        P("dir", None),
        P(None, "dir"),
        P("dir"),
        P("dir", None),
        P("dir"),
        P("dir", None),
        P("dp", "dir", None),
    )
    out_specs = (
        P("dp", "dir", None),
        P("dp", "dir", None),
        P("dp", None),
        P("dp", "dir"),
        P("dp"),
        P("dp", "dir"),
        P("dir", None),
        P("dir"),
        P("dir", None),
        P(None, "dir"),
        P("dir"),
        P("dir", None),
        P("dir"),
        P("dir", "dp"),
    )
    return jax.shard_map(local, mesh=mesh, in_specs=in_specs, out_specs=out_specs, check_vma=False)
```

```python
import functools

import jax
import jax.numpy as jnp
from jax import lax
from jax.experimental import pallas as pl
from jax.experimental.pallas import tpu as pltpu
from jax.sharding import PartitionSpec as P

EPSILON = 1e-06
LOG2E = 1.4426950408889634
CHUNK = 16
MARGIN = 8

bf16 = jnp.bfloat16
f32 = jnp.float32


def swap(block, axis, bit):
    count = lax.axis_size(axis)
    return lax.ppermute(block, axis, [(at, at ^ (1 << bit)) for at in range(count)])


def contract_rows(left, right):
    return lax.dot_general(
        left, right, (((0,), (0,)), ((), ())), preferred_element_type=f32
    )


def contract_cols(left, right):
    return lax.dot_general(
        left, right, (((1,), (1,)), ((), ())), preferred_element_type=f32
    )


def matmul(left, right):
    return jnp.dot(left, right, preferred_element_type=f32)


def ordered(bit, own, other, axis):
    return jnp.where(
        bit == 0,
        jnp.concatenate([own, other], axis),
        jnp.concatenate([other, own], axis),
    )


def halves(values, bit, axis):
    size = values.shape[axis] // 2
    keep = lax.dynamic_slice_in_dim(values, bit * size, size, axis)
    send = lax.dynamic_slice_in_dim(values, (1 - bit) * size, size, axis)
    return keep, send


class Scatter:
    def __init__(self, values, axis, order):
        self.axis, self.order = axis, list(order)
        bits = len(order)
        self.values = values.reshape((2,) * bits + (values.shape[0] >> bits,) + values.shape[1:])
        self.left = sorted(order, reverse=True)
        self.split()

    def split(self):
        if not self.order:
            return
        at = self.left.index(self.order[0])
        mine = (lax.axis_index(self.axis) >> self.order[0]) & 1
        self.keep = lax.dynamic_index_in_dim(self.values, mine, at, keepdims=False)
        send = lax.dynamic_index_in_dim(self.values, 1 - mine, at, keepdims=False)
        self.send = send.astype(bf16)

    def step(self, *earlier):
        bit = self.order.pop(0)
        self.left.remove(bit)
        arrived = after(swap(self.send, self.axis, bit), *earlier)
        self.values = self.keep.astype(f32) + arrived.astype(f32)
        self.split()


class SharedSum:
    def __init__(self, values, axis, order):
        self.axis = axis
        few = list(order[:2])
        self.plan = [("halve", bit) for bit in few] + [("add", bit) for bit in order[2:]]
        self.plan += [("join", bit) for bit in few[::-1]]
        self.start(*values)

    def start(self, keep, send):
        self.keep, self.send = keep, send

    def begin(self):
        kind, bit = self.plan[0] if self.plan else ("", 0)
        self.mine = (lax.axis_index(self.axis) >> bit) & 1
        if kind == "halve":
            self.keep, self.send = halves(self.values, self.mine, 0)
            self.send = self.send.astype(bf16)
        else:
            self.keep = self.send = self.values.astype(bf16)

    def step(self, *earlier):
        kind, bit = self.plan.pop(0)
        arrived = after(swap(self.send, self.axis, bit), *earlier)
        if kind == "join":
            self.values = ordered(self.mine, self.keep, arrived, 0)
        else:
            self.values = self.keep.astype(f32) + arrived.astype(f32)
        self.begin()

    def last(self, *earlier):
        _, bit = self.plan.pop(0)
        return self.keep, after(swap(self.send, self.axis, bit), *earlier)


def after(values, *earlier):
    return lax.optimization_barrier((values, earlier))[0] if earlier else values


def gather_bit(values, axis, bit, have, *earlier):
    at = len([other for other in have if other > bit])
    mine = (lax.axis_index(axis) >> bit) & 1
    arrived = after(swap(values, axis, bit), *earlier)
    have.append(bit)
    return jnp.where(
        mine == 0, jnp.stack([values, arrived], at), jnp.stack([arrived, values], at)
    )


def gather_rest(values, axis, bits, *earlier):
    codes = [code << bits[0] for code in range(1 << len(bits))]
    got = [values] + [
        lax.ppermute(values, axis, [(at, at ^ code) for at in range(lax.axis_size(axis))])
        for code in codes[1:]
    ]
    got = after(got, *earlier)
    mine = lax.axis_index(axis) >> bits[0]
    stacked = jnp.stack(got)
    return jnp.take(stacked, jnp.arange(len(codes)) ^ mine, axis=0)


def bit_orders(axis):
    bits = lax.axis_size(axis).bit_length() - 1
    first = list(range(bits))
    second = list(range(bits))
    if bits > 1:
        second[0], second[1] = 1, 0
    return first, second


def kernel_params(megabytes):
    return pltpu.CompilerParams(vmem_limit_bytes=megabytes * 1024 * 1024)


LIGHT = pl.CostEstimate(flops=1000, bytes_accessed=1000, transcendentals=0)


def whole(*shape):
    return pl.BlockSpec(shape, lambda *at: (0,) * len(shape))


def scalars():
    return pl.BlockSpec(memory_space=pltpu.SMEM)


def shaped(shape, kind):
    return jax.ShapeDtypeStruct(shape, kind)


def outer(shape, kind):
    return pltpu.HBM(shape, kind)


def held(values):
    return pltpu.with_memory_space_constraint(values, pltpu.HBM)


def split_columns(values_ref, side_ref, chunk, keep_ref, give_ref):
    for side in range(2):

        @pl.when(side_ref[0] == side)
        def _():
            for at, start in enumerate(range(0, values_ref.shape[1], 2 * chunk)):
                to = slice(at * chunk, (at + 1) * chunk)
                first = values_ref[:, start : start + chunk]
                second = values_ref[:, start + chunk : start + 2 * chunk]
                keep_ref[:, to] = second if side else first
                give_ref[:, to] = first if side else second


def norm_kernel(
    chunk, me_ref, side_ref, own_ref, over_ref, beside_ref, far_ref, mask_ref, mod_ref, weight_ref,
    keep_ref, give_ref, proj_ref, normed_s
):
    slots, rows, _ = own_ref.shape
    length = mask_ref.shape[1]

    @pl.when(pl.program_id(0) == 0)
    def _():
        for slot in range(slots):
            shift = mod_ref[slot, 0:1, :]
            scale = mod_ref[slot, 1:2, :]
            for code, block in ((0, own_ref), (2, over_ref), (1, beside_ref), (3, far_ref)):
                start = pl.multiple_of((me_ref[0] ^ code) * rows, rows)
                raw = block[slot].astype(f32)
                centred = raw - jnp.mean(raw, axis=1, keepdims=True)
                spread = jnp.mean(centred * centred, axis=1, keepdims=True)
                hat = centred * lax.rsqrt(spread + EPSILON)
                mask = mask_ref[slot, pl.ds(start, rows), :]
                normed_s[pl.ds(slot * length + start, rows), :] = (
                    mask * (hat * (1.0 + scale) + shift)
                ).astype(bf16)
        split_columns(normed_s, side_ref, chunk, keep_ref, give_ref)

    proj_ref[...] = matmul(normed_s[...], weight_ref[...]).astype(bf16)


def norm_call(me, side, blocks, mask, mods, weight, width, chunk):
    slots, rows, model = blocks[0].shape
    count = slots * mask.shape[1]
    channels = weight.shape[1]
    return pl.pallas_call(
        functools.partial(norm_kernel, chunk),
        grid=(channels // width,),
        in_specs=[scalars(), scalars()]
        + [whole(slots, rows, model)] * 4
        + [whole(*mask.shape), whole(slots, 3, model), pl.BlockSpec((model, width), lambda j: (0, j))],
        out_specs=[
            whole(count, model // 2),
            whole(count, model // 2),
            pl.BlockSpec((count, width), lambda j: (0, j)),
        ],
        out_shape=[
            shaped((count, model // 2), bf16),
            shaped((count, model // 2), bf16),
            shaped((count, channels), bf16),
        ],
        scratch_shapes=[pltpu.VMEM((count, model), bf16)],
        compiler_params=kernel_params(20),
        cost_estimate=LIGHT,
        name="norm_project",
    )(me, side, *blocks, mask, mods, held(weight))


def gate_kernel(
    chunk, me_ref, side_ref, own_ref, over_ref, beside_ref, far_ref, mask_ref, mod_ref, mine_ref,
    theirs_ref, keep_ref, give_ref, out_ref, grad_s
):
    slots, rows, _ = own_ref.shape
    length = mask_ref.shape[1]
    step = pl.program_id(0)

    @pl.when(step == 0)
    def _():
        for slot in range(slots):
            gate = mod_ref[slot, 2:3, :]
            for code, block in ((0, own_ref), (2, over_ref), (1, beside_ref), (3, far_ref)):
                start = pl.multiple_of((me_ref[0] ^ code) * rows, rows)
                mask = mask_ref[slot, pl.ds(start, rows), :]
                grad_s[pl.ds(slot * length + start, rows), :] = (
                    mask * block[slot].astype(f32) * gate
                ).astype(bf16)
        split_columns(grad_s, side_ref, chunk, keep_ref, give_ref)

    @pl.when(step < pl.num_programs(0) // 2)
    def _():
        out_ref[...] = contract_cols(grad_s[...], mine_ref[...]).astype(bf16)

    @pl.when(step >= pl.num_programs(0) // 2)
    def _():
        out_ref[...] = contract_cols(grad_s[...], theirs_ref[...]).astype(bf16)


def gate_call(me, side, blocks, mask, mods, mine, theirs, chunk):
    slots, rows, model = blocks[0].shape
    count = slots * mask.shape[1]
    quarter = mine.shape[0]
    parts = 2
    width = quarter // parts

    def out_at(j, me_ref, side_ref):
        return (0, ((me_ref[0] & 1) ^ (j // parts)) * parts + j % parts)

    fixed = lambda *shape: pl.BlockSpec(shape, lambda j, *refs: (0,) * len(shape))
    return pl.pallas_call(
        functools.partial(gate_kernel, chunk),
        grid_spec=pltpu.PrefetchScalarGridSpec(
            num_scalar_prefetch=2,
            grid=(2 * parts,),
            in_specs=[fixed(slots, rows, model)] * 4
            + [
                fixed(*mask.shape),
                fixed(slots, 3, model),
                pl.BlockSpec((width, model), lambda j, *refs: (jnp.minimum(j, parts - 1), 0)),
                pl.BlockSpec((width, model), lambda j, *refs: (jnp.maximum(j - parts, 0), 0)),
            ],
            out_specs=[
                fixed(count, model // 2),
                fixed(count, model // 2),
                pl.BlockSpec((count, width), out_at),
            ],
            scratch_shapes=[pltpu.VMEM((count, model), bf16)],
        ),
        out_shape=[
            shaped((count, model // 2), bf16),
            shaped((count, model // 2), bf16),
            outer((count, 2 * quarter), bf16),
        ],
        compiler_params=kernel_params(20),
        cost_estimate=LIGHT,
        name="gate_project",
    )(me, side, *blocks, mask, mods, mine, theirs)


def pair_kernel(first_ref, second_ref, third_ref, fourth_ref, left_ref, right_ref):
    left_ref[...] = (first_ref[...].astype(f32) + second_ref[...].astype(f32)).astype(bf16)
    right_ref[...] = (third_ref[...].astype(f32) + fourth_ref[...].astype(f32)).astype(bf16)


def pair_call(first, second, third, fourth, blocks):
    rows, cols = first.shape
    block = pl.BlockSpec((rows // blocks, cols), lambda i: (i, 0))
    return pl.pallas_call(
        pair_kernel,
        grid=(blocks,),
        in_specs=[block] * 4,
        out_specs=[block] * 2,
        out_shape=[shaped((rows, cols), bf16)] * 2,
        compiler_params=kernel_params(10),
        cost_estimate=LIGHT,
        name="pair_sums",
    )(held(first), held(second), held(third), held(fourth))


def join_kernel(keep_ref, there_ref, out_ref):
    out_ref[...] = (keep_ref[...].astype(f32) + there_ref[...].astype(f32)).astype(bf16)


def join_call(keep, there):
    return pl.pallas_call(
        join_kernel,
        out_shape=shaped(keep.shape, bf16),
        compiler_params=kernel_params(8),
        cost_estimate=LIGHT,
        name="join_sums",
    )(keep, there)


def pack_kernel(side_ref, conv_ref, scan_ref, keep_ref, send_ref, total):
    count = conv_ref.shape[0]
    rows = keep_ref.shape[0]
    total[0:count, :] = conv_ref[...]
    total[count:, :] = scan_ref[...]
    side = side_ref[0]
    keep_ref[...] = total[pl.ds(pl.multiple_of(side * rows, rows), rows), :]
    send_ref[...] = total[pl.ds(pl.multiple_of((1 - side) * rows, rows), rows), :].astype(bf16)


def pack_call(side, conv, scan):
    cols = conv.shape[1]
    rows = (conv.shape[0] + scan.shape[0]) // 2
    return pl.pallas_call(
        pack_kernel,
        in_specs=[scalars(), whole(*conv.shape), whole(*scan.shape)],
        out_specs=[whole(rows, cols)] * 2,
        grid=(1,),
        out_shape=[shaped((rows, cols), f32), shaped((rows, cols), bf16)],
        scratch_shapes=[pltpu.VMEM((2 * rows, cols), f32)],
        compiler_params=kernel_params(14),
        cost_estimate=LIGHT,
        name="pack_sums",
    )(side, conv, scan)


def unpack_kernel(
    spots, side_ref, keep_ref, there_ref, xproj_ref, taps_ref, dtproj_ref, rates_ref, vec_ref, total
):
    rows = keep_ref.shape[0]
    cols, tap_count, base, rank, states = spots
    side = side_ref[0]
    total[pl.ds(pl.multiple_of(side * rows, rows), rows), :] = keep_ref[...].astype(f32)
    total[pl.ds(pl.multiple_of((1 - side) * rows, rows), rows), :] = there_ref[...].astype(f32)
    dtproj_ref[...] = total[base : base + rank, :]
    taps_ref[...] = total[cols : cols + tap_count, :]
    first = base + rank
    rates_ref[...] = total[first : first + states, :]
    vec_ref[...] = jnp.zeros_like(vec_ref)
    vec_ref[0:1, :] = total[cols + tap_count : cols + tap_count + 1, :]
    vec_ref[1:3, :] = total[first + states : first + states + 2, :]
    for at in range(0, total.shape[1], 128):
        here = slice(at, at + 128)
        xproj_ref[here, :] = jnp.transpose(total[0:cols, here])


def unpack_call(side, keep, there, cols, tap_count, base, rank, states):
    rows, channels = keep.shape
    shapes = [(channels, cols), (tap_count, channels), (rank, channels), (states, channels)]
    shapes += [(8, channels)]
    return pl.pallas_call(
        functools.partial(unpack_kernel, (cols, tap_count, base, rank, states)),
        grid=(1,),
        in_specs=[scalars(), whole(rows, channels), whole(rows, channels)],
        out_specs=[whole(*shape) for shape in shapes],
        out_shape=[shaped(shape, f32) for shape in shapes],
        scratch_shapes=[pltpu.VMEM((2 * rows, channels), f32)],
        compiler_params=kernel_params(16),
        cost_estimate=LIGHT,
        name="unpack_sums",
    )(side, keep, there)


def fold_kernel(rows, me_ref, *refs):
    mine_ref, sent_ref = refs[-2:]
    count = len(refs) // 2 - 1
    items = refs[0].shape[0] // rows // 2
    chip = me_ref[0] >> 1
    for at in range(count):
        keep_ref, there_ref = refs[at], refs[count + at]
        for item in range(items):
            for which, out_ref in ((chip, mine_ref), (1 - chip, sent_ref)):
                here = pl.ds(pl.multiple_of((2 * item + which) * rows, rows), rows)
                total = keep_ref[here, :] + there_ref[here, :].astype(f32)
                out_ref[at * items + item] = total.astype(out_ref.dtype)


def fold_call(me, keeps, theres, rows):
    count, model = keeps[0].shape
    slots = len(keeps) * count // rows // 2
    return pl.pallas_call(
        functools.partial(fold_kernel, rows),
        grid=(1,),
        in_specs=[scalars()] + [whole(count, model)] * (2 * len(keeps)),
        out_specs=[whole(slots, rows, model)] * 2,
        out_shape=[shaped((slots, rows, model), f32), shaped((slots, rows, model), bf16)],
        compiler_params=kernel_params(14),
        cost_estimate=LIGHT,
        name="fold_rows",
    )(me, *keeps, *theres)


def rows_kernel(
    tokens_ref, cot_ref, mask_ref, mod_ref, branch_ref, branch_far_ref, norm_ref, norm_far_ref,
    mixed_ref, grad_ref, mod_grad_ref
):
    raw = tokens_ref[...].astype(f32)
    mask = mask_ref[...]
    gate = mod_ref[2:3, :]
    branch = branch_ref[...] + branch_far_ref[...].astype(f32)
    mixed_ref[...] = mask * (raw + gate * branch)
    res_grad = mask * cot_ref[...].astype(f32)
    centred = raw - jnp.mean(raw, axis=1, keepdims=True)
    spread = jnp.mean(centred * centred, axis=1, keepdims=True)
    inverse = lax.rsqrt(spread + EPSILON)
    hat = centred * inverse
    normed_grad = mask * (norm_ref[...] + norm_far_ref[...].astype(f32))
    q = normed_grad * (1.0 + mod_ref[1:2, :])
    grad_ref[...] = res_grad + inverse * (
        q - jnp.mean(q, axis=1, keepdims=True) - hat * jnp.mean(q * hat, axis=1, keepdims=True)
    )
    mod_grad_ref[0:1, :] = jnp.sum(normed_grad, axis=0, keepdims=True)
    mod_grad_ref[1:2, :] = jnp.sum(normed_grad * hat, axis=0, keepdims=True)
    mod_grad_ref[2:3, :] = jnp.sum(res_grad * branch, axis=0, keepdims=True)


def rows_call(tokens, cot, mask, mods, branch, branch_far, norm, norm_far):
    slots, rows, model = tokens.shape
    row = pl.BlockSpec((None, rows, model), lambda i: (i, 0, 0))
    mod = pl.BlockSpec((None, 3, model), lambda i: (i, 0, 0))
    return pl.pallas_call(
        rows_kernel,
        grid=(slots,),
        in_specs=[row, row, pl.BlockSpec((None, rows, 1), lambda i: (i, 0, 0)), mod, row, row, row, row],
        out_specs=[row, row, mod],
        out_shape=[
            shaped((slots, rows, model), f32),
            shaped((slots, rows, model), f32),
            shaped((slots, 3, model), f32),
        ],
        compiler_params=kernel_params(14),
        cost_estimate=LIGHT,
        name="owned_rows",
    )(tokens, cot, mask, mods, branch, branch_far, norm, norm_far)


def pick_rows(values_ref, parity, chips, rows):
    blocks = []
    for at in range(values_ref.shape[0] // rows // 2):
        start = pl.multiple_of((2 * at + parity) * rows, rows)
        blocks.append(values_ref[pl.ds(start, rows), :])
    return jnp.concatenate(blocks, 0)


def branch_kernel(rows, flip_ref, values_ref, weight_ref, keep_ref, send_ref):
    core = flip_ref[0]
    keep_ref[...] = matmul(pick_rows(values_ref, core, 2, rows), weight_ref[...])
    send_ref[...] = matmul(pick_rows(values_ref, 1 - core, 2, rows), weight_ref[...]).astype(bf16)


def branch_call(flip, values, weight, rows, width):
    count, depth = values.shape
    model = weight.shape[1]
    out = [shaped((count // 2, model), f32), shaped((count // 2, model), bf16)]
    return pl.pallas_call(
        functools.partial(branch_kernel, rows),
        grid=(model // width,),
        in_specs=[
            pl.BlockSpec(memory_space=pltpu.SMEM),
            pl.BlockSpec((count, depth), lambda j: (0, 0)),
            pl.BlockSpec((depth, width), lambda j: (0, j)),
        ],
        out_specs=[pl.BlockSpec((count // 2, width), lambda j: (0, j))] * 2,
        out_shape=out,
        compiler_params=kernel_params(10),
        cost_estimate=pl.CostEstimate(flops=1000, bytes_accessed=1000, transcendentals=0),
        name="branch_rows",
    )(flip, values, weight)


def proj_back_kernel(rows, slots, flip_ref, *refs):
    x_refs = refs[:slots]
    z_ref, weight_ref, there_ref, keep_ref, send_ref, x_s, z_s, mine_s = refs[slots:]
    core = flip_ref[0]
    half = there_ref.shape[1]
    length = x_refs[0].shape[0]

    def place(x_to, z_to, mine):
        for slot in range(slots):
            x_to[slot * length : (slot + 1) * length, :] = x_refs[slot][...]
        z_to[...] = z_ref[...]
        mine_s[...] = mine

    pl.when(core == 0)(lambda: place(x_s, z_s, weight_ref[:, :half]))
    pl.when(core == 1)(lambda: place(z_s, x_s, weight_ref[:, half:]))
    for parity, out_ref in ((core, keep_ref), (1 - core, send_ref)):
        total = contract_cols(pick_rows(x_s, parity, 2, rows), mine_s[...]) + contract_cols(
            pick_rows(z_s, parity, 2, rows), there_ref[...]
        )
        out_ref[...] = total.astype(out_ref.dtype)


def proj_back_call(flip, xs, z, weight, there, rows, width):
    length, depth = xs[0].shape
    count = z.shape[0]
    model = there.shape[0]
    return pl.pallas_call(
        functools.partial(proj_back_kernel, rows, len(xs)),
        grid=(model // width,),
        in_specs=[scalars()]
        + [whole(length, depth)] * len(xs)
        + [
            whole(count, depth),
            pl.BlockSpec((width, 2 * depth), lambda j: (j, 0)),
            pl.BlockSpec((width, depth), lambda j: (j, 0)),
        ],
        out_specs=[pl.BlockSpec((count // 2, width), lambda j: (0, j))] * 2,
        out_shape=[shaped((count // 2, model), f32), shaped((count // 2, model), bf16)],
        scratch_shapes=[pltpu.VMEM((count, depth), bf16)] * 2 + [pltpu.VMEM((width, depth), bf16)],
        compiler_params=kernel_params(18),
        cost_estimate=LIGHT,
        name="proj_back",
    )(flip, *xs, z, held(weight), held(there))


def cond_kernel(mod_ref, weight_ref, cond_ref, out_ref):
    value = cond_ref[...].astype(f32)
    sig = jax.nn.sigmoid(value)
    out_ref[...] = contract_cols(mod_ref[...], weight_ref[...]) * sig * (1.0 + value * (1.0 - sig))


def cond_call(mods, weight, cond, start, count):
    slots, columns = mods.shape
    width = 256 if count % 256 == 0 else 128
    first = start // width
    return pl.pallas_call(
        cond_kernel,
        grid=(count // width,),
        in_specs=[
            whole(slots, columns),
            pl.BlockSpec((width, columns), lambda j: (first + j, 0)),
            pl.BlockSpec((slots, width), lambda j: (0, first + j)),
        ],
        out_specs=pl.BlockSpec((slots, width), lambda j: (0, j)),
        out_shape=shaped((slots, count), f32),
        compiler_params=kernel_params(14),
        cost_estimate=LIGHT,
        name="cond_rows",
    )(mods, held(weight), cond)


def tap_sum(pad, taps_ref, here, sign, length):
    taps = taps_ref.shape[0] - 1
    total = pad[MARGIN : MARGIN + length, :] * taps_ref[taps - 1 : taps, here]
    for by in range(1, taps):
        start = MARGIN - sign * by
        total = total + pad[start : start + length, :] * taps_ref[taps - 1 - by : taps - by, here]
    return total


def conv_kernel(
    flip_ref, own_ref, other_ref, mask_ref, taps_ref, xproj_ref, x_ref, z_ref, u_ref, slope_ref,
    dbl_ref, pads
):
    step = pl.program_id(1)
    length, width = own_ref.shape
    taps = taps_ref.shape[0] - 1
    flip = flip_ref[0]

    def run(flipped):
        x_from, z_from = (other_ref, own_ref) if flipped else (own_ref, other_ref)
        x_ref[...] = x_from[...]
        z_ref[...] = z_from[...]
        mask = jnp.broadcast_to(mask_ref[...], (length, 128))
        for tile in range(width // 128):
            here = slice(tile * 128, (tile + 1) * 128)
            pad = pads.at[tile]
            pad[0:MARGIN, :] = jnp.zeros((MARGIN, 128), f32)
            pad[MARGIN + length :, :] = jnp.zeros((MARGIN, 128), f32)
            pad[MARGIN : MARGIN + length, :] = x_from[:, here].astype(f32)
            conv = taps_ref[taps : taps + 1, here] + tap_sum(pad, taps_ref, here, -1 if flipped else 1, length)
            sig = 0.5 + 0.5 * jnp.tanh(0.5 * conv)
            u_ref[:, here] = (mask * (conv * sig)).astype(bf16)
            slope_ref[:, here] = mask * (sig * (1.0 + conv * (1.0 - sig)))

    pl.when(flip == 0)(lambda: run(False))
    pl.when(flip == 1)(lambda: run(True))
    part = matmul(u_ref[...], xproj_ref[...])

    @pl.when(step == 0)
    def _():
        dbl_ref[...] = part

    @pl.when(step > 0)
    def _():
        dbl_ref[...] += part


def conv_back_kernel(
    flip_ref, x_ref, u_ref, slope_ref, taps_ref, xproj_ref, us_ref, dg_ref, prev_ref, keep_ref,
    send_ref, packed_ref, grad_s, pads, grad_pads
):
    length, width = x_ref.shape
    flip = flip_ref[0]
    taps = taps_ref.shape[0] - 1
    dg = dg_ref[...]
    cols = dg.shape[1]
    grad_s[...] = (us_ref[...] + contract_cols(dg, xproj_ref[...])) * slope_ref[...]
    packed_ref[0:cols, :] = prev_ref[0:cols, :] + matmul(
        jnp.transpose(dg.astype(f32)).astype(bf16), u_ref[...]
    )
    rest = packed_ref.shape[0] - cols - taps - 1
    packed_ref[cols + taps + 1 :, :] = jnp.zeros((rest, width), f32)

    def run(flipped, out_ref):
        sign = -1 if flipped else 1
        for tile in range(width // 128):
            here = slice(tile * 128, (tile + 1) * 128)
            pad, grad_pad = pads.at[tile], grad_pads.at[tile]
            for ref in (pad, grad_pad):
                ref[0:MARGIN, :] = jnp.zeros((MARGIN, 128), f32)
                ref[MARGIN + length :, :] = jnp.zeros((MARGIN, 128), f32)
            conv_grad = grad_s[:, here]
            pad[MARGIN : MARGIN + length, :] = x_ref[:, here].astype(f32)
            grad_pad[MARGIN : MARGIN + length, :] = conv_grad
            for by in range(taps):
                start = MARGIN - sign * by
                row = cols + taps - 1 - by
                packed_ref[row : row + 1, here] = prev_ref[row : row + 1, here] + jnp.sum(
                    conv_grad * pad[start : start + length, :], axis=0, keepdims=True
                )
            row = cols + taps
            packed_ref[row : row + 1, here] = prev_ref[row : row + 1, here] + jnp.sum(
                conv_grad, axis=0, keepdims=True
            )
            out_ref[:, here] = tap_sum(grad_pad, taps_ref, here, -sign, length).astype(bf16)

    for flipped in (False, True):
        for block in range(2):
            out_ref = keep_ref if block == int(flipped) else send_ref
            pl.when((flip == int(flipped)) & (pl.program_id(0) == block))(
                functools.partial(run, flipped, out_ref)
            )


def conv_call(flip, own, other, mask, taps, xproj, width):
    slots, length = mask.shape[:2]
    channels = own.shape[1]
    cols = xproj.shape[1]
    block = pl.BlockSpec((length, width), lambda i, j: (i, j))
    return pl.pallas_call(
        conv_kernel,
        grid=(slots, channels // width),
        in_specs=[
            scalars(),
            block,
            block,
            pl.BlockSpec((None, length, 1), lambda i, j: (i, 0, 0)),
            pl.BlockSpec((taps.shape[0], width), lambda i, j: (0, j)),
            pl.BlockSpec((width, cols), lambda i, j: (j, 0)),
        ],
        out_specs=[block] * 4 + [pl.BlockSpec((length, cols), lambda i, j: (i, 0))],
        out_shape=[outer((slots * length, channels), bf16)] * 3
        + [outer((slots * length, channels), f32), outer((slots * length, cols), f32)],
        scratch_shapes=[pltpu.VMEM((width // 128, length + 2 * MARGIN, 128), f32)],
        compiler_params=kernel_params(16),
        cost_estimate=LIGHT,
        name="conv_forward",
    )(flip, own, other, mask, taps, xproj)


def conv_back_call(flip, slot, length, x, u, slope, taps, xproj, us, dg, prev):
    channels = x.shape[1]
    cols = xproj.shape[1]
    width = channels // 2
    rows = prev.shape[0]
    item = pl.BlockSpec((length, width), lambda j: (slot, j))
    pads = pltpu.VMEM((width // 128, length + 2 * MARGIN, 128), f32)
    return pl.pallas_call(
        conv_back_kernel,
        grid=(2,),
        in_specs=[
            scalars(),
            item,
            item,
            item,
            pl.BlockSpec((taps.shape[0], width), lambda j: (0, j)),
            pl.BlockSpec((width, cols), lambda j: (j, 0)),
            pl.BlockSpec((length, width), lambda j: (0, j)),
            whole(length, cols),
            pl.BlockSpec((rows, width), lambda j: (0, j)),
        ],
        out_specs=[
            whole(length, width),
            whole(length, width),
            pl.BlockSpec((rows, width), lambda j: (0, j)),
        ],
        out_shape=[
            shaped((length, width), bf16),
            shaped((length, width), bf16),
            shaped((rows, channels), f32),
        ],
        scratch_shapes=[pltpu.VMEM((length, width), f32), pads, pads],
        compiler_params=kernel_params(18),
        cost_estimate=LIGHT,
        name="conv_backward",
    )(flip, held(x), held(u), held(slope), taps, xproj, held(us), dg, prev)


def spread(dbl_ref, first, b_wide, c_wide, rows_s, states):
    length, cols = dbl_ref.shape
    rest = dbl_ref[...]
    row = lax.broadcasted_iota(jnp.int32, (cols, cols), 0)
    col = lax.broadcasted_iota(jnp.int32, (cols, cols), 1)
    rows = jnp.zeros((length, cols), f32)
    for part in range(3):
        piece = rest.astype(bf16)
        rest = rest - piece.astype(f32)
        pick = ((row == first + col % (2*states)) & (col // (2*states) == part))
        rows = rows + matmul(piece, jnp.where(pick, 1.0, 0.0).astype(bf16))
    rows_s[...] = rows
    which = lax.broadcasted_iota(jnp.int32, (states, cols), 0)
    lane = lax.broadcasted_iota(jnp.int32, (states, cols), 1)
    mine = jnp.where(lane % states == which, 1.0, 0.0)
    row = lax.broadcasted_iota(jnp.int32, (cols, 2*cols), 0)
    col = lax.broadcasted_iota(jnp.int32, (cols, 2*cols), 1)
    wide = jnp.where((row % (2*states)) // states == col // cols, 1.0, 0.0).astype(bf16)
    def some(at, _):
        left = [(mine*jnp.broadcast_to(rows_s[pl.ds(at*CHUNK+t, 1), :], (states, cols))).astype(bf16) for t in range(CHUNK)]
        got = matmul(jnp.concatenate(left, 0), wide)
        here = pl.ds(pl.multiple_of(at*CHUNK*states, CHUNK*states), CHUNK*states)
        b_wide[here, :] = got[:, :cols]
        c_wide[here, :] = got[:, cols:]
        return 0
    lax.fori_loop(0, length//CHUNK, some, 0, unroll=4)

def tiles_of(values):
    return [values[:, at:at+128] for at in range(0, values.shape[1], 128)]

def fold(values, tmp, tt, states):
    for at, tile in enumerate(tiles_of(values)):
        total = tile[:8]
        for part in range(1, states//8):
            total = total + tile[part*8:(part+1)*8]
        tmp[at, pl.ds(tt//8*64 + tt%8, 8, stride=8), :] = total

def add_tiles(values):
    parts = tiles_of(values)
    total = parts[0]
    for part in parts[1:]:
        total = total + part
    return total

def unfold(tmp, out, base):
    for at in range(out.shape[1]//128):
        for part in range(CHUNK//8):
            acc = tmp[at, part*64:part*64+8, :]
            for row in range(1, 8):
                acc = acc + tmp[at, part*64+row*8:part*64+row*8+8, :]
            out[pl.ds(pl.multiple_of(base+part*8, 8), 8), at*128:(at+1)*128] = acc

def collect(acc, tmp, out, length, states):
    which = lax.broadcasted_iota(jnp.int32, (states, 128), 0)
    lane = lax.broadcasted_iota(jnp.int32, (states, 128), 1)
    mine = which == lane
    def some(at, _):
        base = pl.multiple_of(at*CHUNK, CHUNK)
        for tt in range(CHUNK):
            sums = jnp.sum(acc[pl.ds((base+tt)*states, states), :], axis=1, keepdims=True)
            fold(jnp.where(mine, sums, 0.0), tmp, tt, states)
        unfold(tmp, out, base)
        return 0
    lax.fori_loop(0, length//CHUNK, some, 0, unroll=4)

def fwd_kernel(states, flip_ref, dbl_ref, dtp_ref, vec_ref, rate2_ref, u_ref, z_ref, gg_ref,
               gate_keep, gate_send, z_keep, z_send, delta_ref, yg_ref, prior_ref, cout_ref,
               b_wide, c_wide, drive_s, sig_s, y_s, y_tmp, c_acc, rows_s):
    step = pl.program_id(1)
    length, width = u_ref.shape
    rank = dtp_ref.shape[0]
    group = CHUNK*states
    chunks = length//CHUNK
    flip = flip_ref[0]
    @pl.when(step == 0)
    def _():
        spread(dbl_ref, rank, b_wide, c_wide, rows_s, states)
        c_acc[...] = jnp.zeros_like(c_acc)
    low = dbl_ref[:, :rank].astype(bf16)
    pre = matmul(low, dtp_ref[...]) + vec_ref[0:1, :]
    delta = jnp.maximum(pre, 0.0) + jnp.log1p(jnp.exp(-jnp.abs(pre)))
    delta_ref[...] = delta
    drive_s[...] = delta * u_ref[...].astype(f32)
    z = z_ref[...].astype(f32)
    sig = 0.5 + 0.5*jnp.tanh(0.5*z)
    sig_s[...] = sig
    yg_ref[...] = gg_ref[...].astype(f32) * (z * sig)
    def run(flipped):
        def ahead(chunk, state):
            place = chunks-1-chunk if flipped else chunk
            base = pl.multiple_of(place*CHUNK, CHUNK)
            wide = pl.multiple_of(place*group, group)
            for at in range(CHUNK):
                tt = CHUNK-1-at if flipped else at
                t = base + tt
                here = pl.ds(wide + tt*states, states)
                d = jnp.broadcast_to(delta_ref[pl.ds(t,1),:], (states,width))
                x = jnp.broadcast_to(drive_s[pl.ds(t,1),:], (states,width))
                g = jnp.broadcast_to(yg_ref[pl.ds(t,1),:], (states,width))
                b = jnp.concatenate([b_wide[here,:]]*(width//128), axis=1)
                c = jnp.concatenate([c_wide[here,:]]*(width//128), axis=1)
                prior = jnp.exp2(d*rate2_ref[...])*state
                state = prior + x*b
                prior_ref[here,:] = prior.astype(bf16)
                fold(state*c, y_tmp, tt, states)
                c_acc[here,:] += add_tiles(state*g)
            unfold(y_tmp, y_s, base)
            return state
        lax.fori_loop(0, chunks, ahead, jnp.zeros((states,width), f32))
    pl.when(flip == 0)(lambda: run(False))
    pl.when(flip == 1)(lambda: run(True))
    u = u_ref[...].astype(f32)
    z = z_ref[...].astype(f32)
    sig = sig_s[...]
    y = y_s[...] + vec_ref[1:2,:]*u
    gated = (y*(z*sig)).astype(bf16)
    zg = (gg_ref[...].astype(f32)*y*(sig*(1.0+z*(1.0-sig)))).astype(bf16)
    half = gate_keep.shape[1]
    for at in range(2*half//width):
        for core in range(2):
            def put(at=at, core=core):
                for side in range(2):
                    low, high = max(at*width, side*half), min((at+1)*width, (side+1)*half)
                    if low < high:
                        to = slice(low-side*half, high-side*half)
                        of = slice(low-at*width, high-at*width)
                        (gate_keep if side == core else gate_send)[:, to] = gated[:, of]
                        (z_keep if side == core else z_send)[:, to] = zg[:, of]
            pl.when((step == at) & (flip == core))(put)
    @pl.when(step == pl.num_programs(1)-1)
    def _():
        collect(c_acc, y_tmp, rows_s, length, states)
        cout_ref[...] = rows_s[:, :states]

def bwd_kernel(states, flip_ref, dbl_ref, dtp_ref, vec_ref, rate2_ref, u_ref, delta_ref, yg_ref, prior_ref, cout_ref, prev_ref,
               us_ref, part_ref, packed_ref,
               b_wide, c_wide, drive_s, r_s, w_s, low_t, rank_s, r_tmp, w_tmp, b_acc, rows_s):
    step = pl.program_id(0)
    length, width = u_ref.shape
    rank = dtp_ref.shape[0]
    group = CHUNK*states
    chunks = length//CHUNK
    flip = flip_ref[0]
    @pl.when(step == 0)
    def _():
        low_t[...] = jnp.transpose(dbl_ref[...])[:rank,:].astype(bf16)
        spread(dbl_ref, rank, b_wide, c_wide, rows_s, states)
        b_acc[...] = jnp.zeros_like(b_acc)
        rank_s[...] = jnp.zeros_like(rank_s)
    u = u_ref[...].astype(f32)
    drive_s[...] = delta_ref[...]*u
    def run(flipped):
        def back(chunk, carry):
            carried, total = carry
            place = chunk if flipped else chunks-1-chunk
            base = pl.multiple_of(place*CHUNK, CHUNK)
            wide = pl.multiple_of(place*group, group)
            for at in range(CHUNK):
                tt = at if flipped else CHUNK-1-at
                t = base + tt
                here = pl.ds(wide + tt*states, states)
                d = jnp.broadcast_to(delta_ref[pl.ds(t,1),:], (states,width))
                x = jnp.broadcast_to(yg_ref[pl.ds(t,1),:], (states,width))
                e = jnp.broadcast_to(drive_s[pl.ds(t,1),:], (states,width))
                b = jnp.concatenate([b_wide[here,:]]*(width//128), axis=1)
                c = jnp.concatenate([c_wide[here,:]]*(width//128), axis=1)
                power = d*rate2_ref[...]
                adj = carried + x*c
                moved = (adj*prior_ref[here,:].astype(f32))*power
                total = total + moved
                fold(moved, w_tmp, tt, states)
                fold(adj*b, r_tmp, tt, states)
                b_acc[here,:] += add_tiles(adj*e)
                carried = jnp.exp2(power)*adj
            unfold(w_tmp, w_s, base)
            unfold(r_tmp, r_s, base)
            return carried, total
        zero = jnp.zeros((states,width), f32)
        _, total = lax.fori_loop(0, chunks, back, (zero, zero))
        packed_ref[rank:rank+states,:] = prev_ref[rank:rank+states,:] + total*(1.0/LOG2E)
    pl.when(flip == 0)(lambda: run(False))
    pl.when(flip == 1)(lambda: run(True))
    yg = yg_ref[...]
    r = r_s[...]
    delta = delta_ref[...]
    us_ref[...] = delta*r + vec_ref[1:2,:]*yg
    low = dbl_ref[:, :rank].astype(bf16)
    pre = matmul(low, dtp_ref[...]) + vec_ref[0:1,:]
    sig = jnp.exp(pre-delta)
    ratio = jnp.where(delta > 1e-30, sig/jnp.maximum(delta, 1e-30), 1.0)
    pre_grad = w_s[...]*(1.0/LOG2E)*ratio + u*r*sig
    pre_low = pre_grad.astype(bf16)
    rank_s[...] += contract_cols(pre_low, dtp_ref[...])
    packed_ref[0:rank,:] = prev_ref[0:rank,:] + matmul(low_t[...], pre_low)
    packed_ref[rank+states:rank+states+1,:] = prev_ref[rank+states:rank+states+1,:] + jnp.sum(pre_grad, axis=0, keepdims=True)
    packed_ref[rank+states+1:rank+states+2,:] = prev_ref[rank+states+1:rank+states+2,:] + jnp.sum(yg*u, axis=0, keepdims=True)
    rest = packed_ref.shape[0]-rank-states-2
    packed_ref[rank+states+2:,:] = jnp.zeros((rest,width), f32)
    @pl.when(step == pl.num_programs(0)-1)
    def _():
        collect(b_acc, r_tmp, rows_s, length, states)
        part_ref[...] = jnp.concatenate([rank_s[...], rows_s[:, :states], cout_ref[...]], axis=1)


def forward_call(flip, dbl, dtproj, vec, rates2, u, z, gg, slots, width):
    count, channels = u.shape
    length = count // slots
    half = channels // 2
    states, rank, cols = rates2.shape[0], dtproj.shape[0], dbl.shape[1]
    weight = lambda rows: pl.BlockSpec((rows, width), lambda i, j: (0, j))
    block = lambda rows: pl.BlockSpec((rows, width), lambda i, j: (i, j))
    item = lambda wide: pl.BlockSpec((length, wide), lambda i, j: (i, 0))
    return pl.pallas_call(
        functools.partial(fwd_kernel, states),
        grid=(slots, channels // width),
        in_specs=[scalars(), item(cols), weight(rank), weight(2), weight(states)] + [block(length)] * 3,
        out_specs=[item(half)] * 4 + [block(length)] * 2 + [block(length * states), item(states)],
        out_shape=[outer((count, half), bf16)] * 4
        + [outer((count, channels), f32)] * 2
        + [outer((count * states, channels), bf16), shaped((count, states), f32)],
        scratch_shapes=[
            pltpu.VMEM((length * states, 128), f32),
            pltpu.VMEM((length * states, 128), f32),
            pltpu.VMEM((length, width), f32),
            pltpu.VMEM((length, width), f32),
            pltpu.VMEM((length, width), f32),
            pltpu.VMEM((width // 128, CHUNK * 8, 128), f32),
            pltpu.VMEM((length * states, 128), f32),
            pltpu.VMEM((length, cols), f32),
        ],
        compiler_params=kernel_params(40),
        cost_estimate=pl.CostEstimate(
            flops=32000000000, bytes_accessed=40000000, transcendentals=14000000
        ),
        name="scan_forward",
    )(flip, dbl, dtproj, vec, rates2, held(u), held(z), held(gg))


def backward_call(flip, slot, slots, dbl, dtproj, vec, rates2, u, delta, yg, prior, cout, prev, width):
    count, channels = u.shape
    length = count // slots
    states, rank, cols = rates2.shape[0], dtproj.shape[0], dbl.shape[1]
    rows = prev.shape[0]
    weight = lambda rows: pl.BlockSpec((rows, width), lambda j: (0, j))
    block = lambda rows: pl.BlockSpec((rows, width), lambda j: (slot, j))
    item = lambda wide: pl.BlockSpec((length, wide), lambda j: (slot, 0))
    return pl.pallas_call(
        functools.partial(bwd_kernel, states),
        grid=(channels // width,),
        in_specs=[scalars(), item(cols), weight(rank), weight(2), weight(states)]
        + [block(length)] * 3
        + [block(length * states), item(states), weight(rows)],
        out_specs=[weight(length), whole(length, cols), weight(rows)],
        out_shape=[
            outer((length, channels), f32),
            shaped((length, cols), f32),
            shaped((rows, channels), f32),
        ],
        scratch_shapes=[
            pltpu.VMEM((length * states, 128), f32),
            pltpu.VMEM((length * states, 128), f32),
            pltpu.VMEM((length, width), f32),
            pltpu.VMEM((length, width), f32),
            pltpu.VMEM((length, width), f32),
            pltpu.VMEM((rank, length), bf16),
            pltpu.VMEM((length, rank), f32),
            pltpu.VMEM((width // 128, CHUNK * 8, 128), f32),
            pltpu.VMEM((width // 128, CHUNK * 8, 128), f32),
            pltpu.VMEM((length * states, 128), f32),
            pltpu.VMEM((length, cols), f32),
        ],
        compiler_params=kernel_params(40),
        cost_estimate=pl.CostEstimate(
            flops=22000000000, bytes_accessed=20000000, transcendentals=7000000
        ),
        name="scan_backward",
    )(flip, dbl, dtproj, vec, rates2, held(u), held(delta), held(yg), held(prior), cout, prev)


def local(
    tokens,
    cond,
    counts,
    valid,
    ada_weight,
    ada_bias,
    in_weight,
    conv_weight,
    conv_bias,
    xproj_weight,
    dtproj_weight,
    dt_bias,
    a_log,
    skip_gain,
    out_weight,
    cotangent,
):
    slot_count, shard_rows, model = tokens.shape
    dirs = lax.axis_size("dir")
    dps = lax.axis_size("dp")
    me = lax.axis_index("dir")
    dp_index = lax.axis_index("dp")
    core = me & 1
    half = in_weight.shape[1] // 2
    rank = dtproj_weight.shape[0]
    states = a_log.shape[1]
    tap_count = conv_weight.shape[1]
    cols = xproj_weight.shape[1]
    slots = range(slot_count)
    width = 512 if dt_bias.shape[0] % 512 == 0 else 128
    first, second = bit_orders("dp")
    z_bit, out_bit = first[0], second[0]
    scalar = lambda value: value.astype(jnp.int32).reshape(1)
    flip, me_ref = scalar(core), scalar(me)
    z_side, out_side = scalar((dp_index >> z_bit) & 1), scalar((dp_index >> out_bit) & 1)

    live_slots = (jnp.arange(slot_count) < counts[0]).astype(f32)
    full_mask = valid.astype(f32) * live_slots[:, None]
    mask_cols = full_mask[:, :, None]
    local_mask = lax.dynamic_slice_in_dim(full_mask, me * shard_rows, shard_rows, 1)[:, :, None]

    def gather_rows(block, *earlier):
        over = after(swap(block, "dir", 1), *earlier)
        return block, over, swap(block, "dir", 0), swap(over, "dir", 0)

    cond_act = jax.nn.silu(cond.astype(f32)).astype(bf16)
    modulation = matmul(cond_act, ada_weight) + ada_bias.astype(f32)[None, :]
    mods = modulation.reshape(slot_count, 3, model)
    token_blocks = gather_rows(tokens, modulation)
    out_there = swap(out_weight, "dir", 0)

    taps = jnp.concatenate(
        [jnp.transpose(conv_weight.astype(f32)), conv_bias.astype(f32)[None, :]], 0
    )
    vec = jnp.stack([dt_bias, skip_gain])
    rates2 = -jnp.exp(jnp.transpose(a_log)) * LOG2E

    left_mine, left_give, own = norm_call(
        me_ref,
        z_side,
        token_blocks,
        mask_cols,
        mods,
        in_weight,
        width,
        model // dps << z_bit,
    )
    in_send = lax.dynamic_slice_in_dim(after(in_weight, left_mine), (1 - core) * half, half, 1)
    in_there = swap(in_send, "dir", 0)
    other = after(swap(own, "dir", 0), in_send)
    x, z, u, slope, part = conv_call(flip, own, other, mask_cols, taps, xproj_weight, half)
    part_there = swap(part, "dir", 1)
    cot_blocks = gather_rows(cotangent, part)
    branch_mine, branch_give, gg = gate_call(
        me_ref,
        out_side,
        cot_blocks,
        mask_cols,
        after(mods, part),
        out_weight,
        out_there,
        model // dps << out_bit,
    )
    left_there = swap(left_give, "dp", z_bit)
    branch_there = swap(branch_give, "dp", out_bit)
    dbl = part + after(part_there, gg)
    gate_keep, gate_send, z_keep, z_send, *saved = forward_call(
        flip, dbl, dtproj_weight, vec, rates2, u, z, gg, slot_count, width
    )
    gate_send, z_send = after((gate_send, z_send), left_there, branch_there)
    gate_all, z_all = pair_call(
        gate_keep, swap(gate_send, "dir", 0), z_keep, swap(z_send, "dir", 0), slot_count
    )
    gate_there = swap(gate_all, "dp", out_bit)
    z_there = swap(z_all, "dp", z_bit)

    rows_keep, rows_give = branch_call(flip, gate_all, out_weight, shard_rows, width)
    rows_there = swap(rows_give, "dir", 0)

    rest = lambda out: [bit for bit in first if bit != out]
    scan_rows = -(-(rank + states + 2) // 8) * 8
    packed = jnp.zeros((scan_rows, dt_bias.shape[0]), f32)
    conv_rows = -(-(cols + tap_count + 1) // 8) * 8
    conv_packed = jnp.zeros((conv_rows, dt_bias.shape[0]), f32)
    length = mask_cols.shape[1]

    def back_conv(slot, us, dg, conv_packed):
        return conv_back_call(
            flip, slot, length, x, u, slope, taps, xproj_weight, us, dg, conv_packed
        )

    x_sums, x_theres = [], []
    u_tied = after(u, z_all, rows_give)
    for slot in slots:
        us, part_back, packed = backward_call(
            flip, slot, slot_count, dbl, dtproj_weight, vec, rates2, u_tied, *saved, packed, width
        )
        there = swap(part_back, "dir", 1)
        if slot == 0:
            z_part = Scatter(
                contract_rows(left_mine, after(z_all, part_back))
                + contract_rows(left_there, after(z_there, part_back)),
                "dp",
                rest(z_bit),
            )
            out_part = Scatter(
                contract_rows(branch_mine, after(gate_all, part_back))
                + contract_rows(branch_there, after(gate_there, part_back)),
                "dp",
                rest(out_bit)[::-1],
            )
        if slot + 1 < slot_count:
            dg = (part_back + after(there, z_part.send, out_part.send)).astype(bf16)
            keep, send, conv_packed = back_conv(slot, us, dg, conv_packed)
            send_there = swap(send, "dir", 0)
            if slot == 0:
                rows_mine, branch_sent = fold_call(
                    me_ref, [rows_keep], [after(rows_there, send)], shard_rows
                )
                branch_far = swap(branch_sent, "dir", 1)
            x_sums.append(join_call(keep, after(send_there, branch_sent)))
            x_theres.append(swap(x_sums[-1], "dp", z_bit))
            u_tied, z_part.send, out_part.send = after((u, z_part.send, out_part.send), x_sums[-1])

    z_part.step(part_back, branch_far, *x_theres)
    out_part.step(part_back)
    dg = (part_back + after(there, z_part.send, out_part.send)).astype(bf16)
    keep, send, conv_packed = back_conv(slot_count - 1, us, dg, conv_packed)
    shared = SharedSum(pack_call(out_side, conv_packed, packed), "dp", second)
    send_there = swap(after(send, shared.send), "dir", 0)
    x_sums.append(join_call(keep, send_there))
    x_there = swap(x_sums[-1], "dp", z_bit)
    norm_keep, norm_give = proj_back_call(
        flip, x_sums, z_all, in_weight, in_there, shard_rows, width
    )
    z_part.step(norm_give)
    out_part.step(norm_give)
    shared.step(z_part.values, out_part.values)
    x_theres.append(after(x_there, shared.send))
    norm_there = swap(norm_give, "dir", 0)
    norm_mine, norm_sent = fold_call(
        me_ref, [norm_keep], [after(norm_there, x_theres[-1])], shard_rows
    )
    norm_far = swap(norm_sent, "dir", 1)
    x_part = contract_rows(left_mine, jnp.concatenate(after(x_sums, norm_sent), 0)) + contract_rows(
        left_there, jnp.concatenate(after(x_theres, norm_sent), 0)
    )
    x_part = Scatter(x_part, "dp", rest(z_bit))
    shared.step(x_part.send)

    mixed, token_grads, mod_part = rows_call(
        tokens,
        cotangent,
        local_mask,
        mods,
        rows_mine,
        branch_far,
        norm_mine,
        after(norm_far, shared.send),
    )
    mod_parts = [
        lax.ppermute(mod_part, "dir", [(at, at ^ code) for at in range(dirs)])
        for code in range(1, dirs)
    ]
    shared.step(mod_part)
    x_part.step(shared.send)
    beside, *over = after(mod_parts, x_part.send)
    mod_total = mod_part + beside
    if over:
        mod_total = mod_total + (over[0] + over[1])
    mod_low = mod_total.astype(bf16).reshape(slot_count, 3 * model)
    have = []
    sides = jnp.concatenate([mod_low, cond_act], 1)
    sides = gather_bit(sides, "dp", first[0], have)
    while len(shared.plan) > 1:
        shared.step(sides)
    cond_grad = cond_call(after(mod_low, sides, shared.send), ada_weight, cond, 0, model)
    sides = gather_rest(sides, "dp", first[1:], cond_grad)
    sides = sides.reshape(dps * slot_count, -1)
    total_columns = ada_weight.shape[1]
    columns = total_columns // dirs
    rows = ada_weight.shape[0] // dps
    mod_all = lax.dynamic_slice_in_dim(sides, me * columns, columns, 1)
    act_mine = lax.dynamic_slice_in_dim(sides, total_columns + dp_index * rows, rows, 1)
    ada_sum = contract_rows(act_mine, mod_all)
    portion = total_columns // dps
    bias_part = lax.dynamic_slice_in_dim(sides, dp_index * portion, portion, 1)
    bias_sum = jnp.sum(bias_part.astype(f32), axis=0)

    keep, there = shared.last(cond_grad)
    xproj_sum, kernel_sum, dtproj_sum, rate_sum, vec_sum = unpack_call(
        out_side, keep, there, cols, tap_count, conv_rows, rank, states
    )
    while x_part.order:
        x_part.step(xproj_sum)
    while z_part.order:
        z_part.step(xproj_sum)
    while out_part.order:
        out_part.step(xproj_sum)
    x_sum = x_part.values
    z_sum = z_part.values
    out_sum = jnp.transpose(out_part.values)
    keep_sum = jnp.where(core == 0, x_sum, z_sum)
    send_sum = jnp.where(core == 0, z_sum, x_sum)
    in_sum = ordered(core, keep_sum, swap(send_sum, "dir", 0), 1)

    return (
        mixed,
        token_grads,
        cond_grad,
        ada_sum,
        bias_sum,
        in_sum,
        jnp.transpose(kernel_sum),
        vec_sum[0],
        xproj_sum,
        dtproj_sum,
        vec_sum[1],
        jnp.transpose(rate_sum),
        vec_sum[2],
        out_sum,
    )


def solution(mesh):
    in_specs = (
        P("dp", "dir", None),
        P("dp", None),
        P("dp"),
        P("dp", None),
        P(),
        P(),
        P(None, "dir"),
        P("dir", None),
        P("dir"),
        P("dir", None),
        P(None, "dir"),
        P("dir"),
        P("dir", None),
        P("dir"),
        P("dir", None),
        P("dp", "dir", None),
    )
    out_specs = (
        P("dp", "dir", None),
        P("dp", "dir", None),
        P("dp", None),
        P("dp", "dir"),
        P("dp"),
        P("dp", "dir"),
        P("dir", None),
        P("dir"),
        P("dir", None),
        P(None, "dir"),
        P("dir"),
        P("dir", None),
        P("dir"),
        P("dir", "dp"),
    )
    return jax.shard_map(local, mesh=mesh, in_specs=in_specs, out_specs=out_specs, check_vma=False)
```

```python
import functools

import jax
import jax.numpy as jnp
from jax import lax
from jax.experimental import pallas as pl
from jax.experimental.pallas import tpu as pltpu
from jax.sharding import PartitionSpec as P

EPSILON = 1e-06
LOG2E = 1.4426950408889634
CHUNK = 16
MARGIN = 8

bf16 = jnp.bfloat16
f32 = jnp.float32


def swap(block, axis, bit):
    count = lax.axis_size(axis)
    return lax.ppermute(block, axis, [(at, at ^ (1 << bit)) for at in range(count)])


def contract_rows(left, right):
    return lax.dot_general(
        left, right, (((0,), (0,)), ((), ())), preferred_element_type=f32
    )


def contract_cols(left, right):
    return lax.dot_general(
        left, right, (((1,), (1,)), ((), ())), preferred_element_type=f32
    )


def matmul(left, right):
    return jnp.dot(left, right, preferred_element_type=f32)


def ordered(bit, own, other, axis):
    return jnp.where(
        bit == 0,
        jnp.concatenate([own, other], axis),
        jnp.concatenate([other, own], axis),
    )


def halves(values, bit, axis):
    size = values.shape[axis] // 2
    keep = lax.dynamic_slice_in_dim(values, bit * size, size, axis)
    send = lax.dynamic_slice_in_dim(values, (1 - bit) * size, size, axis)
    return keep, send


class Scatter:
    def __init__(self, values, axis, order):
        self.axis, self.order = axis, list(order)
        bits = len(order)
        values = values.astype(bf16)
        self.values = values.reshape((2,) * bits + (values.shape[0] >> bits,) + values.shape[1:])
        self.left = sorted(order, reverse=True)
        self.split()

    def split(self):
        if not self.order:
            return
        at = self.left.index(self.order[0])
        mine = (lax.axis_index(self.axis) >> self.order[0]) & 1
        self.keep = lax.dynamic_index_in_dim(self.values, mine, at, keepdims=False)
        send = lax.dynamic_index_in_dim(self.values, 1 - mine, at, keepdims=False)
        self.send = send.astype(bf16)

    def step(self, *earlier):
        bit = self.order.pop(0)
        self.left.remove(bit)
        arrived = after(swap(self.send, self.axis, bit), *earlier)
        self.values = self.keep.astype(f32) + arrived.astype(f32)
        self.split()


class SharedSum:
    def __init__(self, values, axis, order):
        self.axis = axis
        few = list(order[:2])
        self.plan = [("halve", bit) for bit in few] + [("add", bit) for bit in order[2:]]
        self.plan += [("join", bit) for bit in few[::-1]]
        self.start(*values)

    def start(self, keep, send):
        self.keep, self.send = keep, send

    def begin(self):
        kind, bit = self.plan[0] if self.plan else ("", 0)
        self.mine = (lax.axis_index(self.axis) >> bit) & 1
        if kind == "halve":
            self.keep, self.send = halves(self.values, self.mine, 0)
            self.send = self.send.astype(bf16)
        else:
            self.keep = self.send = self.values.astype(bf16)

    def step(self, *earlier):
        kind, bit = self.plan.pop(0)
        arrived = after(swap(self.send, self.axis, bit), *earlier)
        if kind == "join":
            self.values = ordered(self.mine, self.keep, arrived, 0)
        else:
            self.values = self.keep.astype(f32) + arrived.astype(f32)
        self.begin()

    def last(self, *earlier):
        _, bit = self.plan.pop(0)
        return self.keep, after(swap(self.send, self.axis, bit), *earlier)


def after(values, *earlier):
    return lax.optimization_barrier((values, earlier))[0] if earlier else values


def gather_bit(values, axis, bit, have, *earlier):
    at = len([other for other in have if other > bit])
    mine = (lax.axis_index(axis) >> bit) & 1
    arrived = after(swap(values, axis, bit), *earlier)
    have.append(bit)
    return jnp.where(
        mine == 0, jnp.stack([values, arrived], at), jnp.stack([arrived, values], at)
    )


def gather_rest(values, axis, bits, *earlier):
    codes = [code << bits[0] for code in range(1 << len(bits))]
    got = [values] + [
        lax.ppermute(values, axis, [(at, at ^ code) for at in range(lax.axis_size(axis))])
        for code in codes[1:]
    ]
    got = after(got, *earlier)
    mine = lax.axis_index(axis) >> bits[0]
    stacked = jnp.stack(got)
    return jnp.take(stacked, jnp.arange(len(codes)) ^ mine, axis=0)


def bit_orders(axis):
    bits = lax.axis_size(axis).bit_length() - 1
    first = list(range(bits))
    second = list(range(bits))
    if bits > 1:
        second[0], second[1] = 1, 0
    return first, second


def kernel_params(megabytes):
    return pltpu.CompilerParams(vmem_limit_bytes=megabytes * 1024 * 1024)


LIGHT = pl.CostEstimate(flops=1000, bytes_accessed=1000, transcendentals=0)


def whole(*shape):
    return pl.BlockSpec(shape, lambda *at: (0,) * len(shape))


def scalars():
    return pl.BlockSpec(memory_space=pltpu.SMEM)


def shaped(shape, kind):
    return jax.ShapeDtypeStruct(shape, kind)


def outer(shape, kind):
    return pltpu.HBM(shape, kind)


def held(values):
    return pltpu.with_memory_space_constraint(values, pltpu.HBM)


def split_columns(values_ref, side_ref, chunk, keep_ref, give_ref):
    for side in range(2):

        @pl.when(side_ref[0] == side)
        def _():
            for at, start in enumerate(range(0, values_ref.shape[1], 2 * chunk)):
                to = slice(at * chunk, (at + 1) * chunk)
                first = values_ref[:, start : start + chunk]
                second = values_ref[:, start + chunk : start + 2 * chunk]
                keep_ref[:, to] = second if side else first
                give_ref[:, to] = first if side else second


def norm_kernel(
    chunk, me_ref, side_ref, own_ref, over_ref, beside_ref, far_ref, mask_ref, mod_ref, weight_ref,
    keep_ref, give_ref, proj_ref, normed_s
):
    slots, rows, _ = own_ref.shape
    length = mask_ref.shape[1]

    @pl.when(pl.program_id(0) == 0)
    def _():
        for slot in range(slots):
            shift = mod_ref[slot, 0:1, :]
            scale = mod_ref[slot, 1:2, :]
            for code, block in ((0, own_ref), (2, over_ref), (1, beside_ref), (3, far_ref)):
                start = pl.multiple_of((me_ref[0] ^ code) * rows, rows)
                raw = block[slot].astype(f32)
                centred = raw - jnp.mean(raw, axis=1, keepdims=True)
                spread = jnp.mean(centred * centred, axis=1, keepdims=True)
                hat = centred * lax.rsqrt(spread + EPSILON)
                mask = mask_ref[slot, pl.ds(start, rows), :]
                normed_s[pl.ds(slot * length + start, rows), :] = (
                    mask * (hat * (1.0 + scale) + shift)
                ).astype(bf16)
        split_columns(normed_s, side_ref, chunk, keep_ref, give_ref)

    proj_ref[...] = matmul(normed_s[...], weight_ref[...]).astype(bf16)


def norm_call(me, side, blocks, mask, mods, weight, width, chunk):
    slots, rows, model = blocks[0].shape
    count = slots * mask.shape[1]
    channels = weight.shape[1]
    return pl.pallas_call(
        functools.partial(norm_kernel, chunk),
        grid=(channels // width,),
        in_specs=[scalars(), scalars()]
        + [whole(slots, rows, model)] * 4
        + [whole(*mask.shape), whole(slots, 3, model), pl.BlockSpec((model, width), lambda j: (0, j))],
        out_specs=[
            whole(count, model // 2),
            whole(count, model // 2),
            pl.BlockSpec((count, width), lambda j: (0, j)),
        ],
        out_shape=[
            shaped((count, model // 2), bf16),
            shaped((count, model // 2), bf16),
            shaped((count, channels), bf16),
        ],
        scratch_shapes=[pltpu.VMEM((count, model), bf16)],
        compiler_params=kernel_params(20),
        cost_estimate=LIGHT,
        name="norm_project",
    )(me, side, *blocks, mask, mods, held(weight))


def gate_kernel(
    chunk, me_ref, side_ref, own_ref, over_ref, beside_ref, far_ref, mask_ref, mod_ref, mine_ref,
    theirs_ref, keep_ref, give_ref, out_ref, grad_s
):
    slots, rows, _ = own_ref.shape
    length = mask_ref.shape[1]
    step = pl.program_id(0)

    @pl.when(step == 0)
    def _():
        for slot in range(slots):
            gate = mod_ref[slot, 2:3, :]
            for code, block in ((0, own_ref), (2, over_ref), (1, beside_ref), (3, far_ref)):
                start = pl.multiple_of((me_ref[0] ^ code) * rows, rows)
                mask = mask_ref[slot, pl.ds(start, rows), :]
                grad_s[pl.ds(slot * length + start, rows), :] = (
                    mask * block[slot].astype(f32) * gate
                ).astype(bf16)
        split_columns(grad_s, side_ref, chunk, keep_ref, give_ref)

    @pl.when(step < pl.num_programs(0) // 2)
    def _():
        out_ref[...] = contract_cols(grad_s[...], mine_ref[...]).astype(bf16)

    @pl.when(step >= pl.num_programs(0) // 2)
    def _():
        out_ref[...] = contract_cols(grad_s[...], theirs_ref[...]).astype(bf16)


def gate_call(me, side, blocks, mask, mods, mine, theirs, chunk):
    slots, rows, model = blocks[0].shape
    count = slots * mask.shape[1]
    quarter = mine.shape[0]
    parts = 2
    width = quarter // parts

    def out_at(j, me_ref, side_ref):
        return (0, ((me_ref[0] & 1) ^ (j // parts)) * parts + j % parts)

    fixed = lambda *shape: pl.BlockSpec(shape, lambda j, *refs: (0,) * len(shape))
    return pl.pallas_call(
        functools.partial(gate_kernel, chunk),
        grid_spec=pltpu.PrefetchScalarGridSpec(
            num_scalar_prefetch=2,
            grid=(2 * parts,),
            in_specs=[fixed(slots, rows, model)] * 4
            + [
                fixed(*mask.shape),
                fixed(slots, 3, model),
                pl.BlockSpec((width, model), lambda j, *refs: (jnp.minimum(j, parts - 1), 0)),
                pl.BlockSpec((width, model), lambda j, *refs: (jnp.maximum(j - parts, 0), 0)),
            ],
            out_specs=[
                fixed(count, model // 2),
                fixed(count, model // 2),
                pl.BlockSpec((count, width), out_at),
            ],
            scratch_shapes=[pltpu.VMEM((count, model), bf16)],
        ),
        out_shape=[
            shaped((count, model // 2), bf16),
            shaped((count, model // 2), bf16),
            outer((count, 2 * quarter), bf16),
        ],
        compiler_params=kernel_params(20),
        cost_estimate=LIGHT,
        name="gate_project",
    )(me, side, *blocks, mask, mods, mine, theirs)


def pair_kernel(first_ref, second_ref, third_ref, fourth_ref, left_ref, right_ref):
    left_ref[...] = (first_ref[...].astype(f32) + second_ref[...].astype(f32)).astype(bf16)
    right_ref[...] = (third_ref[...].astype(f32) + fourth_ref[...].astype(f32)).astype(bf16)


def pair_call(first, second, third, fourth, blocks):
    rows, cols = first.shape
    block = pl.BlockSpec((rows // blocks, cols), lambda i: (i, 0))
    return pl.pallas_call(
        pair_kernel,
        grid=(blocks,),
        in_specs=[block] * 4,
        out_specs=[block] * 2,
        out_shape=[shaped((rows, cols), bf16)] * 2,
        compiler_params=kernel_params(10),
        cost_estimate=LIGHT,
        name="pair_sums",
    )(held(first), held(second), held(third), held(fourth))


def join_kernel(keep_ref, there_ref, out_ref):
    out_ref[...] = (keep_ref[...].astype(f32) + there_ref[...].astype(f32)).astype(bf16)


def join_call(keep, there):
    return pl.pallas_call(
        join_kernel,
        out_shape=shaped(keep.shape, bf16),
        compiler_params=kernel_params(8),
        cost_estimate=LIGHT,
        name="join_sums",
    )(keep, there)


def pack_kernel(side_ref, conv_ref, scan_ref, keep_ref, send_ref, total):
    count = conv_ref.shape[0]
    rows = keep_ref.shape[0]
    total[0:count, :] = conv_ref[...]
    total[count:, :] = scan_ref[...]
    side = side_ref[0]
    keep_ref[...] = total[pl.ds(pl.multiple_of(side * rows, rows), rows), :]
    send_ref[...] = total[pl.ds(pl.multiple_of((1 - side) * rows, rows), rows), :].astype(bf16)


def pack_call(side, conv, scan):
    cols = conv.shape[1]
    rows = (conv.shape[0] + scan.shape[0]) // 2
    return pl.pallas_call(
        pack_kernel,
        in_specs=[scalars(), whole(*conv.shape), whole(*scan.shape)],
        out_specs=[whole(rows, cols)] * 2,
        grid=(1,),
        out_shape=[shaped((rows, cols), f32), shaped((rows, cols), bf16)],
        scratch_shapes=[pltpu.VMEM((2 * rows, cols), f32)],
        compiler_params=kernel_params(14),
        cost_estimate=LIGHT,
        name="pack_sums",
    )(side, conv, scan)


def unpack_kernel(
    spots, side_ref, keep_ref, there_ref, xproj_ref, taps_ref, dtproj_ref, rates_ref, vec_ref, total
):
    rows = keep_ref.shape[0]
    cols, tap_count, base, rank, states = spots
    side = side_ref[0]
    total[pl.ds(pl.multiple_of(side * rows, rows), rows), :] = keep_ref[...].astype(f32)
    total[pl.ds(pl.multiple_of((1 - side) * rows, rows), rows), :] = there_ref[...].astype(f32)
    dtproj_ref[...] = total[base : base + rank, :]
    taps_ref[...] = total[cols : cols + tap_count, :]
    first = base + rank
    rates_ref[...] = total[first : first + states, :]
    vec_ref[...] = jnp.zeros_like(vec_ref)
    vec_ref[0:1, :] = total[cols + tap_count : cols + tap_count + 1, :]
    vec_ref[1:3, :] = total[first + states : first + states + 2, :]
    for at in range(0, total.shape[1], 128):
        here = slice(at, at + 128)
        xproj_ref[here, :] = jnp.transpose(total[0:cols, here])


def unpack_call(side, keep, there, cols, tap_count, base, rank, states):
    rows, channels = keep.shape
    shapes = [(channels, cols), (tap_count, channels), (rank, channels), (states, channels)]
    shapes += [(8, channels)]
    return pl.pallas_call(
        functools.partial(unpack_kernel, (cols, tap_count, base, rank, states)),
        grid=(1,),
        in_specs=[scalars(), whole(rows, channels), whole(rows, channels)],
        out_specs=[whole(*shape) for shape in shapes],
        out_shape=[shaped(shape, f32) for shape in shapes],
        scratch_shapes=[pltpu.VMEM((2 * rows, channels), f32)],
        compiler_params=kernel_params(16),
        cost_estimate=LIGHT,
        name="unpack_sums",
    )(side, keep, there)


def fold_kernel(rows, me_ref, *refs):
    mine_ref, sent_ref = refs[-2:]
    count = len(refs) // 2 - 1
    items = refs[0].shape[0] // rows // 2
    chip = me_ref[0] >> 1
    for at in range(count):
        keep_ref, there_ref = refs[at], refs[count + at]
        for item in range(items):
            for which, out_ref in ((chip, mine_ref), (1 - chip, sent_ref)):
                here = pl.ds(pl.multiple_of((2 * item + which) * rows, rows), rows)
                total = keep_ref[here, :] + there_ref[here, :].astype(f32)
                out_ref[at * items + item] = total.astype(out_ref.dtype)


def fold_call(me, keeps, theres, rows):
    count, model = keeps[0].shape
    slots = len(keeps) * count // rows // 2
    return pl.pallas_call(
        functools.partial(fold_kernel, rows),
        grid=(1,),
        in_specs=[scalars()] + [whole(count, model)] * (2 * len(keeps)),
        out_specs=[whole(slots, rows, model)] * 2,
        out_shape=[shaped((slots, rows, model), f32), shaped((slots, rows, model), bf16)],
        compiler_params=kernel_params(14),
        cost_estimate=LIGHT,
        name="fold_rows",
    )(me, *keeps, *theres)


def rows_kernel(
    tokens_ref, cot_ref, mask_ref, mod_ref, branch_ref, branch_far_ref, norm_ref, norm_far_ref,
    mixed_ref, grad_ref, mod_grad_ref
):
    raw = tokens_ref[...].astype(f32)
    mask = mask_ref[...]
    gate = mod_ref[2:3, :]
    branch = branch_ref[...] + branch_far_ref[...].astype(f32)
    mixed_ref[...] = mask * (raw + gate * branch)
    res_grad = mask * cot_ref[...].astype(f32)
    centred = raw - jnp.mean(raw, axis=1, keepdims=True)
    spread = jnp.mean(centred * centred, axis=1, keepdims=True)
    inverse = lax.rsqrt(spread + EPSILON)
    hat = centred * inverse
    normed_grad = mask * (norm_ref[...] + norm_far_ref[...].astype(f32))
    q = normed_grad * (1.0 + mod_ref[1:2, :])
    grad_ref[...] = res_grad + inverse * (
        q - jnp.mean(q, axis=1, keepdims=True) - hat * jnp.mean(q * hat, axis=1, keepdims=True)
    )
    mod_grad_ref[0:1, :] = jnp.sum(normed_grad, axis=0, keepdims=True)
    mod_grad_ref[1:2, :] = jnp.sum(normed_grad * hat, axis=0, keepdims=True)
    mod_grad_ref[2:3, :] = jnp.sum(res_grad * branch, axis=0, keepdims=True)


def rows_call(tokens, cot, mask, mods, branch, branch_far, norm, norm_far):
    slots, rows, model = tokens.shape
    row = pl.BlockSpec((None, rows, model), lambda i: (i, 0, 0))
    mod = pl.BlockSpec((None, 3, model), lambda i: (i, 0, 0))
    return pl.pallas_call(
        rows_kernel,
        grid=(slots,),
        in_specs=[row, row, pl.BlockSpec((None, rows, 1), lambda i: (i, 0, 0)), mod, row, row, row, row],
        out_specs=[row, row, mod],
        out_shape=[
            shaped((slots, rows, model), f32),
            shaped((slots, rows, model), f32),
            shaped((slots, 3, model), f32),
        ],
        compiler_params=kernel_params(14),
        cost_estimate=LIGHT,
        name="owned_rows",
    )(tokens, cot, mask, mods, branch, branch_far, norm, norm_far)


def pick_rows(values_ref, parity, chips, rows):
    blocks = []
    for at in range(values_ref.shape[0] // rows // 2):
        start = pl.multiple_of((2 * at + parity) * rows, rows)
        blocks.append(values_ref[pl.ds(start, rows), :])
    return jnp.concatenate(blocks, 0)


def branch_kernel(rows, flip_ref, values_ref, weight_ref, keep_ref, send_ref):
    core = flip_ref[0]
    keep_ref[...] = matmul(pick_rows(values_ref, core, 2, rows), weight_ref[...])
    send_ref[...] = matmul(pick_rows(values_ref, 1 - core, 2, rows), weight_ref[...]).astype(bf16)


def branch_call(flip, values, weight, rows, width):
    count, depth = values.shape
    model = weight.shape[1]
    out = [shaped((count // 2, model), f32), shaped((count // 2, model), bf16)]
    return pl.pallas_call(
        functools.partial(branch_kernel, rows),
        grid=(model // width,),
        in_specs=[
            pl.BlockSpec(memory_space=pltpu.SMEM),
            pl.BlockSpec((count, depth), lambda j: (0, 0)),
            pl.BlockSpec((depth, width), lambda j: (0, j)),
        ],
        out_specs=[pl.BlockSpec((count // 2, width), lambda j: (0, j))] * 2,
        out_shape=out,
        compiler_params=kernel_params(10),
        cost_estimate=pl.CostEstimate(flops=1000, bytes_accessed=1000, transcendentals=0),
        name="branch_rows",
    )(flip, values, weight)


def proj_back_kernel(rows, slots, flip_ref, *refs):
    x_refs = refs[:slots]
    z_ref, weight_ref, there_ref, keep_ref, send_ref, x_s, z_s, mine_s = refs[slots:]
    core = flip_ref[0]
    half = there_ref.shape[1]
    length = x_refs[0].shape[0]

    def place(x_to, z_to, mine):
        for slot in range(slots):
            x_to[slot * length : (slot + 1) * length, :] = x_refs[slot][...]
        z_to[...] = z_ref[...]
        mine_s[...] = mine

    pl.when(core == 0)(lambda: place(x_s, z_s, weight_ref[:, :half]))
    pl.when(core == 1)(lambda: place(z_s, x_s, weight_ref[:, half:]))
    for parity, out_ref in ((core, keep_ref), (1 - core, send_ref)):
        total = contract_cols(pick_rows(x_s, parity, 2, rows), mine_s[...]) + contract_cols(
            pick_rows(z_s, parity, 2, rows), there_ref[...]
        )
        out_ref[...] = total.astype(out_ref.dtype)


def proj_back_call(flip, xs, z, weight, there, rows, width):
    length, depth = xs[0].shape
    count = z.shape[0]
    model = there.shape[0]
    return pl.pallas_call(
        functools.partial(proj_back_kernel, rows, len(xs)),
        grid=(model // width,),
        in_specs=[scalars()]
        + [whole(length, depth)] * len(xs)
        + [
            whole(count, depth),
            pl.BlockSpec((width, 2 * depth), lambda j: (j, 0)),
            pl.BlockSpec((width, depth), lambda j: (j, 0)),
        ],
        out_specs=[pl.BlockSpec((count // 2, width), lambda j: (0, j))] * 2,
        out_shape=[shaped((count // 2, model), f32), shaped((count // 2, model), bf16)],
        scratch_shapes=[pltpu.VMEM((count, depth), bf16)] * 2 + [pltpu.VMEM((width, depth), bf16)],
        compiler_params=kernel_params(18),
        cost_estimate=LIGHT,
        name="proj_back",
    )(flip, *xs, z, held(weight), held(there))


def cond_kernel(mod_ref, weight_ref, cond_ref, out_ref):
    value = cond_ref[...].astype(f32)
    sig = jax.nn.sigmoid(value)
    out_ref[...] = contract_cols(mod_ref[...], weight_ref[...]) * sig * (1.0 + value * (1.0 - sig))


def cond_call(mods, weight, cond, start, count):
    slots, columns = mods.shape
    width = 256 if count % 256 == 0 else 128
    first = start // width
    return pl.pallas_call(
        cond_kernel,
        grid=(count // width,),
        in_specs=[
            whole(slots, columns),
            pl.BlockSpec((width, columns), lambda j: (first + j, 0)),
            pl.BlockSpec((slots, width), lambda j: (0, first + j)),
        ],
        out_specs=pl.BlockSpec((slots, width), lambda j: (0, j)),
        out_shape=shaped((slots, count), f32),
        compiler_params=kernel_params(14),
        cost_estimate=LIGHT,
        name="cond_rows",
    )(mods, held(weight), cond)


def tap_sum(pad, taps_ref, here, sign, length):
    taps = taps_ref.shape[0] - 1
    total = pad[MARGIN : MARGIN + length, :] * taps_ref[taps - 1 : taps, here]
    for by in range(1, taps):
        start = MARGIN - sign * by
        total = total + pad[start : start + length, :] * taps_ref[taps - 1 - by : taps - by, here]
    return total


def conv_kernel(
    flip_ref, own_ref, other_ref, mask_ref, taps_ref, xproj_ref, x_ref, z_ref, u_ref, slope_ref,
    dbl_ref, pads
):
    step = pl.program_id(1)
    length, width = own_ref.shape
    taps = taps_ref.shape[0] - 1
    flip = flip_ref[0]

    def run(flipped):
        x_from, z_from = (other_ref, own_ref) if flipped else (own_ref, other_ref)
        x_ref[...] = x_from[...]
        z_ref[...] = z_from[...]
        mask = jnp.broadcast_to(mask_ref[...], (length, 128))
        for tile in range(width // 128):
            here = slice(tile * 128, (tile + 1) * 128)
            pad = pads.at[tile]
            pad[0:MARGIN, :] = jnp.zeros((MARGIN, 128), f32)
            pad[MARGIN + length :, :] = jnp.zeros((MARGIN, 128), f32)
            pad[MARGIN : MARGIN + length, :] = x_from[:, here].astype(f32)
            conv = taps_ref[taps : taps + 1, here] + tap_sum(pad, taps_ref, here, -1 if flipped else 1, length)
            sig = 0.5 + 0.5 * jnp.tanh(0.5 * conv)
            u_ref[:, here] = (mask * (conv * sig)).astype(bf16)
            slope_ref[:, here] = mask * (sig * (1.0 + conv * (1.0 - sig)))

    pl.when(flip == 0)(lambda: run(False))
    pl.when(flip == 1)(lambda: run(True))
    part = matmul(u_ref[...], xproj_ref[...])

    @pl.when(step == 0)
    def _():
        dbl_ref[...] = part

    @pl.when(step > 0)
    def _():
        dbl_ref[...] += part


def conv_back_kernel(
    flip_ref, x_ref, u_ref, slope_ref, taps_ref, xproj_ref, us_ref, dg_ref, prev_ref, keep_ref,
    send_ref, packed_ref, grad_s, pads, grad_pads
):
    length, width = x_ref.shape
    flip = flip_ref[0]
    taps = taps_ref.shape[0] - 1
    dg = dg_ref[...]
    cols = dg.shape[1]
    grad_s[...] = (us_ref[...] + contract_cols(dg, xproj_ref[...])) * slope_ref[...]
    packed_ref[0:cols, :] = prev_ref[0:cols, :] + matmul(
        jnp.transpose(dg.astype(f32)).astype(bf16), u_ref[...]
    )
    rest = packed_ref.shape[0] - cols - taps - 1
    packed_ref[cols + taps + 1 :, :] = jnp.zeros((rest, width), f32)

    def run(flipped, out_ref):
        sign = -1 if flipped else 1
        for tile in range(width // 128):
            here = slice(tile * 128, (tile + 1) * 128)
            pad, grad_pad = pads.at[tile], grad_pads.at[tile]
            for ref in (pad, grad_pad):
                ref[0:MARGIN, :] = jnp.zeros((MARGIN, 128), f32)
                ref[MARGIN + length :, :] = jnp.zeros((MARGIN, 128), f32)
            conv_grad = grad_s[:, here]
            pad[MARGIN : MARGIN + length, :] = x_ref[:, here].astype(f32)
            grad_pad[MARGIN : MARGIN + length, :] = conv_grad
            for by in range(taps):
                start = MARGIN - sign * by
                row = cols + taps - 1 - by
                packed_ref[row : row + 1, here] = prev_ref[row : row + 1, here] + jnp.sum(
                    conv_grad * pad[start : start + length, :], axis=0, keepdims=True
                )
            row = cols + taps
            packed_ref[row : row + 1, here] = prev_ref[row : row + 1, here] + jnp.sum(
                conv_grad, axis=0, keepdims=True
            )
            out_ref[:, here] = tap_sum(grad_pad, taps_ref, here, -sign, length).astype(bf16)

    for flipped in (False, True):
        for block in range(2):
            out_ref = keep_ref if block == int(flipped) else send_ref
            pl.when((flip == int(flipped)) & (pl.program_id(0) == block))(
                functools.partial(run, flipped, out_ref)
            )


def conv_call(flip, own, other, mask, taps, xproj, width):
    slots, length = mask.shape[:2]
    channels = own.shape[1]
    cols = xproj.shape[1]
    block = pl.BlockSpec((length, width), lambda i, j: (i, j))
    return pl.pallas_call(
        conv_kernel,
        grid=(slots, channels // width),
        in_specs=[
            scalars(),
            block,
            block,
            pl.BlockSpec((None, length, 1), lambda i, j: (i, 0, 0)),
            pl.BlockSpec((taps.shape[0], width), lambda i, j: (0, j)),
            pl.BlockSpec((width, cols), lambda i, j: (j, 0)),
        ],
        out_specs=[block] * 4 + [pl.BlockSpec((length, cols), lambda i, j: (i, 0))],
        out_shape=[outer((slots * length, channels), bf16)] * 3
        + [outer((slots * length, channels), f32), outer((slots * length, cols), f32)],
        scratch_shapes=[pltpu.VMEM((width // 128, length + 2 * MARGIN, 128), f32)],
        compiler_params=kernel_params(16),
        cost_estimate=LIGHT,
        name="conv_forward",
    )(flip, own, other, mask, taps, xproj)


def conv_back_call(flip, slot, length, x, u, slope, taps, xproj, us, dg, prev):
    channels = x.shape[1]
    cols = xproj.shape[1]
    width = channels // 2
    rows = prev.shape[0]
    item = pl.BlockSpec((length, width), lambda j: (slot, j))
    pads = pltpu.VMEM((width // 128, length + 2 * MARGIN, 128), f32)
    return pl.pallas_call(
        conv_back_kernel,
        grid=(2,),
        in_specs=[
            scalars(),
            item,
            item,
            item,
            pl.BlockSpec((taps.shape[0], width), lambda j: (0, j)),
            pl.BlockSpec((width, cols), lambda j: (j, 0)),
            pl.BlockSpec((length, width), lambda j: (0, j)),
            whole(length, cols),
            pl.BlockSpec((rows, width), lambda j: (0, j)),
        ],
        out_specs=[
            whole(length, width),
            whole(length, width),
            pl.BlockSpec((rows, width), lambda j: (0, j)),
        ],
        out_shape=[
            shaped((length, width), bf16),
            shaped((length, width), bf16),
            shaped((rows, channels), f32),
        ],
        scratch_shapes=[pltpu.VMEM((length, width), f32), pads, pads],
        compiler_params=kernel_params(18),
        cost_estimate=LIGHT,
        name="conv_backward",
    )(flip, held(x), held(u), held(slope), taps, xproj, held(us), dg, prev)


def spread(dbl_ref, first, b_wide, c_wide, rows_s, states):
    length, cols = dbl_ref.shape
    rest = dbl_ref[...]
    row = lax.broadcasted_iota(jnp.int32, (cols, cols), 0)
    col = lax.broadcasted_iota(jnp.int32, (cols, cols), 1)
    rows = jnp.zeros((length, cols), f32)
    for part in range(3):
        piece = rest.astype(bf16)
        rest = rest - piece.astype(f32)
        pick = ((row == first + col % (2*states)) & (col // (2*states) == part))
        rows = rows + matmul(piece, jnp.where(pick, 1.0, 0.0).astype(bf16))
    rows_s[...] = rows
    which = lax.broadcasted_iota(jnp.int32, (states, cols), 0)
    lane = lax.broadcasted_iota(jnp.int32, (states, cols), 1)
    mine = jnp.where(lane % states == which, 1.0, 0.0)
    row = lax.broadcasted_iota(jnp.int32, (cols, 2*cols), 0)
    col = lax.broadcasted_iota(jnp.int32, (cols, 2*cols), 1)
    wide = jnp.where((row % (2*states)) // states == col // cols, 1.0, 0.0).astype(bf16)
    def some(at, _):
        left = [(mine*jnp.broadcast_to(rows_s[pl.ds(at*CHUNK+t, 1), :], (states, cols))).astype(bf16) for t in range(CHUNK)]
        got = matmul(jnp.concatenate(left, 0), wide)
        here = pl.ds(pl.multiple_of(at*CHUNK*states, CHUNK*states), CHUNK*states)
        b_wide[here, :] = got[:, :cols]
        c_wide[here, :] = got[:, cols:]
        return 0
    lax.fori_loop(0, length//CHUNK, some, 0, unroll=4)

def tiles_of(values):
    return [values[:, at:at+128] for at in range(0, values.shape[1], 128)]

def fold(values, tmp, tt, states):
    for at, tile in enumerate(tiles_of(values)):
        total = tile[:8]
        for part in range(1, states//8):
            total = total + tile[part*8:(part+1)*8]
        tmp[at, pl.ds(tt//8*64 + tt%8, 8, stride=8), :] = total

def add_tiles(values):
    parts = tiles_of(values)
    total = parts[0]
    for part in parts[1:]:
        total = total + part
    return total

def unfold(tmp, out, base):
    for at in range(out.shape[1]//128):
        for part in range(CHUNK//8):
            acc = tmp[at, part*64:part*64+8, :]
            for row in range(1, 8):
                acc = acc + tmp[at, part*64+row*8:part*64+row*8+8, :]
            out[pl.ds(pl.multiple_of(base+part*8, 8), 8), at*128:(at+1)*128] = acc

def collect(acc, tmp, out, length, states):
    which = lax.broadcasted_iota(jnp.int32, (states, 128), 0)
    lane = lax.broadcasted_iota(jnp.int32, (states, 128), 1)
    mine = which == lane
    def some(at, _):
        base = pl.multiple_of(at*CHUNK, CHUNK)
        for tt in range(CHUNK):
            sums = jnp.sum(acc[pl.ds((base+tt)*states, states), :], axis=1, keepdims=True)
            fold(jnp.where(mine, sums, 0.0), tmp, tt, states)
        unfold(tmp, out, base)
        return 0
    lax.fori_loop(0, length//CHUNK, some, 0, unroll=4)

def fwd_kernel(states, flip_ref, dbl_ref, dtp_ref, vec_ref, rate2_ref, u_ref, z_ref, gg_ref,
               gate_keep, gate_send, z_keep, z_send, delta_ref, yg_ref, prior_ref, cout_ref,
               b_wide, c_wide, drive_s, sig_s, y_s, y_tmp, c_acc, rows_s):
    step = pl.program_id(1)
    length, width = u_ref.shape
    rank = dtp_ref.shape[0]
    group = CHUNK*states
    chunks = length//CHUNK
    flip = flip_ref[0]
    @pl.when(step == 0)
    def _():
        spread(dbl_ref, rank, b_wide, c_wide, rows_s, states)
        c_acc[...] = jnp.zeros_like(c_acc)
    low = dbl_ref[:, :rank].astype(bf16)
    pre = matmul(low, dtp_ref[...]) + vec_ref[0:1, :]
    delta = jnp.maximum(pre, 0.0) + jnp.log1p(jnp.exp(-jnp.abs(pre)))
    delta_ref[...] = delta
    drive_s[...] = delta * u_ref[...].astype(f32)
    z = z_ref[...].astype(f32)
    sig = 0.5 + 0.5*jnp.tanh(0.5*z)
    sig_s[...] = sig
    yg_ref[...] = gg_ref[...].astype(f32) * (z * sig)
    def run(flipped):
        def ahead(chunk, state):
            place = chunks-1-chunk if flipped else chunk
            base = pl.multiple_of(place*CHUNK, CHUNK)
            wide = pl.multiple_of(place*group, group)
            for at in range(CHUNK):
                tt = CHUNK-1-at if flipped else at
                t = base + tt
                here = pl.ds(wide + tt*states, states)
                d = jnp.broadcast_to(delta_ref[pl.ds(t,1),:], (states,width))
                x = jnp.broadcast_to(drive_s[pl.ds(t,1),:], (states,width))
                g = jnp.broadcast_to(yg_ref[pl.ds(t,1),:], (states,width))
                b = jnp.concatenate([b_wide[here,:]]*(width//128), axis=1)
                c = jnp.concatenate([c_wide[here,:]]*(width//128), axis=1)
                prior = jnp.exp2(d*rate2_ref[...])*state
                state = prior + x*b
                prior_ref[here,:] = prior.astype(bf16)
                fold(state*c, y_tmp, tt, states)
                c_acc[here,:] += add_tiles(state*g)
            unfold(y_tmp, y_s, base)
            return state
        lax.fori_loop(0, chunks, ahead, jnp.zeros((states,width), f32))
    pl.when(flip == 0)(lambda: run(False))
    pl.when(flip == 1)(lambda: run(True))
    u = u_ref[...].astype(f32)
    z = z_ref[...].astype(f32)
    sig = sig_s[...]
    y = y_s[...] + vec_ref[1:2,:]*u
    gated = (y*(z*sig)).astype(bf16)
    zg = (gg_ref[...].astype(f32)*y*(sig*(1.0+z*(1.0-sig)))).astype(bf16)
    half = gate_keep.shape[1]
    for at in range(2*half//width):
        for core in range(2):
            def put(at=at, core=core):
                for side in range(2):
                    low, high = max(at*width, side*half), min((at+1)*width, (side+1)*half)
                    if low < high:
                        to = slice(low-side*half, high-side*half)
                        of = slice(low-at*width, high-at*width)
                        (gate_keep if side == core else gate_send)[:, to] = gated[:, of]
                        (z_keep if side == core else z_send)[:, to] = zg[:, of]
            pl.when((step == at) & (flip == core))(put)
    @pl.when(step == pl.num_programs(1)-1)
    def _():
        collect(c_acc, y_tmp, rows_s, length, states)
        cout_ref[...] = rows_s[:, :states]

def bwd_kernel(states, flip_ref, dbl_ref, dtp_ref, vec_ref, rate2_ref, u_ref, delta_ref, yg_ref, prior_ref, cout_ref, prev_ref,
               us_ref, part_ref, packed_ref,
               b_wide, c_wide, drive_s, r_s, w_s, low_t, rank_s, r_tmp, w_tmp, b_acc, rows_s):
    step = pl.program_id(0)
    length, width = u_ref.shape
    rank = dtp_ref.shape[0]
    group = CHUNK*states
    chunks = length//CHUNK
    flip = flip_ref[0]
    @pl.when(step == 0)
    def _():
        low_t[...] = jnp.transpose(dbl_ref[...])[:rank,:].astype(bf16)
        spread(dbl_ref, rank, b_wide, c_wide, rows_s, states)
        b_acc[...] = jnp.zeros_like(b_acc)
        rank_s[...] = jnp.zeros_like(rank_s)
    u = u_ref[...].astype(f32)
    drive_s[...] = delta_ref[...]*u
    def run(flipped):
        def back(chunk, carry):
            carried, total = carry
            place = chunk if flipped else chunks-1-chunk
            base = pl.multiple_of(place*CHUNK, CHUNK)
            wide = pl.multiple_of(place*group, group)
            for at in range(CHUNK):
                tt = at if flipped else CHUNK-1-at
                t = base + tt
                here = pl.ds(wide + tt*states, states)
                d = jnp.broadcast_to(delta_ref[pl.ds(t,1),:], (states,width))
                x = jnp.broadcast_to(yg_ref[pl.ds(t,1),:], (states,width))
                e = jnp.broadcast_to(drive_s[pl.ds(t,1),:], (states,width))
                b = jnp.concatenate([b_wide[here,:]]*(width//128), axis=1)
                c = jnp.concatenate([c_wide[here,:]]*(width//128), axis=1)
                power = d*rate2_ref[...]
                adj = carried + x*c
                moved = (adj*prior_ref[here,:].astype(f32))*power
                total = total + moved
                fold(moved, w_tmp, tt, states)
                fold(adj*b, r_tmp, tt, states)
                b_acc[here,:] += add_tiles(adj*e)
                carried = jnp.exp2(power)*adj
            unfold(w_tmp, w_s, base)
            unfold(r_tmp, r_s, base)
            return carried, total
        zero = jnp.zeros((states,width), f32)
        _, total = lax.fori_loop(0, chunks, back, (zero, zero))
        packed_ref[rank:rank+states,:] = prev_ref[rank:rank+states,:] + total*(1.0/LOG2E)
    pl.when(flip == 0)(lambda: run(False))
    pl.when(flip == 1)(lambda: run(True))
    yg = yg_ref[...]
    r = r_s[...]
    delta = delta_ref[...]
    us_ref[...] = delta*r + vec_ref[1:2,:]*yg
    low = dbl_ref[:, :rank].astype(bf16)
    pre = matmul(low, dtp_ref[...]) + vec_ref[0:1,:]
    sig = jnp.exp(pre-delta)
    ratio = jnp.where(delta > 1e-30, sig/jnp.maximum(delta, 1e-30), 1.0)
    pre_grad = w_s[...]*(1.0/LOG2E)*ratio + u*r*sig
    pre_low = pre_grad.astype(bf16)
    rank_s[...] += contract_cols(pre_low, dtp_ref[...])
    packed_ref[0:rank,:] = prev_ref[0:rank,:] + matmul(low_t[...], pre_low)
    packed_ref[rank+states:rank+states+1,:] = prev_ref[rank+states:rank+states+1,:] + jnp.sum(pre_grad, axis=0, keepdims=True)
    packed_ref[rank+states+1:rank+states+2,:] = prev_ref[rank+states+1:rank+states+2,:] + jnp.sum(yg*u, axis=0, keepdims=True)
    rest = packed_ref.shape[0]-rank-states-2
    packed_ref[rank+states+2:,:] = jnp.zeros((rest,width), f32)
    @pl.when(step == pl.num_programs(0)-1)
    def _():
        collect(b_acc, r_tmp, rows_s, length, states)
        part_ref[...] = jnp.concatenate([rank_s[...], rows_s[:, :states], cout_ref[...]], axis=1)


def forward_call(flip, dbl, dtproj, vec, rates2, u, z, gg, slots, width):
    count, channels = u.shape
    length = count // slots
    half = channels // 2
    states, rank, cols = rates2.shape[0], dtproj.shape[0], dbl.shape[1]
    weight = lambda rows: pl.BlockSpec((rows, width), lambda i, j: (0, j))
    block = lambda rows: pl.BlockSpec((rows, width), lambda i, j: (i, j))
    item = lambda wide: pl.BlockSpec((length, wide), lambda i, j: (i, 0))
    return pl.pallas_call(
        functools.partial(fwd_kernel, states),
        grid=(slots, channels // width),
        in_specs=[scalars(), item(cols), weight(rank), weight(2), weight(states)] + [block(length)] * 3,
        out_specs=[item(half)] * 4 + [block(length)] * 2 + [block(length * states), item(states)],
        out_shape=[outer((count, half), bf16)] * 4
        + [outer((count, channels), f32)] * 2
        + [outer((count * states, channels), bf16), shaped((count, states), f32)],
        scratch_shapes=[
            pltpu.VMEM((length * states, 128), f32),
            pltpu.VMEM((length * states, 128), f32),
            pltpu.VMEM((length, width), f32),
            pltpu.VMEM((length, width), f32),
            pltpu.VMEM((length, width), f32),
            pltpu.VMEM((width // 128, CHUNK * 8, 128), f32),
            pltpu.VMEM((length * states, 128), f32),
            pltpu.VMEM((length, cols), f32),
        ],
        compiler_params=kernel_params(40),
        cost_estimate=pl.CostEstimate(
            flops=32000000000, bytes_accessed=40000000, transcendentals=14000000
        ),
        name="scan_forward",
    )(flip, dbl, dtproj, vec, rates2, held(u), held(z), held(gg))


def backward_call(flip, slot, slots, dbl, dtproj, vec, rates2, u, delta, yg, prior, cout, prev, width):
    count, channels = u.shape
    length = count // slots
    states, rank, cols = rates2.shape[0], dtproj.shape[0], dbl.shape[1]
    rows = prev.shape[0]
    weight = lambda rows: pl.BlockSpec((rows, width), lambda j: (0, j))
    block = lambda rows: pl.BlockSpec((rows, width), lambda j: (slot, j))
    item = lambda wide: pl.BlockSpec((length, wide), lambda j: (slot, 0))
    return pl.pallas_call(
        functools.partial(bwd_kernel, states),
        grid=(channels // width,),
        in_specs=[scalars(), item(cols), weight(rank), weight(2), weight(states)]
        + [block(length)] * 3
        + [block(length * states), item(states), weight(rows)],
        out_specs=[weight(length), whole(length, cols), weight(rows)],
        out_shape=[
            outer((length, channels), f32),
            shaped((length, cols), f32),
            shaped((rows, channels), f32),
        ],
        scratch_shapes=[
            pltpu.VMEM((length * states, 128), f32),
            pltpu.VMEM((length * states, 128), f32),
            pltpu.VMEM((length, width), f32),
            pltpu.VMEM((length, width), f32),
            pltpu.VMEM((length, width), f32),
            pltpu.VMEM((rank, length), bf16),
            pltpu.VMEM((length, rank), f32),
            pltpu.VMEM((width // 128, CHUNK * 8, 128), f32),
            pltpu.VMEM((width // 128, CHUNK * 8, 128), f32),
            pltpu.VMEM((length * states, 128), f32),
            pltpu.VMEM((length, cols), f32),
        ],
        compiler_params=kernel_params(40),
        cost_estimate=pl.CostEstimate(
            flops=22000000000, bytes_accessed=20000000, transcendentals=7000000
        ),
        name="scan_backward",
    )(flip, dbl, dtproj, vec, rates2, held(u), held(delta), held(yg), held(prior), cout, prev)


def local(
    tokens,
    cond,
    counts,
    valid,
    ada_weight,
    ada_bias,
    in_weight,
    conv_weight,
    conv_bias,
    xproj_weight,
    dtproj_weight,
    dt_bias,
    a_log,
    skip_gain,
    out_weight,
    cotangent,
):
    slot_count, shard_rows, model = tokens.shape
    dirs = lax.axis_size("dir")
    dps = lax.axis_size("dp")
    me = lax.axis_index("dir")
    dp_index = lax.axis_index("dp")
    core = me & 1
    half = in_weight.shape[1] // 2
    rank = dtproj_weight.shape[0]
    states = a_log.shape[1]
    tap_count = conv_weight.shape[1]
    cols = xproj_weight.shape[1]
    slots = range(slot_count)
    width = 512 if dt_bias.shape[0] % 512 == 0 else 128
    first, second = bit_orders("dp")
    z_bit, out_bit = first[0], second[0]
    scalar = lambda value: value.astype(jnp.int32).reshape(1)
    flip, me_ref = scalar(core), scalar(me)
    z_side, out_side = scalar((dp_index >> z_bit) & 1), scalar((dp_index >> out_bit) & 1)

    live_slots = (jnp.arange(slot_count) < counts[0]).astype(f32)
    full_mask = valid.astype(f32) * live_slots[:, None]
    mask_cols = full_mask[:, :, None]
    local_mask = lax.dynamic_slice_in_dim(full_mask, me * shard_rows, shard_rows, 1)[:, :, None]

    def gather_rows(block, *earlier):
        over = after(swap(block, "dir", 1), *earlier)
        return block, over, swap(block, "dir", 0), swap(over, "dir", 0)

    cond_act = jax.nn.silu(cond.astype(f32)).astype(bf16)
    modulation = matmul(cond_act, ada_weight) + ada_bias.astype(f32)[None, :]
    mods = modulation.reshape(slot_count, 3, model)
    token_blocks = gather_rows(tokens, modulation)
    out_there = swap(out_weight, "dir", 0)

    taps = jnp.concatenate(
        [jnp.transpose(conv_weight.astype(f32)), conv_bias.astype(f32)[None, :]], 0
    )
    vec = jnp.stack([dt_bias, skip_gain])
    rates2 = -jnp.exp(jnp.transpose(a_log)) * LOG2E

    left_mine, left_give, own = norm_call(
        me_ref,
        z_side,
        token_blocks,
        mask_cols,
        mods,
        in_weight,
        width,
        model // dps << z_bit,
    )
    in_send = lax.dynamic_slice_in_dim(after(in_weight, left_mine), (1 - core) * half, half, 1)
    in_there = swap(in_send, "dir", 0)
    other = after(swap(own, "dir", 0), in_send)
    x, z, u, slope, part = conv_call(flip, own, other, mask_cols, taps, xproj_weight, half)
    part_there = swap(part, "dir", 1)
    cot_blocks = gather_rows(cotangent, part)
    branch_mine, branch_give, gg = gate_call(
        me_ref,
        out_side,
        cot_blocks,
        mask_cols,
        after(mods, part),
        out_weight,
        out_there,
        model // dps << out_bit,
    )
    left_there = swap(left_give, "dp", z_bit)
    branch_there = swap(branch_give, "dp", out_bit)
    dbl = part + after(part_there, gg)
    gate_keep, gate_send, z_keep, z_send, *saved = forward_call(
        flip, dbl, dtproj_weight, vec, rates2, u, z, gg, slot_count, width
    )
    gate_send, z_send = after((gate_send, z_send), left_there, branch_there)
    gate_all, z_all = pair_call(
        gate_keep, swap(gate_send, "dir", 0), z_keep, swap(z_send, "dir", 0), slot_count
    )
    gate_there = swap(gate_all, "dp", out_bit)
    z_there = swap(z_all, "dp", z_bit)

    rows_keep, rows_give = branch_call(flip, gate_all, out_weight, shard_rows, width)
    rows_there = swap(rows_give, "dir", 0)

    rest = lambda out: [bit for bit in first if bit != out]
    scan_rows = -(-(rank + states + 2) // 8) * 8
    packed = jnp.zeros((scan_rows, dt_bias.shape[0]), f32)
    conv_rows = -(-(cols + tap_count + 1) // 8) * 8
    conv_packed = jnp.zeros((conv_rows, dt_bias.shape[0]), f32)
    length = mask_cols.shape[1]

    def back_conv(slot, us, dg, conv_packed):
        return conv_back_call(
            flip, slot, length, x, u, slope, taps, xproj_weight, us, dg, conv_packed
        )

    x_sums, x_theres = [], []
    u_tied = after(u, z_all, rows_give)
    for slot in slots:
        us, part_back, packed = backward_call(
            flip, slot, slot_count, dbl, dtproj_weight, vec, rates2, u_tied, *saved, packed, width
        )
        there = swap(part_back, "dir", 1)
        if slot == 0:
            z_part = Scatter(
                contract_rows(left_mine, after(z_all, part_back))
                + contract_rows(left_there, after(z_there, part_back)),
                "dp",
                rest(z_bit),
            )
            out_part = Scatter(
                contract_rows(branch_mine, after(gate_all, part_back))
                + contract_rows(branch_there, after(gate_there, part_back)),
                "dp",
                rest(out_bit)[::-1],
            )
        if slot + 1 < slot_count:
            dg = (part_back + after(there, z_part.send, out_part.send)).astype(bf16)
            keep, send, conv_packed = back_conv(slot, us, dg, conv_packed)
            send_there = swap(send, "dir", 0)
            if slot == 0:
                rows_mine, branch_sent = fold_call(
                    me_ref, [rows_keep], [after(rows_there, send)], shard_rows
                )
                branch_far = swap(branch_sent, "dir", 1)
            x_sums.append(join_call(keep, after(send_there, branch_sent)))
            x_theres.append(swap(x_sums[-1], "dp", z_bit))
            u_tied, z_part.send, out_part.send = after((u, z_part.send, out_part.send), x_sums[-1])

    z_part.step(part_back, branch_far, *x_theres)
    out_part.step(part_back)
    dg = (part_back + after(there, z_part.send, out_part.send)).astype(bf16)
    keep, send, conv_packed = back_conv(slot_count - 1, us, dg, conv_packed)
    shared = SharedSum(pack_call(out_side, conv_packed, packed), "dp", second)
    send_there = swap(after(send, shared.send), "dir", 0)
    x_sums.append(join_call(keep, send_there))
    x_there = swap(x_sums[-1], "dp", z_bit)
    norm_keep, norm_give = proj_back_call(
        flip, x_sums, z_all, in_weight, in_there, shard_rows, width
    )
    z_part.step(norm_give)
    out_part.step(norm_give)
    shared.step(z_part.values, out_part.values)
    x_theres.append(after(x_there, shared.send))
    norm_there = swap(norm_give, "dir", 0)
    norm_mine, norm_sent = fold_call(
        me_ref, [norm_keep], [after(norm_there, x_theres[-1])], shard_rows
    )
    norm_far = swap(norm_sent, "dir", 1)
    x_part = contract_rows(left_mine, jnp.concatenate(after(x_sums, norm_sent), 0)) + contract_rows(
        left_there, jnp.concatenate(after(x_theres, norm_sent), 0)
    )
    x_part = Scatter(x_part, "dp", rest(z_bit))
    shared.step(x_part.send)

    mixed, token_grads, mod_part = rows_call(
        tokens,
        cotangent,
        local_mask,
        mods,
        rows_mine,
        branch_far,
        norm_mine,
        after(norm_far, shared.send),
    )
    mod_parts = [
        lax.ppermute(mod_part, "dir", [(at, at ^ code) for at in range(dirs)])
        for code in range(1, dirs)
    ]
    shared.step(mod_part)
    x_part.step(shared.send)
    beside, *over = after(mod_parts, x_part.send)
    mod_total = mod_part + beside
    if over:
        mod_total = mod_total + (over[0] + over[1])
    mod_low = mod_total.astype(bf16).reshape(slot_count, 3 * model)
    have = []
    sides = jnp.concatenate([mod_low, cond_act], 1)
    sides = gather_bit(sides, "dp", first[0], have)
    while len(shared.plan) > 1:
        shared.step(sides)
    cond_grad = cond_call(after(mod_low, sides, shared.send), ada_weight, cond, 0, model)
    sides = gather_rest(sides, "dp", first[1:], cond_grad)
    sides = sides.reshape(dps * slot_count, -1)
    total_columns = ada_weight.shape[1]
    columns = total_columns // dirs
    rows = ada_weight.shape[0] // dps
    mod_all = lax.dynamic_slice_in_dim(sides, me * columns, columns, 1)
    act_mine = lax.dynamic_slice_in_dim(sides, total_columns + dp_index * rows, rows, 1)
    ada_sum = contract_rows(act_mine, mod_all)
    portion = total_columns // dps
    bias_part = lax.dynamic_slice_in_dim(sides, dp_index * portion, portion, 1)
    bias_sum = jnp.sum(bias_part.astype(f32), axis=0)

    keep, there = shared.last(ada_sum, bias_sum)
    xproj_sum, kernel_sum, dtproj_sum, rate_sum, vec_sum = unpack_call(
        out_side, keep, there, cols, tap_count, conv_rows, rank, states
    )
    while x_part.order:
        x_part.step(xproj_sum)
    while z_part.order:
        z_part.step(xproj_sum)
    while out_part.order:
        out_part.step(xproj_sum)
    x_sum = x_part.values
    z_sum = z_part.values
    out_sum = jnp.transpose(out_part.values)
    keep_sum = jnp.where(core == 0, x_sum, z_sum)
    send_sum = jnp.where(core == 0, z_sum, x_sum)
    in_sum = ordered(core, keep_sum, swap(send_sum, "dir", 0), 1)

    return (
        mixed,
        token_grads,
        cond_grad,
        ada_sum,
        bias_sum,
        in_sum,
        jnp.transpose(kernel_sum),
        vec_sum[0],
        xproj_sum,
        dtproj_sum,
        vec_sum[1],
        jnp.transpose(rate_sum),
        vec_sum[2],
        out_sum,
    )


def solution(mesh):
    in_specs = (
        P("dp", "dir", None),
        P("dp", None),
        P("dp"),
        P("dp", None),
        P(),
        P(),
        P(None, "dir"),
        P("dir", None),
        P("dir"),
        P("dir", None),
        P(None, "dir"),
        P("dir"),
        P("dir", None),
        P("dir"),
        P("dir", None),
        P("dp", "dir", None),
    )
    out_specs = (
        P("dp", "dir", None),
        P("dp", "dir", None),
        P("dp", None),
        P("dp", "dir"),
        P("dp"),
        P("dp", "dir"),
        P("dir", None),
        P("dir"),
        P("dir", None),
        P(None, "dir"),
        P("dir"),
        P("dir", None),
        P("dir"),
        P("dir", "dp"),
    )
    return jax.shard_map(local, mesh=mesh, in_specs=in_specs, out_specs=out_specs, check_vma=False)
```
